32 devices in a mesh: ctx: 16 (over z, y, core), fsdp: 2 (over x).
Axes of the slice: x: 2, y: 2, z: 4, core: 2. Of those that a mesh axis runs over, the one named last changes fastest.
Arguments:
- tokens: bfloat16 [3, 2, 1024, 768], P(None, 'fsdp', 'ctx'), may hold values from -6 to 6
- offsets: int32 [3, 2, 16], P(None, 'fsdp'), may hold values from 0 to 15, each once within a row
- norm1_gain: float32 [768], replicated, may hold values from 0.5 to 1.5
- norm2_gain: float32 [768], replicated, may hold values from 0.5 to 1.5
- bias_table: float32 [32, 12], replicated, may hold values from -4 to 4
- w_query: bfloat16 [768, 768], P('fsdp'), may hold values from -0.109375 to 0.109375
- w_key: bfloat16 [768, 768], P('fsdp'), may hold values from -0.109375 to 0.109375
- w_value: bfloat16 [768, 768], P('fsdp'), may hold values from -0.21875 to 0.21875
- w_out: bfloat16 [768, 768], P('fsdp'), may hold values from -1.75 to 1.75
- w_gate: bfloat16 [768, 2048], P('fsdp'), may hold values from -0.21875 to 0.21875
- w_up: bfloat16 [768, 2048], P('fsdp'), may hold values from -0.21875 to 0.21875
- w_down: bfloat16 [2048, 768], P('fsdp'), may hold values from -0.125 to 0.125
- cotangent: bfloat16 [3, 2, 1024, 768], P(None, 'fsdp', 'ctx'), may hold values from -6 to 6
Outputs:
- out: bfloat16 [3, 2, 1024, 768], P(None, 'fsdp', 'ctx')
- x_grad: float32 [3, 2, 1024, 768], P(None, 'fsdp', 'ctx')
- norm1_gain_grad: float32 [768], P('fsdp')
- norm2_gain_grad: float32 [768], P('fsdp')
- bias_table_grad: float32 [32, 12], P('fsdp')
- w_query_grad: float32 [768, 768], P('fsdp')
- w_key_grad: float32 [768, 768], P('fsdp')
- w_value_grad: float32 [768, 768], P('fsdp')
- w_out_grad: float32 [768, 768], P('fsdp')
- w_gate_grad: float32 [768, 2048], P('fsdp')
- w_up_grad: float32 [768, 2048], P('fsdp')
- w_down_grad: float32 [2048, 768], P('fsdp')
The draws below stay inside these ranges and needn't reach their ends.
Inputs may be any that keep to these rules, and one draw needn't show every extreme that they name: `offsets`: each row along the last dimension is a permutation of 0 to 15.
All inputs are finite; a program needn't handle non-finite values.
Results may differ from the reference program's by a relative error of at most 0.015.
The reference program's roundings to bfloat16 on the way count: a program that leaves them out, or rounds other values in their place, can miss the bound.
Values may be sent and summed in bfloat16 or wider, within the bound.
No kernel may reach another device: no remote copies, remote signals or barrier semaphores. Data moves between devices by JAX's collectives and lax.ppermute only.
A program may use at most 192 MiB of HBM per device.

```python
import math
import jax
import jax.numpy as jnp
from jax import lax

D = 768
HEADS = 12
HEAD_DIM = 64
FF = 2048
BUCKETS = 32
TOK_DEV = 64
MICRO = 3
SEQS = 2
BLOCKS = 16
LENGTH = 1024


def levels(stream_key, extent, split, least, largest):
    factor_of, own = 1.0, jax.random.fold_in(stream_key, 6)
    for axis_at, blocks in split:
        draws = jnp.exp(jax.random.uniform(jax.random.fold_in(own, axis_at), (blocks,), jnp.float32, least / len(split), largest / len(split)))
        factor_of = factor_of * jnp.repeat(draws, extent[axis_at] // blocks).reshape([-1 if axis == axis_at else 1 for axis in range(len(extent))])
    return factor_of


def noise(own_key, shape, spread, limit, cuts=(), held_as=jnp.bfloat16):
    loudness = levels(own_key, shape, cuts, -0.22, 0.18) if cuts else 1.0
    entries = jax.random.normal(own_key, shape, jnp.float32) * spread * loudness
    return jnp.minimum(jnp.maximum(entries, -limit), limit).astype(held_as)


def setup_inputs(seed: int = 0) -> dict:
    arg_keys = jax.random.split(jax.random.key(seed), 14)
    tokens = noise(arg_keys[0], (MICRO, SEQS, LENGTH, D), 1.0, 6.0, ((1, 2), (2, 16)))
    offsets = jax.vmap(lambda own: jax.random.permutation(own, BLOCKS))(jax.random.split(arg_keys[1], MICRO * SEQS)).reshape((MICRO, SEQS, BLOCKS)).astype(jnp.int32)
    norm1_gain = jnp.clip(1.0 + 0.1 * jax.random.normal(arg_keys[2], (D,), jnp.float32), 0.5, 1.5)
    norm2_gain = jnp.clip(1.0 + 0.1 * jax.random.normal(arg_keys[3], (D,), jnp.float32), 0.5, 1.5)
    bias_table = noise(arg_keys[4], (BUCKETS, HEADS), 1.0, 4.0, (), jnp.float32)
    w_query = noise(arg_keys[5], (D, HEADS * HEAD_DIM), (4 * D) ** -0.5, 0.109375, ((0, 2),))
    w_key = noise(arg_keys[6], (D, HEADS * HEAD_DIM), (4 * D) ** -0.5, 0.109375, ((0, 2),))
    w_value = noise(arg_keys[7], (D, HEADS * HEAD_DIM), D ** -0.5, 0.21875, ((0, 2),))
    w_out = noise(arg_keys[8], (HEADS * HEAD_DIM, D), (HEADS * HEAD_DIM // 64) ** -0.5, 1.75, ((0, 2),))
    w_gate = noise(arg_keys[9], (D, FF), D ** -0.5, 0.21875, ((0, 2),))
    w_up = noise(arg_keys[10], (D, FF), D ** -0.5, 0.21875, ((0, 2),))
    w_down = noise(arg_keys[11], (FF, D), FF ** -0.5, 0.125, ((0, 2),))
    cotangent = noise(arg_keys[12], (MICRO, SEQS, LENGTH, D), 1.0, 6.0, ((1, 2), (2, 16)))
    return {"tokens": tokens, "offsets": offsets, "norm1_gain": norm1_gain, "norm2_gain": norm2_gain, "bias_table": bias_table, "w_query": w_query, "w_key": w_key, "w_value": w_value, "w_out": w_out, "w_gate": w_gate, "w_up": w_up, "w_down": w_down, "cotangent": cotangent}


@jax.custom_vjp
def low(v):
    return lax.optimization_barrier(v.astype(jnp.bfloat16)).astype(jnp.float32)

@jax.custom_vjp
def low_back(v):
    return v

def low_keep(v):
    return (low(v), None)

def low_pass(kept, grad):
    return (grad,)

def back_keep(v):
    return (v, None)

def back_low(kept, grad):
    return (low(grad),)
low.defvjp(low_keep, low_pass)
low_back.defvjp(back_keep, back_low)
PRECISE = lax.Precision.HIGHEST

def bucket_of(relative):
    distance = jnp.abs(relative)
    squared = distance * distance
    counted = jnp.zeros_like(relative)
    for exponent in range(1, 8):
        counted = counted + (squared >= 64 * 2 ** exponent).astype(jnp.int32)
    within = jnp.where(distance < 8, distance, 8 + counted)
    return jnp.where(relative > 0, 16, 0).astype(jnp.int32) + within

def matmul(left, right):
    return jnp.dot(left, right, precision=PRECISE, preferred_element_type=jnp.float32)

def rms_norm(values, gain_vector):
    scale = lax.rsqrt(lax.optimization_barrier(jnp.mean(values * values, axis=-1, keepdims=True)) + 1e-06)
    return values * scale * gain_vector

def attend(query, keys, values, positions, table):
    row_count, head_count, head_width = query.shape
    block_rows = math.gcd(row_count, 512)
    query_parts = query.reshape(row_count // block_rows, block_rows, head_count, head_width)
    place_parts = positions.reshape(row_count // block_rows, block_rows)

    def one_block(pieces):
        query_part, place_part = pieces
        labels = bucket_of(positions[None, :] - place_part[:, None])
        bias = jnp.transpose(table[labels], (2, 0, 1))
        scores = jnp.einsum('qhd,khd->hqk', query_part, keys, precision=PRECISE) + bias
        scores = low_back(scores)
        weights_soft = jnp.exp(scores - jax.nn.logsumexp(scores, axis=-1, keepdims=True))
        return jnp.einsum('hqk,khd->qhd', low(weights_soft), values, precision=PRECISE)
    mixed = lax.map(jax.checkpoint(one_block), (query_parts, place_parts))
    return mixed.reshape(row_count, head_count * head_width)

def layer(inputs_f, positions, params):
    gain_one, gain_two, table, w_query, w_key, w_value, w_out, w_gate, w_up, w_down = params
    row_count = inputs_f.shape[0]
    head_count = table.shape[1]
    act_one = low(rms_norm(inputs_f, gain_one))
    query = low_back(low(matmul(act_one, w_query)))
    keys = low_back(low(matmul(act_one, w_key)))
    values = low_back(low(matmul(act_one, w_value)))
    mixed = attend(query.reshape(row_count, head_count, -1), keys.reshape(row_count, head_count, -1), values.reshape(row_count, head_count, -1), positions, table)
    mixed = low_back(low(mixed))
    resid = inputs_f + low_back(matmul(mixed, w_out))
    act_two = low(rms_norm(resid, gain_two))
    gate_pre = low_back(matmul(act_two, w_gate))
    up_pre = low_back(matmul(act_two, w_up))
    hidden = low(jax.nn.gelu(gate_pre, approximate=True) * up_pre)
    return resid + low_back(matmul(hidden, w_down))

def reference(tokens, offsets, norm1_gain, norm2_gain, bias_table, w_query, w_key, w_value, w_out, w_gate, w_up, w_down, cotangent):
    params = (norm1_gain, norm2_gain, bias_table) + tuple((matrix.astype(jnp.float32) for matrix in (w_query, w_key, w_value, w_out, w_gate, w_up, w_down)))
    width = tokens.shape[-1]
    inputs_all = tokens.astype(jnp.float32).reshape(-1, LENGTH, width)
    grads_all = cotangent.astype(jnp.float32).reshape(-1, LENGTH, width)
    starts_all = offsets.reshape(-1, BLOCKS)

    def per_sequence(totals, items):
        inputs_f, grad_in, starts = items
        positions = (starts[:, None] * TOK_DEV + jnp.arange(TOK_DEV, dtype=jnp.int32)[None, :]).reshape(-1)

        def apply_layer(values, weights):
            return layer(values, positions, weights)
        result, pullback = jax.vjp(apply_layer, inputs_f, params)
        grad_x, grad_params = pullback(grad_in)

        def add_pair(first, second):
            return first + second
        totals = jax.tree.map(add_pair, totals, grad_params)
        return (totals, (result.astype(jnp.bfloat16), grad_x))
    zeros = jax.tree.map(jnp.zeros_like, params)
    grads, (results, input_grads) = lax.scan(per_sequence, zeros, (inputs_all, grads_all, starts_all))
    return (results.reshape(tokens.shape), input_grads.reshape(tokens.shape), grads[0], grads[1], grads[2], grads[3], grads[4], grads[5], grads[6], grads[7], grads[8], grads[9])
```

```python
import functools

import jax
import jax.numpy as jnp
from jax import lax
from jax.experimental import pallas as pl
from jax.experimental.pallas import tpu as pltpu
from jax.sharding import PartitionSpec as P

EPSILON = 1e-06
GROUPS = 4
WIDE = jnp.float32
LOW = jnp.bfloat16
FAR = 91
NEAR_LEAD = 96
VMEM_LIMIT = 60 * 1024 * 1024


def dot(a, b):
    return jnp.dot(a, b, preferred_element_type=WIDE)


def dot_t(a, b):
    return lax.dot_general(a, b, (((1,), (1,)), ((), ())), preferred_element_type=WIDE)


def t_dot(a, b):
    return lax.dot_general(a, b, (((0,), (0,)), ((), ())), preferred_element_type=WIDE)


def bucket_of(relative):
    distance = jnp.abs(relative)
    squared = distance * distance
    counted = jnp.zeros_like(relative)
    for exponent in range(1, 8):
        counted = counted + (squared >= 64 * 2**exponent).astype(jnp.int32)
    within = jnp.where(distance < 8, distance, 8 + counted)
    return jnp.where(relative > 0, 16, 0).astype(jnp.int32) + within


def hop(v, axis, bit):
    size = lax.axis_size(axis)
    return lax.ppermute(v, axis, [(i, i ^ bit) for i in range(size)])


def bits_down(size):
    bit = size // 2
    while bit >= 1:
        yield bit
        bit //= 2


def bits_up(size):
    return reversed(list(bits_down(size)))


def shift(v, steps):
    size = lax.axis_size("ctx")
    stride = size // GROUPS
    return lax.ppermute(v, "ctx", [(i, (i + steps * stride) % size) for i in range(size)])


def slots_out(v, axis, count):
    slots = {0: v}
    for bit in bits_down(count):
        for j in list(slots):
            slots[j ^ bit] = hop(slots[j], axis, bit)
    return [slots[j] for j in range(count)]


def slots_back(parts, axis, count):
    held = {j: [part] for j, part in enumerate(parts)}
    for bit in bits_up(count):
        for j in sorted(held):
            if j & bit:
                total = held[j][0]
                if len(held[j]) > 1:
                    total = sum(v.astype(WIDE) for v in held[j])
                held[j ^ bit].append(hop(total.astype(LOW), axis, bit))
                del held[j]
    return held[0]


def halve(v, axis, unit):
    count = v.shape[0]
    for bit in bits_down(count):
        v = v[:bit] + hop(v[bit:].astype(LOW), axis, bit * unit).astype(WIDE)
    return v[0]


def strip_kernel(blocks, table_ref, strip_ref):
    centre = 64 * (blocks - 1)
    rows = 2 * 64 * blocks
    near = 256
    start = centre - NEAR_LEAD
    chunk = 128
    heads = table_ref.shape[1]

    def relative(first, count):
        u = lax.broadcasted_iota(jnp.int32, (count, 128), 0) + first
        i = lax.broadcasted_iota(jnp.int32, (count, 128), 1)
        return u - centre - jnp.where(i >= 64, i - 64, i)

    for h in range(heads):
        strip_ref[h, : start, :] = jnp.full((start, 128), table_ref[15, h], WIDE)
        strip_ref[h, start + near :, :] = jnp.full((rows - start - near, 128), table_ref[31, h], WIDE)
    for first in range(start, start + near, chunk):
        label = bucket_of(relative(first, chunk))
        for h in range(heads):
            value = jnp.zeros((chunk, 128), WIDE)
            for b in range(32):
                value = jnp.where(label == b, table_ref[b, h], value)
            strip_ref[h, first : first + chunk, :] = value


def make_strip(table_group, blocks):
    heads = table_group.shape[1]
    return pl.pallas_call(
        functools.partial(strip_kernel, blocks),
        out_shape=jax.ShapeDtypeStruct((heads, 2 * 64 * blocks, 128), WIDE),
        in_specs=[pl.BlockSpec(memory_space=pltpu.SMEM)],
        out_specs=pl.BlockSpec(memory_space=pltpu.VMEM),
        compiler_params=pltpu.CompilerParams(vmem_limit_bytes=VMEM_LIMIT),
        name="bias_strip",
    )(table_group)


def split_heads(wide, second_upper):
    lane = lax.broadcasted_iota(jnp.int32, (wide.shape[0], 128), 1)
    low = lane < 64
    zero = jnp.zeros((wide.shape[0], 128), wide.dtype)
    first, second = wide[:, :128], wide[:, 128:]
    third = jnp.where(low, zero, second) if second_upper else jnp.where(low, second, zero)
    return [jnp.where(low, first, zero), jnp.where(low, zero, first), third]


KEY_COLS = (0, 0, 128)
VALUE_COLS = (256, 256, 128)


def sort_blocks(count, m, kplace_ref, kv_refs, sorted_ref):
    for j in range(count):
        for e in range(GROUPS):
            to = pl.multiple_of(kplace_ref[m, j, e] * 64, 64)
            sorted_ref[pl.ds(to, 64), :] = kv_refs[j][e, 0]


def bias_of(strip_ref, h, offs, half, rows, low):
    a = strip_ref[h, pl.ds(offs[2 * half], rows), :]
    b = strip_ref[h, pl.ds(offs[2 * half + 1], rows), :]
    return jnp.where(low, a, b)


def forward_kernel(count, blocks, qplace_ref, kplace_ref, strip_ref, q_ref, *refs):
    kv_refs = refs[:count]
    o_refs = refs[count : count + GROUPS]
    lse_ref, sorted_ref = refs[count + GROUPS :]
    m = pl.program_id(0)
    rows = 64 * blocks
    sort_blocks(count, m, kplace_ref, kv_refs, sorted_ref)
    offs = [pl.multiple_of((blocks - 1 - qplace_ref[m, e]) * 64, 64) for e in range(GROUPS)]
    queries = split_heads(q_ref[:, 0].reshape(GROUPS * 64, 256), False)
    low = lax.broadcasted_iota(jnp.int32, (rows, 128), 1) < 64
    mixed = []
    for h in range(3):
        keys = sorted_ref[:, KEY_COLS[h] : KEY_COLS[h] + 128]
        values = sorted_ref[:, VALUE_COLS[h] : VALUE_COLS[h] + 128]
        scores = dot_t(keys, queries[h])
        parts = []
        for half in range(2):
            s = scores[:, half * 128 : half * 128 + 128] + bias_of(strip_ref, h, offs, half, rows, low)
            top = jnp.max(s, axis=0, keepdims=True)
            e = jnp.exp(s - top)
            total = jnp.sum(e, axis=0, keepdims=True)
            lse_ref[0, h : h + 1, half * 128 : half * 128 + 128] = top + jnp.log(total)
            parts.append((e * (1.0 / total)).astype(LOW))
        weights = jnp.concatenate(parts, axis=1)
        mixed.append(t_dot(values, weights))
    sub = lax.broadcasted_iota(jnp.int32, (128, GROUPS * 64), 0) < 64
    first = jnp.where(sub, mixed[0], mixed[1]).T
    second = jnp.where(sub, 0.0, mixed[2]).T
    out = jnp.concatenate([first, second], axis=1).astype(LOW)
    for d in range(GROUPS):
        o_refs[d][0] = out[d * 64 : d * 64 + 64]


def attention_forward(places, strip, q, kv_slots, blocks):
    qplace, kplace = places
    count = len(kv_slots)
    micro = q.shape[1]
    rows = 64 * blocks
    kv_cols = kv_slots[0].shape[-1]
    by_micro = lambda width: pl.BlockSpec((GROUPS, 1, 64, width), lambda m, *_: (0, m, 0, 0))
    results = pl.pallas_call(
        functools.partial(forward_kernel, count, blocks),
        out_shape=(jax.ShapeDtypeStruct((micro, 64, 256), LOW),) * GROUPS
        + (jax.ShapeDtypeStruct((micro, 3, GROUPS * 64), WIDE),),
        grid_spec=pltpu.PrefetchScalarGridSpec(
            num_scalar_prefetch=2,
            grid=(micro,),
            in_specs=[pl.BlockSpec(strip.shape, lambda m, *_: (0, 0, 0)), by_micro(256)] + [by_micro(kv_cols)] * count,
            out_specs=(pl.BlockSpec((1, 64, 256), lambda m, *_: (m, 0, 0)),) * GROUPS
            + (pl.BlockSpec((1, 3, GROUPS * 64), lambda m, *_: (m, 0, 0)),),
            scratch_shapes=[pltpu.VMEM((rows, kv_cols), LOW)],
        ),
        compiler_params=pltpu.CompilerParams(vmem_limit_bytes=VMEM_LIMIT),
        cost_estimate=pl.CostEstimate(
            flops=micro * 3 * 2 * 2 * rows * GROUPS * 64 * 128 * 2,
            bytes_accessed=micro * rows * kv_cols * 4,
            transcendentals=micro * 3 * rows * GROUPS * 64,
        ),
        name="attention_forward",
    )(qplace, kplace, strip, q, *kv_slots)
    return list(results[:GROUPS]), results[GROUPS]


def backward_kernel(count, blocks, qplace_ref, kplace_ref, place_ref, strip_ref, q_ref, lse_ref, *refs):
    do_refs, refs = refs[:GROUPS], refs[GROUPS:]
    kv_refs = refs[:count]
    dq_ref = refs[count]
    dkv_refs = refs[count + 1 : 2 * count + 1]
    table_ref = refs[2 * count + 1]
    sorted_ref, grad_ref, lower_ref, upper_ref = refs[2 * count + 2 :]
    m = pl.program_id(0)
    rows = 64 * blocks

    @pl.when(m == 0)
    def _():
        lower_ref[...] = jnp.zeros_like(lower_ref)
        upper_ref[...] = jnp.zeros_like(upper_ref)

    sort_blocks(count, m, kplace_ref, kv_refs, sorted_ref)
    offs = [pl.multiple_of((blocks - 1 - qplace_ref[m, e]) * 64, 64) for e in range(GROUPS)]
    queries = split_heads(q_ref[:, 0].reshape(GROUPS * 64, 256), False)
    grads = split_heads(jnp.concatenate([r[0] for r in do_refs], axis=0), True)
    low = lax.broadcasted_iota(jnp.int32, (rows, 128), 1) < 64
    query_grads, scores_grads, soft = [], [], []
    for h in range(3):
        keys = sorted_ref[:, KEY_COLS[h] : KEY_COLS[h] + 128]
        values = sorted_ref[:, VALUE_COLS[h] : VALUE_COLS[h] + 128]
        scores = dot_t(keys, queries[h])
        weight_grads = dot_t(values, grads[h])
        ds_parts, p_parts = [], []
        for half in range(2):
            cols = slice(half * 128, half * 128 + 128)
            s = scores[:, cols] + bias_of(strip_ref, h, offs, half, rows, low)
            p = jnp.exp(s - lse_ref[0, h : h + 1, cols])
            dp = weight_grads[:, cols]
            delta = jnp.sum(p * dp, axis=0, keepdims=True)
            ds = (p * (dp - delta)).astype(LOW)
            p_parts.append(p.astype(LOW))
            ds_parts.append(ds)
            wide = ds.astype(WIDE)
            at = pl.ds(offs[2 * half], rows)
            lower_ref[h, at, :] += wide
            at = pl.ds(offs[2 * half + 1], rows)
            upper_ref[h, at, :] += wide
        ds_all = jnp.concatenate(ds_parts, axis=1)
        p_all = jnp.concatenate(p_parts, axis=1)
        query_grads.append(t_dot(keys, ds_all))
        scores_grads.append(ds_all)
        soft.append(p_all)
    sub = lax.broadcasted_iota(jnp.int32, (128, GROUPS * 64), 0) < 64
    first = jnp.where(sub, query_grads[0], query_grads[1]).T
    second = jnp.where(sub, query_grads[2], 0.0).T
    dq_ref[:, 0] = jnp.concatenate([first, second], axis=1).astype(LOW).reshape(GROUPS, 64, 256)
    grad_ref[:, 0:128] = (dot(scores_grads[0], queries[0]) + dot(scores_grads[1], queries[1])).astype(LOW)
    grad_ref[:, 128:256] = (dot(scores_grads[2], queries[2]) + dot(soft[2], grads[2])).astype(LOW)
    grad_ref[:, 256:384] = (dot(soft[0], grads[0]) + dot(soft[1], grads[1])).astype(LOW)
    for j in range(count):
        for e in range(GROUPS):
            at = pl.multiple_of(kplace_ref[m, j, e] * 64, 64)
            dkv_refs[j][e, 0] = grad_ref[pl.ds(at, 64), :]

    @pl.when(m == pl.num_programs(0) - 1)
    def _():
        centre = 64 * (blocks - 1)
        start = centre - NEAR_LEAD
        near = 256
        sums_row = lax.broadcasted_iota(jnp.int32, (32, 128), 0)
        side = lax.broadcasted_iota(jnp.int32, (near, 128), 1)
        rel = lax.broadcasted_iota(jnp.int32, (near, 128), 0) + (start - centre) - jnp.where(side >= 64, side - 64, side)
        label = bucket_of(rel)

        def folded(h, first, size):
            lane = lax.broadcasted_iota(jnp.int32, (size, 128), 1) < 64
            return jnp.where(lane, lower_ref[h, first : first + size, :], upper_ref[h, first : first + size, :])

        table = jnp.zeros((32, 128), WIDE)
        for h in range(3):
            before = jnp.sum(folded(h, 0, start), axis=0, keepdims=True)
            last = start + near
            after = jnp.sum(folded(h, last, 2 * rows - last), axis=0, keepdims=True)
            window = folded(h, start, near)
            result = jnp.where(sums_row == 15, before, jnp.where(sums_row == 31, after, 0.0))
            for b in range(32):
                part = jnp.sum(jnp.where(label == b, window, 0.0), axis=0, keepdims=True)
                result = result + jnp.where(sums_row == b, part, 0.0)
            total = jnp.sum(result, axis=1, keepdims=True)
            lanes = lax.broadcasted_iota(jnp.int32, (32, 128), 1)
            table = jnp.where(lanes == place_ref[0] * 3 + h, total, table)
        table_ref[...] = table


def attention_backward(places, place, strip, q, kv_slots, do_slots, lse, blocks):
    qplace, kplace = places
    count = len(kv_slots)
    micro = q.shape[1]
    rows = 64 * blocks
    kv_cols = kv_slots[0].shape[-1]
    by_micro = lambda width: pl.BlockSpec((GROUPS, 1, 64, width), lambda m, *_: (0, m, 0, 0))
    kv_shape = jax.ShapeDtypeStruct(kv_slots[0].shape, LOW)
    results = pl.pallas_call(
        functools.partial(backward_kernel, count, blocks),
        out_shape=(jax.ShapeDtypeStruct(q.shape, LOW),)
        + (kv_shape,) * count
        + (jax.ShapeDtypeStruct((32, 128), WIDE),),
        grid_spec=pltpu.PrefetchScalarGridSpec(
            num_scalar_prefetch=3,
            grid=(micro,),
            in_specs=[
                pl.BlockSpec(strip.shape, lambda m, *_: (0, 0, 0)),
                by_micro(256),
                pl.BlockSpec((1, 3, GROUPS * 64), lambda m, *_: (m, 0, 0)),
            ]
            + [pl.BlockSpec((1, 64, 256), lambda m, *_: (m, 0, 0))] * GROUPS
            + [by_micro(kv_cols)] * count,
            out_specs=(by_micro(256),)
            + (by_micro(kv_cols),) * count
            + (pl.BlockSpec((32, 128), lambda m, *_: (0, 0)),),
            scratch_shapes=[
                pltpu.VMEM((rows, kv_cols), LOW),
                pltpu.VMEM((rows, kv_cols), LOW),
                pltpu.VMEM((3, 2 * rows, 128), WIDE),
                pltpu.VMEM((3, 2 * rows, 128), WIDE),
            ],
        ),
        compiler_params=pltpu.CompilerParams(vmem_limit_bytes=VMEM_LIMIT),
        cost_estimate=pl.CostEstimate(
            flops=micro * 3 * 5 * 2 * rows * GROUPS * 64 * 128 * 2,
            bytes_accessed=micro * rows * kv_cols * 8,
            transcendentals=micro * 3 * rows * GROUPS * 64,
        ),
        name="attention_backward",
    )(qplace, kplace, place, strip, q, lse, *do_slots, *kv_slots)
    return results[0], list(results[1 : count + 1]), results[count + 1]


PLACE = pl.BlockSpec(memory_space=pltpu.SMEM)


def whole(count):
    return [pl.BlockSpec(memory_space=pltpu.VMEM)] * count


def call(kernel, name, place, operands, out_shape, scratch=(), flops=0):
    size = sum(v.size * v.dtype.itemsize for v in operands) + sum(
        v.size * jnp.dtype(v.dtype).itemsize for v in out_shape
    )
    return pl.pallas_call(
        kernel,
        out_shape=tuple(out_shape),
        in_specs=[PLACE] + whole(len(operands)),
        out_specs=tuple(whole(len(out_shape))),
        scratch_shapes=list(scratch),
        compiler_params=pltpu.CompilerParams(vmem_limit_bytes=VMEM_LIMIT),
        cost_estimate=pl.CostEstimate(flops=flops, bytes_accessed=size, transcendentals=0),
        name=name,
    )(place, *operands)


def shaped(*shape, dtype=LOW):
    return jax.ShapeDtypeStruct(shape, dtype)


def place_rows(full_ref, slot_refs, index):
    rows = slot_refs[0].shape[0]
    for j, ref in enumerate(slot_refs):
        full_ref[pl.ds(pl.multiple_of((index ^ j) * rows, rows), rows), :] = ref[...]


def rms_scale(values):
    return lax.rsqrt(jnp.mean(values * values, axis=-1, keepdims=True) + EPSILON)


def norm_back(grad_normed, normed, scale):
    return scale * (grad_normed - normed * jnp.mean(grad_normed * normed, axis=-1, keepdims=True))


def project_kernel(parts_f, place_ref, gain_ref, *refs):
    x_refs, w_refs = refs[:GROUPS], refs[GROUPS : GROUPS + parts_f]
    act_ref, q_ref, kv_ref, full_ref = refs[GROUPS + parts_f :]
    place_rows(full_ref, w_refs, place_ref[2])
    micro, rows, width = x_refs[0].shape
    for d in range(GROUPS):
        x = x_refs[d][...].reshape(micro * rows, width).astype(WIDE)
        act = (x * rms_scale(x) * gain_ref[...]).astype(LOW)
        act_ref[d] = act
        both = dot(act, full_ref[...]).astype(LOW)
        q_ref[d] = both[:, :256].reshape(micro, rows, 256)
        kv_ref[d] = both[:, 256:].reshape(micro, rows, 384)


def project(place, gain, x_slots, w_slots):
    micro, rows, width = x_slots[0].shape
    return call(
        functools.partial(project_kernel, len(w_slots)),
        "project",
        place,
        [gain, *x_slots, *w_slots],
        [
            shaped(GROUPS, micro * rows, width),
            shaped(GROUPS, micro, rows, 256),
            shaped(GROUPS, micro, rows, 384),
        ],
        [pltpu.VMEM((width, 640), LOW)],
        flops=2 * GROUPS * micro * rows * width * 640,
    )


def group_rows(place_ref, d):
    return lax.rem(place_ref[0] + d, GROUPS) * 192


def joined_kernel(parts_f, place_ref, gain_ref, x_ref, *refs):
    o_refs, w_refs = refs[:GROUPS], refs[GROUPS : GROUPS + parts_f]
    resid_ref, act_ref, full_ref = refs[GROUPS + parts_f :]
    place_rows(full_ref, w_refs, place_ref[2])
    micro, rows, width = x_ref.shape
    total = x_ref[...].reshape(micro * rows, width).astype(WIDE)
    for d in range(GROUPS):
        o = o_refs[d][...].reshape(micro * rows, 256)
        at = group_rows(place_ref, d)
        total += dot(o[:, :128], full_ref[pl.ds(pl.multiple_of(at, 64), 128), :])
        total += dot(o[:, 128:], full_ref[pl.ds(pl.multiple_of(at + 64, 64), 128), :])
    resid_ref[...] = total
    act_ref[...] = (total * rms_scale(total) * gain_ref[...]).astype(LOW)


def joined(place, gain, x, o_slots, w_slots):
    micro, rows, width = x.shape
    return call(
        functools.partial(joined_kernel, len(w_slots)),
        "joined",
        place,
        [gain, x, *o_slots, *w_slots],
        [shaped(micro * rows, width, dtype=WIDE), shaped(micro * rows, width)],
        [pltpu.VMEM((width, width), LOW)],
        flops=2 * micro * rows * width * 1024,
    )


GELU_A = 0.7978845608028654
GELU_B = 0.044715


def feed_kernel(parts_f, fast, place_ref, *refs):
    act_refs, refs = refs[:fast], refs[fast:]
    g_refs, refs = refs[:fast], refs[fast:]
    pair_refs, refs = refs[:parts_f], refs[parts_f:]
    down_refs, refs = refs[:parts_f], refs[parts_f:]
    two_refs, refs = refs[:fast], refs[fast:]
    out_refs, refs = refs[:fast], refs[fast:]
    hid_ref, grad_ref, pair_ref, down_ref = refs
    place_rows(pair_ref, pair_refs, place_ref[2])
    place_rows(down_ref, down_refs, place_ref[2])
    cols = hid_ref.shape[-1]
    for j in range(fast):
        both = dot(act_refs[j][...], pair_ref[...])
        z, up = both[:, :cols], both[:, cols:]
        square = z * z
        t = jnp.tanh(GELU_A * (z + GELU_B * square * z))
        half = 0.5 * (1.0 + t)
        gelu = z * half
        slope = half + (0.5 * z) * (1.0 - t * t) * (GELU_A * (1.0 + 3.0 * GELU_B * square))
        hid = (gelu * up).astype(LOW)
        dh = dot_t(g_refs[j][...], down_ref[...])
        grads = jnp.concatenate([(dh * up * slope).astype(LOW), (dh * gelu).astype(LOW)], axis=1)
        hid_ref[j] = hid
        grad_ref[j] = grads
        two_refs[j][...] = dot_t(grads, pair_ref[...]).astype(LOW)
        out_refs[j][...] = dot(hid, down_ref[...]).astype(LOW)


def feed(place, act_slots, g_slots, pair_slots, down_slots):
    fast, parts_f = len(act_slots), len(pair_slots)
    rows, width = act_slots[0].shape
    cols = down_slots[0].shape[0] * parts_f
    results = call(
        functools.partial(feed_kernel, parts_f, fast),
        "feed",
        place,
        [*act_slots, *g_slots, *pair_slots, *down_slots],
        [shaped(rows, width)] * (2 * fast) + [shaped(fast, rows, cols), shaped(fast, rows, 2 * cols)],
        [pltpu.VMEM((width, 2 * cols), LOW), pltpu.VMEM((cols, width), LOW)],
        flops=2 * fast * rows * width * cols * 6,
    )
    return list(results[:fast]), list(results[fast : 2 * fast]), results[-2], results[-1]


def packing(piece, rows):
    if rows == 3 * piece:
        return [(0, k * 256, k * piece, 0, piece, 256) for k in range(3)]
    half = piece // 2
    return [
        (0, 0, 0, 0, piece, 512),
        (0, 512, piece, 0, half, 256),
        (half, 512, piece, 256, half, 256),
    ]


def feed_grads_kernel(parts_f, fast, place_ref, *refs):
    act_refs, refs = refs[:fast], refs[fast:]
    g_refs, refs = refs[:fast], refs[fast:]
    hid_ref, grad_ref, refs = refs[0], refs[1], refs[2:]
    pair_outs, refs = refs[:parts_f], refs[parts_f:]
    down_outs, refs = refs[:parts_f], refs[parts_f:]
    pair_ref, down_ref = refs
    f = place_ref[2]
    fast_, rows, cols = hid_ref.shape
    act = jnp.concatenate([r[...] for r in act_refs], axis=0)
    pair_ref[...] = t_dot(act, grad_ref[...].reshape(fast * rows, 2 * cols))
    g = jnp.concatenate([r[...] for r in g_refs], axis=0)
    down_ref[...] = t_dot(hid_ref[...].reshape(fast * rows, cols), g)
    part_rows = pair_outs[0].shape[0]
    piece = cols // parts_f
    for j in range(parts_f):
        at = pl.multiple_of((f ^ j) * part_rows, part_rows)
        pair_outs[j][...] = pair_ref[pl.ds(at, part_rows), :].astype(pair_outs[j].dtype)
        for r, c, to_r, to_c, n, w in packing(piece, part_rows):
            at = pl.multiple_of((f ^ j) * piece + r, 8)
            down_outs[j][to_r : to_r + n, to_c : to_c + w] = down_ref[pl.ds(at, n), c : c + w].astype(
                down_outs[j].dtype
            )


def feed_grads(place, act_slots, g_slots, hid, grads, parts_f):
    fast, rows, cols = hid.shape
    width = act_slots[0].shape[1]
    part_rows = width // parts_f
    types = [WIDE] + [LOW] * (parts_f - 1)
    results = call(
        functools.partial(feed_grads_kernel, parts_f, fast),
        "feed_grads",
        place,
        [*act_slots, *g_slots, hid, grads],
        [shaped(part_rows, 2 * cols, dtype=t) for t in types] + [shaped(part_rows, cols, dtype=t) for t in types],
        [pltpu.VMEM((width, 2 * cols), WIDE), pltpu.VMEM((cols, width), WIDE)],
        flops=2 * fast * rows * width * cols * 3,
    )
    return list(results[:parts_f]), list(results[parts_f:])


def branch_kernel(parts_f, count, place_ref, gain_ref, resid_ref, g_ref, *refs):
    two_refs, refs = refs[:count], refs[count:]
    w_refs, refs = refs[:parts_f], refs[parts_f:]
    grad_ref, low_ref, gain_out = refs[:3]
    do_refs, full_ref = refs[3 : 3 + GROUPS], refs[3 + GROUPS]
    place_rows(full_ref, w_refs, place_ref[2])
    micro, rows, _ = do_refs[0].shape
    grad_two = sum(r[...].astype(WIDE) for r in two_refs)
    resid = resid_ref[...]
    scale = rms_scale(resid)
    normed = resid * scale
    gain_out[...] = jnp.sum(grad_two * normed, axis=0, keepdims=True)
    grad = g_ref[...].astype(WIDE) + norm_back(grad_two * gain_ref[...], normed, scale)
    grad_ref[...] = grad
    low = grad.astype(LOW)
    low_ref[...] = low
    for d in range(GROUPS):
        at = group_rows(place_ref, d)
        first = dot_t(low, full_ref[pl.ds(pl.multiple_of(at, 64), 128), :])
        second = dot_t(low, full_ref[pl.ds(pl.multiple_of(at + 64, 64), 128), :])
        both = jnp.concatenate([first, second], axis=1).astype(LOW)
        do_refs[d][...] = both.reshape(micro, rows, 256)


def branch(place, gain, resid, g, two_list, w_slots, micro):
    rows, width = resid.shape
    results = call(
        functools.partial(branch_kernel, len(w_slots), len(two_list)),
        "branch",
        place,
        [gain, resid, g, *two_list, *w_slots],
        [shaped(rows, width, dtype=WIDE), shaped(rows, width), shaped(1, width, dtype=WIDE)]
        + [shaped(micro, rows // micro, 256)] * GROUPS,
        [pltpu.VMEM((width, width), LOW)],
        flops=2 * rows * width * 1024,
    )
    return results[0], results[1], results[2], list(results[3:])


def with_rows(index, rows, count, action):
    if rows % 8 == 0:
        action(pl.ds(pl.multiple_of(index * rows, 8), rows))
        return
    for known in range(count):

        @pl.when(index == known)
        def _():
            action(slice(known * rows, known * rows + rows))


def write_chunks(place_ref, full_ref, keep_ref, send_ref):
    parts_f, halves, rows, _ = keep_ref.shape
    for i in range(parts_f):
        for k in range(halves):
            for odd, ref in ((0, keep_ref), (1, send_ref)):
                index = (place_ref[2] ^ i) * (2 * halves) + (place_ref[1] ^ (2 * k + odd))

                def copy(at):
                    ref[i, k] = full_ref[at, :].astype(ref.dtype)

                with_rows(index, rows, 2 * halves * parts_f, copy)


def out_grads_kernel(place_ref, low_ref, *refs):
    o_refs = refs[:GROUPS]
    keep_ref, send_ref, full_ref = refs[GROUPS:]
    micro, rows, _ = o_refs[0].shape
    low = low_ref[...]
    for d in range(GROUPS):
        both = t_dot(o_refs[d][...].reshape(micro * rows, 256), low)
        at = group_rows(place_ref, d)
        full_ref[pl.ds(pl.multiple_of(at, 64), 128), :] = both[:128]
        full_ref[pl.ds(pl.multiple_of(at + 128, 64), 64), :] = both[192:]
    write_chunks(place_ref, full_ref, keep_ref, send_ref)


def out_grads(place, low, o_slots, parts_f, fast):
    rows, width = low.shape
    chunk = (parts_f, fast // 2, width // (parts_f * fast), width)
    return call(
        out_grads_kernel,
        "out_grads",
        place,
        [low, *o_slots],
        [shaped(*chunk, dtype=WIDE), shaped(*chunk)],
        [pltpu.VMEM((width, width), WIDE)],
        flops=2 * rows * width * 1024,
    )


def input_grads_kernel(parts_f, count, place_ref, act_ref, dq_ref, *refs):
    dkv_refs, refs = refs[:count], refs[count:]
    w_refs, refs = refs[:parts_f], refs[parts_f:]
    one_refs, refs = refs[:GROUPS], refs[GROUPS:]
    keep_ref, send_ref, full_ref, sums_ref, both_ref = refs
    place_rows(full_ref, w_refs, place_ref[2])
    groups, rows, width = act_ref.shape
    micro = dq_ref.shape[1]
    for d in range(GROUPS):
        dkv = sum(r[d].astype(WIDE) for r in dkv_refs).astype(LOW).reshape(rows, 384)
        both = jnp.concatenate([dq_ref[d].reshape(rows, 256), dkv], axis=1)
        both_ref[d] = both
        one = dot_t(both, full_ref[...]).astype(LOW)
        one_refs[d][...] = one.reshape(micro, rows // micro, width)
    sums_ref[...] = t_dot(act_ref[...].reshape(groups * rows, width), both_ref[...].reshape(groups * rows, 640))
    write_chunks(place_ref, sums_ref, keep_ref, send_ref)


def input_grads(place, act, dq, dkv_list, w_slots, fast):
    groups, rows, width = act.shape
    micro = dq.shape[1]
    parts_f = len(w_slots)
    chunk = (parts_f, fast // 2, width // (parts_f * fast), 640)
    results = call(
        functools.partial(input_grads_kernel, parts_f, len(dkv_list)),
        "input_grads",
        place,
        [act, dq, *dkv_list, *w_slots],
        [shaped(micro, rows // micro, width)] * GROUPS + [shaped(*chunk, dtype=WIDE), shaped(*chunk)],
        [
            pltpu.VMEM((width, 640), LOW),
            pltpu.VMEM((width, 640), WIDE),
            pltpu.VMEM((groups, rows, 640), LOW),
        ],
        flops=4 * groups * rows * width * 640,
    )
    return list(results[:GROUPS]), results[-2], results[-1]


def last_kernel(count, place_ref, gain_ref, x_ref, grad_ref, resid_ref, *refs):
    one_refs, refs = refs[:GROUPS], refs[GROUPS:]
    out_refs, refs = refs[:count], refs[count:]
    x_grad_ref, out_ref, gain_out = refs
    micro, rows, width = x_ref.shape
    grad_one = sum(r[...].reshape(micro * rows, width).astype(WIDE) for r in one_refs)
    x = x_ref[...].reshape(micro * rows, width).astype(WIDE)
    scale = rms_scale(x)
    normed = x * scale
    gain_out[...] = jnp.sum(grad_one * normed, axis=0, keepdims=True)
    x_grad_ref[...] = grad_ref[...] + norm_back(grad_one * gain_ref[...], normed, scale)
    out_ref[...] = (resid_ref[...] + sum(r[...].astype(WIDE) for r in out_refs)).astype(LOW)


def last(place, gain, x, grad, resid, one_list, out_list):
    rows, width = resid.shape
    return call(
        functools.partial(last_kernel, len(out_list)),
        "last",
        place,
        [gain, x, grad, resid, *one_list, *out_list],
        [shaped(rows, width, dtype=WIDE), shaped(rows, width), shaped(1, width, dtype=WIDE)],
    )


def feed_finish_kernel(parts_f, fast, place_ref, *refs):
    total = fast * GROUPS
    pair_refs, down_refs = refs[:total], refs[total : 2 * total]
    gate_ref, up_ref, down_ref, pack_ref = refs[2 * total :]
    rows, double = pair_refs[0].shape
    cols = double // 2
    piece = cols // parts_f
    for j in range(fast):
        other = place_ref[1] ^ j
        for d in range(GROUPS):
            at = pl.ds(pl.multiple_of(lax.rem(place_ref[0] + GROUPS - d, GROUPS) * rows, 8), rows)
            pair = pair_refs[j * GROUPS + d]
            for start, ref in ((0, gate_ref), (cols, up_ref)):
                for k in range(parts_f):
                    value = pair[:, start + k * piece : start + (k + 1) * piece].astype(WIDE)
                    if piece % 128 == 0:
                        to = pl.multiple_of(k * fast * piece + other * piece, 128)
                        ref[at, pl.ds(to, piece)] = value
                    else:
                        for l in range(fast):

                            @pl.when(other == l)
                            def _():
                                ref[at, (k * fast + l) * piece : (k * fast + l + 1) * piece] = value

            pack_ref[at, :] = down_refs[j * GROUPS + d][...].astype(WIDE)
        for r, c, to_r, to_c, n, w in packing(piece, rows * GROUPS):
            at = pl.ds(pl.multiple_of(other * piece + r, 8), n)
            down_ref[at, c : c + w] = pack_ref[to_r : to_r + n, to_c : to_c + w]


def feed_finish(place, pair_slots, down_slots, parts_f, fast):
    rows, double = pair_slots[0].shape
    cols = double // 2
    piece = cols // parts_f
    return call(
        functools.partial(feed_finish_kernel, parts_f, fast),
        "feed_finish",
        place,
        [*pair_slots, *down_slots],
        [
            shaped(rows * GROUPS, cols * fast, dtype=WIDE),
            shaped(rows * GROUPS, cols * fast, dtype=WIDE),
            shaped(piece * fast, rows * GROUPS * parts_f, dtype=WIDE),
        ],
        [pltpu.VMEM((rows * GROUPS, cols), WIDE)],
    )


def input_finish_kernel(fast, place_ref, *refs):
    total = fast * GROUPS
    in_refs, out_refs = refs[:total], refs[total : total + fast]
    query_ref, key_ref, value_ref, out_ref = refs[total + fast :]
    rows = out_refs[0].shape[0]
    for j in range(fast):
        value = out_refs[j][...].astype(WIDE)

        def place_out(at):
            out_ref[at, :] = value

        with_rows(place_ref[1] ^ j, rows, fast, place_out)
    for h in range(GROUPS):

        @pl.when(place_ref[0] == h)
        def _():
            for j in range(fast):
                blocks = [in_refs[j * GROUPS + (h - g) % GROUPS][...].astype(WIDE) for g in range(GROUPS)]
                query = jnp.concatenate([b[:, :192] for b in blocks], axis=1)
                key = jnp.concatenate([b[:, 256:448] for b in blocks], axis=1)
                value = jnp.concatenate([part for b in blocks for part in (b[:, 512:640], b[:, 448:512])], axis=1)

                def place_in(at):
                    query_ref[at, :] = query
                    key_ref[at, :] = key
                    value_ref[at, :] = value

                with_rows(place_ref[1] ^ j, rows, fast, place_in)


def input_finish(place, in_slots, out_slots, fast):
    rows, width = out_slots[0].shape
    return call(
        functools.partial(input_finish_kernel, fast),
        "input_finish",
        place,
        [*in_slots, *out_slots],
        [shaped(rows * fast, width, dtype=WIDE)] * 4,
    )


def spread_groups(v):
    return [v] + [shift(v, d) for d in range(1, GROUPS)]


def sum_groups(v, hi):
    keep = lax.dynamic_index_in_dim(v, hi, 0, keepdims=False)
    for d in range(1, GROUPS):
        part = lax.dynamic_index_in_dim(v, (hi + d) % GROUPS, 0, keepdims=False).astype(LOW)
        keep = keep + shift(part, d).astype(WIDE)
    return keep


def gather_all(v, fast):
    by_group = spread_groups(v)
    by_slot = [slots_out(one, "ctx", fast) for one in by_group]
    return [by_slot[d][j] for j in range(fast) for d in range(GROUPS)]


def body(
    tokens,
    offsets,
    norm1_gain,
    norm2_gain,
    bias_table,
    w_query,
    w_key,
    w_value,
    w_out,
    w_gate,
    w_up,
    w_down,
    cotangent,
):
    micro, _, block_rows, width = tokens.shape
    blocks = lax.axis_size("ctx")
    parts_f = lax.axis_size("fsdp")
    fast = blocks // GROUPS
    ctx = lax.axis_index("ctx")
    f = lax.axis_index("fsdp")
    hi, lo = ctx // fast, ctx % fast
    group_cols = w_query.shape[1] // GROUPS
    own_rows = micro * block_rows
    hidden = w_gate.shape[1]
    piece = hidden // (parts_f * fast)
    part_rows = w_query.shape[0]
    gain_one = norm1_gain.reshape(1, width)
    gain_two = norm2_gain.reshape(1, width)
    place = jnp.stack([hi, lo, f]).astype(jnp.int32)

    own_x = tokens[:, 0]
    g_low = cotangent[:, 0].reshape(own_rows, width)
    x_slots = spread_groups(own_x)

    def group_of(matrix):
        return lax.dynamic_slice_in_dim(matrix, hi * group_cols, group_cols, axis=1)

    q_part, k_part, v_part = group_of(w_query), group_of(w_key), group_of(w_value)
    gap = jnp.zeros((part_rows, 64), LOW)
    qkv_part = jnp.concatenate([q_part, gap, k_part, v_part[:, 128:], v_part[:, :128]], axis=1)
    qkv_slots = slots_out(qkv_part, "fsdp", parts_f)
    out_w_slots = slots_out(w_out, "fsdp", parts_f)

    def piece_cols(matrix):
        viewed = matrix.reshape(part_rows, parts_f, fast, piece)
        return lax.dynamic_index_in_dim(viewed, lo, 2, keepdims=False).reshape(part_rows, parts_f * piece)

    pair_slots = slots_out(jnp.concatenate([piece_cols(w_gate), piece_cols(w_up)], axis=1), "fsdp", parts_f)
    down_part = lax.dynamic_index_in_dim(w_down.reshape(fast, piece, width), lo, 0, keepdims=False)
    down_slots = slots_out(down_part, "fsdp", parts_f)
    g_slots = slots_out(g_low, "ctx", fast)

    starts = offsets[:, 0]
    group_ids = (hi + GROUPS - jnp.arange(GROUPS, dtype=jnp.int32)) % GROUPS
    slot_ids = lo ^ jnp.arange(fast, dtype=jnp.int32)
    kplace = jnp.take(starts, group_ids[None, :] * fast + slot_ids[:, None], axis=1)
    qplace = kplace[:, 0]
    places = (qplace, kplace)
    table_group = lax.dynamic_slice_in_dim(bias_table, hi * 3, 3, axis=1)
    strip = make_strip(table_group, blocks)

    act_one, q, kv = project(place, gain_one, x_slots, qkv_slots)
    kv_slots = slots_out(kv, "ctx", fast)
    o_group, lse = attention_forward(places, strip, q, kv_slots, blocks)
    o_slots = [o_group[0]] + [shift(o_group[d], -d) for d in range(1, GROUPS)]
    resid, act_two = joined(place, gain_two, own_x, o_slots, out_w_slots)
    act_slots = slots_out(act_two, "ctx", fast)
    two_parts, out_parts, hid, grads = feed(place, act_slots, g_slots, pair_slots, down_slots)
    two_list = slots_back(two_parts, "ctx", fast)
    pair_grads, down_grads = feed_grads(place, act_slots, g_slots, hid, grads, parts_f)
    grad_resid, grad_low, gain_two_part, do_own = branch(place, gain_two, resid, g_low, two_list, out_w_slots, micro)
    do_slots = [do_own[0]] + [shift(do_own[d], d) for d in range(1, GROUPS)]

    def over_weights(parts):
        total = sum(v.astype(WIDE) for v in slots_back(parts, "fsdp", parts_f))
        return total.reshape(GROUPS, part_rows // GROUPS, -1)

    pair_sum = over_weights(pair_grads)
    pair_all = gather_all(sum_groups(pair_sum, hi).astype(LOW), fast)
    dq, dkv_parts, table_part = lax.optimization_barrier(
        attention_backward(places, place, strip, q, kv_slots, do_slots, lse, blocks)
    )
    dkv_list = slots_back(dkv_parts, "ctx", fast)
    down_sum = over_weights(down_grads)
    down_all = gather_all(sum_groups(down_sum, hi).astype(LOW), fast)
    out_list = slots_back(out_parts, "ctx", fast)

    def over_chunks(keep, send):
        total = keep + hop(send, "ctx", 1).astype(WIDE)
        total = halve(total, "fsdp", 1)
        return halve(total, "ctx", 2)

    out_chunk = over_chunks(*out_grads(place, grad_low, o_slots, parts_f, fast))
    for bit in bits_up(GROUPS):
        low = out_chunk.astype(LOW)
        out_chunk = low.astype(WIDE) + hop(low, "ctx", bit * fast).astype(WIDE)
    out_all = slots_out(out_chunk.astype(LOW), "ctx", fast)

    one_parts, keep, send = input_grads(place, act_one, dq, dkv_list, qkv_slots, fast)
    in_all = gather_all(over_chunks(keep, send).astype(LOW), fast)
    one_list = [one_parts[0]] + [shift(one_parts[d], -d) for d in range(1, GROUPS)]
    x_grad, result, gain_one_part = last(place, gain_one, own_x, grad_resid, resid, one_list, out_list)

    w_gate_grad, w_up_grad, w_down_grad = feed_finish(place, pair_all, down_all, parts_f, fast)
    w_query_grad, w_key_grad, w_value_grad, w_out_grad = input_finish(place, in_all, out_all, fast)

    head_count = bias_table.shape[1]
    small = jnp.concatenate([gain_one_part.reshape(-1, 128), gain_two_part.reshape(-1, 128), table_part], axis=0)
    for bit in bits_up(parts_f):
        small = small + hop(small, "fsdp", bit)
    for bit in bits_up(blocks):
        small = small + hop(small, "ctx", bit)
    lines = width // 128
    gain_rows = width // parts_f
    table_rows = bias_table.shape[0] // parts_f
    gain_one_grad = lax.dynamic_slice_in_dim(small[:lines].reshape(width), f * gain_rows, gain_rows)
    gain_two_grad = lax.dynamic_slice_in_dim(small[lines : 2 * lines].reshape(width), f * gain_rows, gain_rows)
    table_grad = lax.dynamic_slice(small, (2 * lines + f * table_rows, 0), (table_rows, head_count))

    return (
        result.reshape(micro, 1, block_rows, width),
        x_grad.reshape(micro, 1, block_rows, width),
        gain_one_grad,
        gain_two_grad,
        table_grad,
        w_query_grad,
        w_key_grad,
        w_value_grad,
        w_out_grad,
        w_gate_grad,
        w_up_grad,
        w_down_grad,
    )


def solution(mesh):
    in_specs = (
        P(None, "fsdp", "ctx", None),
        P(None, "fsdp", None),
        P(),
        P(),
        P(),
        P("fsdp", None),
        P("fsdp", None),
        P("fsdp", None),
        P("fsdp", None),
        P("fsdp", None),
        P("fsdp", None),
        P("fsdp", None),
        P(None, "fsdp", "ctx", None),
    )
    out_specs = (
        P(None, "fsdp", "ctx", None),
        P(None, "fsdp", "ctx", None),
        P("fsdp"),
        P("fsdp"),
        P("fsdp", None),
        P("fsdp", None),
        P("fsdp", None),
        P("fsdp", None),
        P("fsdp", None),
        P("fsdp", None),
        P("fsdp", None),
        P("fsdp", None),
    )
    return jax.shard_map(body, mesh=mesh, in_specs=in_specs, out_specs=out_specs, check_vma=False)
```

```python
import functools

import jax
import jax.numpy as jnp
from jax import lax
from jax.experimental import pallas as pl
from jax.experimental.pallas import tpu as pltpu
from jax.sharding import PartitionSpec as P

EPSILON = 1e-06
GROUPS = 4
WIDE = jnp.float32
LOW = jnp.bfloat16
FAR = 91
NEAR_LEAD = 96
VMEM_LIMIT = 60 * 1024 * 1024


def dot(a, b):
    return jnp.dot(a, b, preferred_element_type=WIDE)


def dot_t(a, b):
    return lax.dot_general(a, b, (((1,), (1,)), ((), ())), preferred_element_type=WIDE)


def t_dot(a, b):
    return lax.dot_general(a, b, (((0,), (0,)), ((), ())), preferred_element_type=WIDE)


def bucket_of(relative):
    distance = jnp.abs(relative)
    squared = distance * distance
    counted = jnp.zeros_like(relative)
    for exponent in range(1, 8):
        counted = counted + (squared >= 64 * 2**exponent).astype(jnp.int32)
    within = jnp.where(distance < 8, distance, 8 + counted)
    return jnp.where(relative > 0, 16, 0).astype(jnp.int32) + within


def hop(v, axis, bit):
    size = lax.axis_size(axis)
    return lax.ppermute(v, axis, [(i, i ^ bit) for i in range(size)])


def bits_down(size):
    bit = size // 2
    while bit >= 1:
        yield bit
        bit //= 2


def bits_up(size):
    return reversed(list(bits_down(size)))


def shift(v, steps):
    size = lax.axis_size("ctx")
    stride = size // GROUPS
    return lax.ppermute(v, "ctx", [(i, (i + steps * stride) % size) for i in range(size)])


def slots_out(v, axis, count):
    slots = {0: v}
    for bit in bits_down(count):
        for j in list(slots):
            slots[j ^ bit] = hop(slots[j], axis, bit)
    return [slots[j] for j in range(count)]


def pairs_on(parts, got, count):
    own, evens, _ = parts
    have = {k: evens[k - 1].astype(WIDE) + got[k].astype(WIDE) for k in range(1, count // 2)}
    mine, sent = [(own, False), (got, True)], []
    for bit in bits_up(count // 2):
        for k in sorted(have):
            if k & bit:
                sent.append(have[k].astype(LOW))
                part = hop(sent[-1], "ctx", 2 * bit)
                if k ^ bit:
                    have[k ^ bit] = have[k ^ bit] + part.astype(WIDE)
                else:
                    mine.append((part, False))
                del have[k]
    return mine, sent


def pairs_back(own, evens, odds, count):
    return pairs_on((own, evens, odds), hop(odds, "ctx", 1), count)


def halve(v, axis, unit):
    count = v.shape[0]
    for bit in bits_down(count):
        v = v[:bit] + hop(v[bit:].astype(LOW), axis, bit * unit).astype(WIDE)
    return v[0]


def strip_kernel(blocks, table_ref, strip_ref):
    centre = 64 * (blocks - 1)
    rows = 2 * 64 * blocks
    near = 256
    start = centre - NEAR_LEAD
    chunk = 128
    heads = table_ref.shape[1]

    def relative(first, count):
        u = lax.broadcasted_iota(jnp.int32, (count, 128), 0) + first
        i = lax.broadcasted_iota(jnp.int32, (count, 128), 1)
        return u - centre - jnp.where(i >= 64, i - 64, i)

    for h in range(heads):
        strip_ref[h, : start, :] = jnp.full((start, 128), table_ref[15, h], WIDE)
        strip_ref[h, start + near :, :] = jnp.full((rows - start - near, 128), table_ref[31, h], WIDE)
    for first in range(start, start + near, chunk):
        label = bucket_of(relative(first, chunk))
        for h in range(heads):
            value = jnp.zeros((chunk, 128), WIDE)
            for b in range(32):
                value = jnp.where(label == b, table_ref[b, h], value)
            strip_ref[h, first : first + chunk, :] = value


def make_strip(table_group, blocks):
    heads = table_group.shape[1]
    return pl.pallas_call(
        functools.partial(strip_kernel, blocks),
        out_shape=jax.ShapeDtypeStruct((heads, 2 * 64 * blocks, 128), WIDE),
        in_specs=[pl.BlockSpec(memory_space=pltpu.SMEM)],
        out_specs=pl.BlockSpec(memory_space=pltpu.VMEM),
        compiler_params=pltpu.CompilerParams(vmem_limit_bytes=VMEM_LIMIT),
        name="bias_strip",
    )(table_group)


def split_heads(wide, second_upper):
    lane = lax.broadcasted_iota(jnp.int32, (wide.shape[0], 128), 1)
    low = lane < 64
    zero = jnp.zeros((wide.shape[0], 128), wide.dtype)
    first, second = wide[:, :128], wide[:, 128:]
    third = jnp.where(low, zero, second) if second_upper else jnp.where(low, second, zero)
    return [jnp.where(low, first, zero), jnp.where(low, zero, first), third]


KEY_COLS = (0, 0, 128)
VALUE_COLS = (256, 256, 128)


def sort_blocks(count, m, kplace_ref, kv_refs, sorted_ref):
    for j in range(count):
        for e in range(GROUPS):
            to = pl.multiple_of(kplace_ref[m, j, e] * 64, 64)
            sorted_ref[pl.ds(to, 64), :] = kv_refs[j][e, 0]


def bias_of(strip_ref, h, offs, half, rows, low):
    a = strip_ref[h, pl.ds(offs[2 * half], rows), :]
    b = strip_ref[h, pl.ds(offs[2 * half + 1], rows), :]
    return jnp.where(low, a, b)


def forward_kernel(count, blocks, qplace_ref, kplace_ref, strip_ref, q_ref, *refs):
    kv_refs = refs[:count]
    o_refs = refs[count : count + GROUPS]
    lse_ref, sorted_ref = refs[count + GROUPS :]
    m = pl.program_id(0)
    rows = 64 * blocks
    sort_blocks(count, m, kplace_ref, kv_refs, sorted_ref)
    offs = [pl.multiple_of((blocks - 1 - qplace_ref[m, e]) * 64, 64) for e in range(GROUPS)]
    queries = split_heads(q_ref[:, 0].reshape(GROUPS * 64, 256), False)
    low = lax.broadcasted_iota(jnp.int32, (rows, 128), 1) < 64
    mixed = []
    for h in range(3):
        keys = sorted_ref[:, KEY_COLS[h] : KEY_COLS[h] + 128]
        values = sorted_ref[:, VALUE_COLS[h] : VALUE_COLS[h] + 128]
        scores = dot_t(keys, queries[h])
        parts = []
        for half in range(2):
            s = scores[:, half * 128 : half * 128 + 128] + bias_of(strip_ref, h, offs, half, rows, low)
            top = jnp.max(s, axis=0, keepdims=True)
            e = jnp.exp(s - top)
            total = jnp.sum(e, axis=0, keepdims=True)
            lse_ref[0, h : h + 1, half * 128 : half * 128 + 128] = top + jnp.log(total)
            parts.append((e * (1.0 / total)).astype(LOW))
        weights = jnp.concatenate(parts, axis=1)
        mixed.append(t_dot(values, weights))
    sub = lax.broadcasted_iota(jnp.int32, (128, GROUPS * 64), 0) < 64
    first = jnp.where(sub, mixed[0], mixed[1]).T
    second = jnp.where(sub, 0.0, mixed[2]).T
    out = jnp.concatenate([first, second], axis=1).astype(LOW)
    for d in range(GROUPS):
        o_refs[d][0] = out[d * 64 : d * 64 + 64]


def attention_forward(places, strip, q, kv_slots, blocks):
    qplace, kplace = places
    count = len(kv_slots)
    micro = q.shape[1]
    rows = 64 * blocks
    kv_cols = kv_slots[0].shape[-1]
    by_micro = lambda width: pl.BlockSpec((GROUPS, 1, 64, width), lambda m, *_: (0, m, 0, 0))
    results = pl.pallas_call(
        functools.partial(forward_kernel, count, blocks),
        out_shape=(jax.ShapeDtypeStruct((micro, 64, 256), LOW),) * GROUPS
        + (jax.ShapeDtypeStruct((micro, 3, GROUPS * 64), WIDE),),
        grid_spec=pltpu.PrefetchScalarGridSpec(
            num_scalar_prefetch=2,
            grid=(micro,),
            in_specs=[pl.BlockSpec(strip.shape, lambda m, *_: (0, 0, 0)), by_micro(256)] + [by_micro(kv_cols)] * count,
            out_specs=(pl.BlockSpec((1, 64, 256), lambda m, *_: (m, 0, 0)),) * GROUPS
            + (pl.BlockSpec((1, 3, GROUPS * 64), lambda m, *_: (m, 0, 0)),),
            scratch_shapes=[pltpu.VMEM((rows, kv_cols), LOW)],
        ),
        compiler_params=pltpu.CompilerParams(vmem_limit_bytes=VMEM_LIMIT),
        cost_estimate=pl.CostEstimate(
            flops=micro * 3 * 2 * 2 * rows * GROUPS * 64 * 128 * 2,
            bytes_accessed=micro * rows * kv_cols * 4,
            transcendentals=micro * 3 * rows * GROUPS * 64,
        ),
        name="attention_forward",
    )(qplace, kplace, strip, q, *kv_slots)
    return list(results[:GROUPS]), results[GROUPS]


def backward_kernel(count, blocks, qplace_ref, kplace_ref, place_ref, strip_ref, q_ref, lse_ref, *refs):
    do_refs, refs = refs[:GROUPS], refs[GROUPS:]
    kv_refs = refs[:count]
    dq_ref = refs[count]
    own_ref, even_ref, odd_ref, table_ref = refs[count + 1 : count + 5]
    sorted_ref, grad_ref, lower_ref, upper_ref = refs[count + 5 :]
    m = pl.program_id(0)
    rows = 64 * blocks

    @pl.when(m == 0)
    def _():
        lower_ref[...] = jnp.zeros_like(lower_ref)
        upper_ref[...] = jnp.zeros_like(upper_ref)

    sort_blocks(count, m, kplace_ref, kv_refs, sorted_ref)
    offs = [pl.multiple_of((blocks - 1 - qplace_ref[m, e]) * 64, 64) for e in range(GROUPS)]
    queries = split_heads(q_ref[:, 0].reshape(GROUPS * 64, 256), False)
    grads = split_heads(jnp.concatenate([r[0] for r in do_refs], axis=0), True)
    low = lax.broadcasted_iota(jnp.int32, (rows, 128), 1) < 64
    query_grads, scores_grads, soft = [], [], []
    for h in range(3):
        keys = sorted_ref[:, KEY_COLS[h] : KEY_COLS[h] + 128]
        values = sorted_ref[:, VALUE_COLS[h] : VALUE_COLS[h] + 128]
        scores = dot_t(keys, queries[h])
        weight_grads = dot_t(values, grads[h])
        ds_parts, p_parts = [], []
        for half in range(2):
            cols = slice(half * 128, half * 128 + 128)
            s = scores[:, cols] + bias_of(strip_ref, h, offs, half, rows, low)
            p = jnp.exp(s - lse_ref[0, h : h + 1, cols])
            dp = weight_grads[:, cols]
            delta = jnp.sum(p * dp, axis=0, keepdims=True)
            ds = (p * (dp - delta)).astype(LOW)
            p_parts.append(p.astype(LOW))
            ds_parts.append(ds)
            wide = ds.astype(WIDE)
            at = pl.ds(offs[2 * half], rows)
            lower_ref[h, at, :] += wide
            at = pl.ds(offs[2 * half + 1], rows)
            upper_ref[h, at, :] += wide
        ds_all = jnp.concatenate(ds_parts, axis=1)
        p_all = jnp.concatenate(p_parts, axis=1)
        query_grads.append(t_dot(keys, ds_all))
        scores_grads.append(ds_all)
        soft.append(p_all)
    sub = lax.broadcasted_iota(jnp.int32, (128, GROUPS * 64), 0) < 64
    first = jnp.where(sub, query_grads[0], query_grads[1]).T
    second = jnp.where(sub, query_grads[2], 0.0).T
    dq_ref[:, 0] = jnp.concatenate([first, second], axis=1).astype(LOW).reshape(GROUPS, 64, 256)
    grad_ref[:, 0:128] = dot(scores_grads[0], queries[0]) + dot(scores_grads[1], queries[1])
    grad_ref[:, 128:256] = dot(scores_grads[2], queries[2]) + dot(soft[2], grads[2])
    grad_ref[:, 256:384] = dot(soft[0], grads[0]) + dot(soft[1], grads[1])
    for j in range(count):
        for e in range(GROUPS):
            at = pl.multiple_of(kplace_ref[m, j, e] * 64, 64)
            value = grad_ref[pl.ds(at, 64), :]
            if j == 0:
                own_ref[e, 0] = value
            elif j % 2:
                odd_ref[j // 2, e, 0] = value.astype(LOW)
            else:
                even_ref[j // 2 - 1, e, 0] = value.astype(LOW)

    @pl.when(m == pl.num_programs(0) - 1)
    def _():
        centre = 64 * (blocks - 1)
        start = centre - NEAR_LEAD
        near = 256
        sums_row = lax.broadcasted_iota(jnp.int32, (32, 128), 0)
        side = lax.broadcasted_iota(jnp.int32, (near, 128), 1)
        rel = lax.broadcasted_iota(jnp.int32, (near, 128), 0) + (start - centre) - jnp.where(side >= 64, side - 64, side)
        label = bucket_of(rel)

        def folded(h, first, size):
            lane = lax.broadcasted_iota(jnp.int32, (size, 128), 1) < 64
            return jnp.where(lane, lower_ref[h, first : first + size, :], upper_ref[h, first : first + size, :])

        table = jnp.zeros((32, 128), WIDE)
        for h in range(3):
            before = jnp.sum(folded(h, 0, start), axis=0, keepdims=True)
            last = start + near
            after = jnp.sum(folded(h, last, 2 * rows - last), axis=0, keepdims=True)
            window = folded(h, start, near)
            result = jnp.where(sums_row == 15, before, jnp.where(sums_row == 31, after, 0.0))
            for b in range(32):
                part = jnp.sum(jnp.where(label == b, window, 0.0), axis=0, keepdims=True)
                result = result + jnp.where(sums_row == b, part, 0.0)
            total = jnp.sum(result, axis=1, keepdims=True)
            lanes = lax.broadcasted_iota(jnp.int32, (32, 128), 1)
            table = jnp.where(lanes == place_ref[0] * 3 + h, total, table)
        table_ref[...] = table


def attention_backward(places, place, strip, q, kv_slots, do_slots, lse, blocks):
    qplace, kplace = places
    count = len(kv_slots)
    micro = q.shape[1]
    rows = 64 * blocks
    kv_cols = kv_slots[0].shape[-1]
    by_micro = lambda width: pl.BlockSpec((GROUPS, 1, 64, width), lambda m, *_: (0, m, 0, 0))
    kv_shape = kv_slots[0].shape
    by_part = lambda n: pl.BlockSpec((n, GROUPS, 1, 64, kv_cols), lambda m, *_: (0, 0, m, 0, 0))
    results = pl.pallas_call(
        functools.partial(backward_kernel, count, blocks),
        out_shape=(jax.ShapeDtypeStruct(q.shape, LOW),)
        + (
            jax.ShapeDtypeStruct(kv_shape, WIDE),
            jax.ShapeDtypeStruct((count // 2 - 1,) + kv_shape, LOW),
            jax.ShapeDtypeStruct((count // 2,) + kv_shape, LOW),
        )
        + (jax.ShapeDtypeStruct((32, 128), WIDE),),
        grid_spec=pltpu.PrefetchScalarGridSpec(
            num_scalar_prefetch=3,
            grid=(micro,),
            in_specs=[
                pl.BlockSpec(strip.shape, lambda m, *_: (0, 0, 0)),
                by_micro(256),
                pl.BlockSpec((1, 3, GROUPS * 64), lambda m, *_: (m, 0, 0)),
            ]
            + [pl.BlockSpec((1, 64, 256), lambda m, *_: (m, 0, 0))] * GROUPS
            + [by_micro(kv_cols)] * count,
            out_specs=(by_micro(256),)
            + (by_micro(kv_cols), by_part(count // 2 - 1), by_part(count // 2))
            + (pl.BlockSpec((32, 128), lambda m, *_: (0, 0)),),
            scratch_shapes=[
                pltpu.VMEM((rows, kv_cols), LOW),
                pltpu.VMEM((rows, kv_cols), WIDE),
                pltpu.VMEM((3, 2 * rows, 128), WIDE),
                pltpu.VMEM((3, 2 * rows, 128), WIDE),
            ],
        ),
        compiler_params=pltpu.CompilerParams(vmem_limit_bytes=VMEM_LIMIT),
        cost_estimate=pl.CostEstimate(
            flops=micro * 3 * 5 * 2 * rows * GROUPS * 64 * 128 * 2,
            bytes_accessed=micro * rows * kv_cols * 8,
            transcendentals=micro * 3 * rows * GROUPS * 64,
        ),
        name="attention_backward",
    )(qplace, kplace, place, strip, q, lse, *do_slots, *kv_slots)
    return results[0], results[1:4], results[4]


PLACE = pl.BlockSpec(memory_space=pltpu.SMEM)


def whole(count):
    return [pl.BlockSpec(memory_space=pltpu.VMEM)] * count


def first_entry(v):
    return pl.BlockSpec((1,) + v.shape[1:], lambda _: (0,) * v.ndim)


def call(kernel, name, place, operands, out_shape, scratch=(), flops=0):
    operands = [v if isinstance(v, tuple) else (v, False) for v in operands]
    grid = {"grid": (1,)} if any(first for _, first in operands) else {}
    specs = [PLACE] + [first_entry(v) if first else whole(1)[0] for v, first in operands]
    operands = [v for v, _ in operands]
    size = sum(v.size * v.dtype.itemsize for v in operands) + sum(
        v.size * jnp.dtype(v.dtype).itemsize for v in out_shape
    )
    return pl.pallas_call(
        kernel,
        out_shape=tuple(out_shape),
        **grid,
        in_specs=specs,
        out_specs=tuple(whole(len(out_shape))),
        scratch_shapes=list(scratch),
        compiler_params=pltpu.CompilerParams(vmem_limit_bytes=VMEM_LIMIT),
        cost_estimate=pl.CostEstimate(flops=flops, bytes_accessed=size, transcendentals=0),
        name=name,
    )(place, *operands)


def shaped(*shape, dtype=LOW):
    return jax.ShapeDtypeStruct(shape, dtype)


def place_rows(full_ref, slot_refs, index):
    rows = slot_refs[0].shape[0]
    for j, ref in enumerate(slot_refs):
        full_ref[pl.ds(pl.multiple_of((index ^ j) * rows, rows), rows), :] = ref[...]


def rms_scale(values):
    return lax.rsqrt(jnp.mean(values * values, axis=-1, keepdims=True) + EPSILON)


def norm_back(grad_normed, normed, scale):
    return scale * (grad_normed - normed * jnp.mean(grad_normed * normed, axis=-1, keepdims=True))


def project_kernel(parts_f, place_ref, gain_ref, *refs):
    x_refs, w_refs = refs[:GROUPS], refs[GROUPS : GROUPS + parts_f]
    act_ref, q_ref, kv_ref, full_ref = refs[GROUPS + parts_f :]
    place_rows(full_ref, w_refs, place_ref[2])
    micro, rows, width = x_refs[0].shape
    for d in range(GROUPS):
        x = x_refs[d][...].reshape(micro * rows, width).astype(WIDE)
        act = (x * rms_scale(x) * gain_ref[...]).astype(LOW)
        act_ref[d] = act
        both = dot(act, full_ref[...]).astype(LOW)
        q_ref[d] = both[:, :256].reshape(micro, rows, 256)
        kv_ref[d] = both[:, 256:].reshape(micro, rows, 384)


def project(place, gain, x_slots, w_slots):
    micro, rows, width = x_slots[0].shape
    return call(
        functools.partial(project_kernel, len(w_slots)),
        "project",
        place,
        [gain, *x_slots, *w_slots],
        [
            shaped(GROUPS, micro * rows, width),
            shaped(GROUPS, micro, rows, 256),
            shaped(GROUPS, micro, rows, 384),
        ],
        [pltpu.VMEM((width, 640), LOW)],
        flops=2 * GROUPS * micro * rows * width * 640,
    )


def group_rows(place_ref, d):
    return lax.rem(place_ref[0] + d, GROUPS) * 192


def joined_kernel(parts_f, place_ref, gain_ref, x_ref, *refs):
    o_refs, w_refs = refs[:GROUPS], refs[GROUPS : GROUPS + parts_f]
    resid_ref, act_ref, full_ref = refs[GROUPS + parts_f :]
    place_rows(full_ref, w_refs, place_ref[2])
    micro, rows, width = x_ref.shape
    total = x_ref[...].reshape(micro * rows, width).astype(WIDE)
    for d in range(GROUPS):
        o = o_refs[d][...].reshape(micro * rows, 256)
        at = group_rows(place_ref, d)
        total += dot(o[:, :128], full_ref[pl.ds(pl.multiple_of(at, 64), 128), :])
        total += dot(o[:, 128:], full_ref[pl.ds(pl.multiple_of(at + 64, 64), 128), :])
    resid_ref[...] = total
    act_ref[...] = (total * rms_scale(total) * gain_ref[...]).astype(LOW)


def joined(place, gain, x, o_slots, w_slots):
    micro, rows, width = x.shape
    return call(
        functools.partial(joined_kernel, len(w_slots)),
        "joined",
        place,
        [gain, x, *o_slots, *w_slots],
        [shaped(micro * rows, width, dtype=WIDE), shaped(micro * rows, width)],
        [pltpu.VMEM((width, width), LOW)],
        flops=2 * micro * rows * width * 1024,
    )


GELU_A = 0.7978845608028654
GELU_B = 0.044715


def put_part(refs, j, value):
    own_ref, even_ref, odd_ref = refs
    if j == 0:
        own_ref[...] = value
    elif j % 2:
        odd_ref[j // 2] = value.astype(odd_ref.dtype)
    else:
        even_ref[j // 2 - 1] = value.astype(even_ref.dtype)


def part_shapes(shape, fast):
    return [
        shaped(*shape, dtype=WIDE),
        shaped(fast // 2 - 1, *shape),
        shaped(fast // 2, *shape),
    ]


def feed_kernel(parts_f, fast, place_ref, *refs):
    act_refs, refs = refs[:fast], refs[fast:]
    g_refs, refs = refs[:fast], refs[fast:]
    pair_refs, refs = refs[:parts_f], refs[parts_f:]
    down_refs, refs = refs[:parts_f], refs[parts_f:]
    two_refs, out_refs, refs = refs[:3], refs[3:6], refs[6:]
    hid_ref, grad_ref, pair_ref, down_ref = refs
    place_rows(pair_ref, pair_refs, place_ref[2])
    place_rows(down_ref, down_refs, place_ref[2])
    cols = hid_ref.shape[-1]
    for j in range(fast):
        both = dot(act_refs[j][...], pair_ref[...])
        z, up = both[:, :cols], both[:, cols:]
        square = z * z
        t = jnp.tanh(GELU_A * (z + GELU_B * square * z))
        half = 0.5 * (1.0 + t)
        gelu = z * half
        slope = half + (0.5 * z) * (1.0 - t * t) * (GELU_A * (1.0 + 3.0 * GELU_B * square))
        hid = (gelu * up).astype(LOW)
        dh = dot_t(g_refs[j][...], down_ref[...])
        grads = jnp.concatenate([(dh * up * slope).astype(LOW), (dh * gelu).astype(LOW)], axis=1)
        hid_ref[j] = hid
        grad_ref[j] = grads
        put_part(two_refs, j, dot_t(grads, pair_ref[...]))
        put_part(out_refs, j, dot(hid, down_ref[...]))


def feed(place, act_slots, g_slots, pair_slots, down_slots):
    fast, parts_f = len(act_slots), len(pair_slots)
    rows, width = act_slots[0].shape
    cols = down_slots[0].shape[0] * parts_f
    results = call(
        functools.partial(feed_kernel, parts_f, fast),
        "feed",
        place,
        [*act_slots, *g_slots, *pair_slots, *down_slots],
        part_shapes((rows, width), fast) * 2 + [shaped(fast, rows, cols), shaped(fast, rows, 2 * cols)],
        [pltpu.VMEM((width, 2 * cols), LOW), pltpu.VMEM((cols, width), LOW)],
        flops=2 * fast * rows * width * cols * 6,
    )
    return results[:3], results[3:6], results[-2], results[-1]


def packing(piece, rows):
    if rows == 3 * piece:
        return [(0, k * 256, k * piece, 0, piece, 256) for k in range(3)]
    half = piece // 2
    return [
        (0, 0, 0, 0, piece, 512),
        (0, 512, piece, 0, half, 256),
        (half, 512, piece, 256, half, 256),
    ]


def pair_grads_kernel(fast, place_ref, *refs):
    act_refs, grad_ref, refs = refs[:fast], refs[fast], refs[fast + 1 :]
    outs, full_ref = refs[:-1], refs[-1]
    act = jnp.concatenate([r[...] for r in act_refs], axis=0)
    full_ref[...] = t_dot(act, grad_ref[...].reshape(act.shape[0], -1))
    rows = outs[0].shape[0]
    for j, out in enumerate(outs):
        at = pl.multiple_of((place_ref[2] ^ j) * rows, rows)
        out[...] = full_ref[pl.ds(at, rows), :].astype(out.dtype)


def pair_grads(place, act_slots, grads, parts_f):
    fast, rows, double = grads.shape
    width = act_slots[0].shape[1]
    types = [WIDE] + [LOW] * (parts_f - 1)
    return call(
        functools.partial(pair_grads_kernel, fast),
        "pair_grads",
        place,
        [*act_slots, grads],
        [shaped(width // parts_f, double, dtype=t) for t in types],
        [pltpu.VMEM((width, double), WIDE)],
        flops=2 * fast * rows * width * double,
    )


def down_grads_kernel(fast, place_ref, *refs):
    g_refs, hid_ref, refs = refs[:fast], refs[fast], refs[fast + 1 :]
    outs, full_ref = refs[:-1], refs[-1]
    g = jnp.concatenate([r[...] for r in g_refs], axis=0)
    full_ref[...] = t_dot(hid_ref[...].reshape(g.shape[0], -1), g)
    rows = outs[0].shape[0]
    piece = full_ref.shape[0] // len(outs)
    for j, out in enumerate(outs):
        for r, c, to_r, to_c, n, w in packing(piece, rows):
            at = pl.multiple_of((place_ref[2] ^ j) * piece + r, 8)
            out[to_r : to_r + n, to_c : to_c + w] = full_ref[pl.ds(at, n), c : c + w].astype(out.dtype)


def down_grads(place, g_slots, hid, parts_f):
    fast, rows, cols = hid.shape
    width = g_slots[0].shape[1]
    types = [WIDE] + [LOW] * (parts_f - 1)
    return call(
        functools.partial(down_grads_kernel, fast),
        "down_grads",
        place,
        [*g_slots, hid],
        [shaped(width // parts_f, cols, dtype=t) for t in types],
        [pltpu.VMEM((cols, width), WIDE)],
        flops=2 * fast * rows * width * cols,
    )


def group_split_kernel(count, place_ref, *refs):
    own_ref, send_refs = refs[count], refs[count + 1 :]
    rows = own_ref.shape[0]

    def part(d):
        at = pl.ds(pl.multiple_of(lax.rem(place_ref[0] + d, GROUPS) * rows, 8), rows)
        return sum(r[at, :].astype(WIDE) for r in refs[:count])

    own_ref[...] = part(0)
    for d, ref in enumerate(send_refs, 1):
        ref[...] = part(d).astype(ref.dtype)


def group_split(place, parts):
    rows, cols = parts[0].shape
    cut = rows // GROUPS
    results = call(
        functools.partial(group_split_kernel, len(parts)),
        "group_split",
        place,
        parts,
        [shaped(cut, cols, dtype=WIDE)] + [shaped(cut, cols)] * (GROUPS - 1),
    )
    return results[0], list(results[1:])


def group_halves_kernel(count, place_ref, *refs):
    keep_ref, send_ref = refs[count:]
    rows = keep_ref.shape[1]
    for d in range(GROUPS):
        at = pl.ds(pl.multiple_of((place_ref[0] ^ d) * rows, 8), rows)
        total = sum(r[at, :].astype(WIDE) for r in refs[:count])
        if d % 2:
            send_ref[d // 2] = total.astype(send_ref.dtype)
        else:
            keep_ref[d // 2] = total


def group_halves(place, parts):
    rows, cols = parts[0].shape
    cut = (GROUPS // 2, rows // GROUPS, cols)
    return call(
        functools.partial(group_halves_kernel, len(parts)),
        "group_halves",
        place,
        parts,
        [shaped(*cut, dtype=WIDE), shaped(*cut)],
    )


def summed(refs):
    return sum((r[0] if len(r.shape) == 3 else r[...]).astype(WIDE) for r in refs)


def branch_kernel(parts_f, count, place_ref, gain_ref, resid_ref, g_ref, *refs):
    two_refs, refs = refs[:count], refs[count:]
    w_refs, refs = refs[:parts_f], refs[parts_f:]
    grad_ref, low_ref, gain_out = refs[:3]
    do_refs, full_ref = refs[3 : 3 + GROUPS], refs[3 + GROUPS]
    place_rows(full_ref, w_refs, place_ref[2])
    micro, rows, _ = do_refs[0].shape
    grad_two = summed(two_refs)
    resid = resid_ref[...]
    scale = rms_scale(resid)
    normed = resid * scale
    gain_out[...] = jnp.sum(grad_two * normed, axis=0, keepdims=True)
    grad = g_ref[...].astype(WIDE) + norm_back(grad_two * gain_ref[...], normed, scale)
    grad_ref[...] = grad
    low = grad.astype(LOW)
    low_ref[...] = low
    for d in range(GROUPS):
        at = group_rows(place_ref, d)
        first = dot_t(low, full_ref[pl.ds(pl.multiple_of(at, 64), 128), :])
        second = dot_t(low, full_ref[pl.ds(pl.multiple_of(at + 64, 64), 128), :])
        both = jnp.concatenate([first, second], axis=1).astype(LOW)
        do_refs[d][...] = both.reshape(micro, rows, 256)


def branch(place, gain, resid, g, two_list, w_slots, micro):
    rows, width = resid.shape
    results = call(
        functools.partial(branch_kernel, len(w_slots), len(two_list)),
        "branch",
        place,
        [gain, resid, g, *two_list, *w_slots],
        [shaped(rows, width, dtype=WIDE), shaped(rows, width), shaped(1, width, dtype=WIDE)]
        + [shaped(micro, rows // micro, 256)] * GROUPS,
        [pltpu.VMEM((width, width), LOW)],
        flops=2 * rows * width * 1024,
    )
    return results[0], results[1], results[2], list(results[3:])


def with_rows(index, rows, count, action):
    if rows % 8 == 0:
        action(pl.ds(pl.multiple_of(index * rows, 8), rows))
        return
    for known in range(count):

        @pl.when(index == known)
        def _():
            action(slice(known * rows, known * rows + rows))


def write_chunks(place_ref, full_ref, keep_ref, send_ref):
    parts_f, halves, rows, _ = keep_ref.shape
    for i in range(parts_f):
        for k in range(halves):
            for odd, ref in ((0, keep_ref), (1, send_ref)):
                index = (place_ref[2] ^ i) * (2 * halves) + (place_ref[1] ^ (2 * k + odd))

                def copy(at):
                    ref[i, k] = full_ref[at, :].astype(ref.dtype)

                with_rows(index, rows, 2 * halves * parts_f, copy)


def out_grads_kernel(place_ref, low_ref, *refs):
    o_refs = refs[:GROUPS]
    keep_ref, send_ref, full_ref = refs[GROUPS:]
    micro, rows, _ = o_refs[0].shape
    low = low_ref[...]
    for d in range(GROUPS):
        both = t_dot(o_refs[d][...].reshape(micro * rows, 256), low)
        at = group_rows(place_ref, d)
        full_ref[pl.ds(pl.multiple_of(at, 64), 128), :] = both[:128]
        full_ref[pl.ds(pl.multiple_of(at + 128, 64), 64), :] = both[192:]
    write_chunks(place_ref, full_ref, keep_ref, send_ref)


def out_grads(place, low, o_slots, parts_f, fast):
    rows, width = low.shape
    chunk = (parts_f, fast // 2, width // (parts_f * fast), width)
    return call(
        out_grads_kernel,
        "out_grads",
        place,
        [low, *o_slots],
        [shaped(*chunk, dtype=WIDE), shaped(*chunk)],
        [pltpu.VMEM((width, width), WIDE)],
        flops=2 * rows * width * 1024,
    )


def input_grads_kernel(parts_f, count, place_ref, act_ref, dq_ref, *refs):
    x_refs, refs = refs[:GROUPS], refs[GROUPS:]
    dkv_refs, refs = refs[:count], refs[count:]
    w_refs, refs = refs[:parts_f], refs[parts_f:]
    one_keep, one_send, gain_out, keep_ref, send_ref, full_ref, sums_ref, both_ref, one_ref = refs
    place_rows(full_ref, w_refs, place_ref[2])
    groups, rows, width = act_ref.shape
    micro = dq_ref.shape[1]
    gain_total = jnp.zeros((1, width), WIDE)
    for d in range(GROUPS):
        dkv = sum((r[0, d] if len(r.shape) == 5 else r[d]).astype(WIDE) for r in dkv_refs)
        dkv = dkv.astype(LOW).reshape(rows, 384)
        both = jnp.concatenate([dq_ref[d].reshape(rows, 256), dkv], axis=1)
        both_ref[d] = both
        one = dot_t(both, full_ref[...])
        x = x_refs[d][...].reshape(rows, width).astype(WIDE)
        gain_total = gain_total + jnp.sum(one * (x * rms_scale(x)), axis=0, keepdims=True)
        one_ref[lax.rem(place_ref[0] + GROUPS - d, GROUPS)] = one
    for d in range(GROUPS):
        value = one_ref[place_ref[0] ^ d]
        if d % 2:
            one_send[d // 2] = value.astype(LOW)
        else:
            one_keep[d // 2] = value
    gain_out[...] = gain_total
    sums_ref[...] = t_dot(act_ref[...].reshape(groups * rows, width), both_ref[...].reshape(groups * rows, 640))
    write_chunks(place_ref, sums_ref, keep_ref, send_ref)


def input_grads(place, act, dq, x_slots, dkv_list, w_slots, fast):
    groups, rows, width = act.shape
    micro = dq.shape[1]
    parts_f = len(w_slots)
    chunk = (parts_f, fast // 2, width // (parts_f * fast), 640)
    return call(
        functools.partial(input_grads_kernel, parts_f, len(dkv_list)),
        "input_grads",
        place,
        [act, dq, *x_slots, *dkv_list, *w_slots],
        [shaped(GROUPS // 2, rows, width, dtype=WIDE), shaped(GROUPS // 2, rows, width)]
        + [shaped(1, width, dtype=WIDE), shaped(*chunk, dtype=WIDE), shaped(*chunk)],
        [
            pltpu.VMEM((width, 640), LOW),
            pltpu.VMEM((width, 640), WIDE),
            pltpu.VMEM((groups, rows, 640), LOW),
            pltpu.VMEM((groups, rows, width), WIDE),
        ],
        flops=4 * groups * rows * width * 640,
    )


def last_kernel(count, place_ref, gain_ref, x_ref, grad_ref, resid_ref, *refs):
    one_ref, got_ref, refs = refs[0], refs[1], refs[2:]
    out_refs, refs = refs[:count], refs[count:]
    x_grad_ref, out_ref = refs
    micro, rows, width = x_ref.shape
    grad_one = one_ref[...] + got_ref[...].astype(WIDE)
    x = x_ref[...].reshape(micro * rows, width).astype(WIDE)
    scale = rms_scale(x)
    normed = x * scale
    x_grad_ref[...] = grad_ref[...] + norm_back(grad_one * gain_ref[...], normed, scale)
    out_ref[...] = (resid_ref[...] + summed(out_refs)).astype(LOW)


def last(place, gain, x, grad, resid, one, one_got, out_list):
    rows, width = resid.shape
    return call(
        functools.partial(last_kernel, len(out_list)),
        "last",
        place,
        [gain, x, grad, resid, one, one_got, *out_list],
        [shaped(rows, width, dtype=WIDE), shaped(rows, width)],
    )


LOW_ORDER = (0, 2, 1, 3)


def feed_finish_kernel(parts_f, fast, place_ref, *refs):
    pair_refs, low_refs = refs[:fast], refs[fast : 2 * fast]
    gate_ref, up_ref, down_ref, pack_ref = refs[2 * fast :]
    _, rows, double = pair_refs[0].shape
    cols = double // 2
    piece = cols // parts_f
    for j in range(fast):
        other = place_ref[1] ^ j
        for d in range(GROUPS):
            at = pl.ds(pl.multiple_of(lax.rem(place_ref[0] + GROUPS - d, GROUPS) * rows, 8), rows)
            for start, ref in ((0, gate_ref), (cols, up_ref)):
                for k in range(parts_f):
                    value = pair_refs[j][d, :, start + k * piece : start + (k + 1) * piece].astype(WIDE)
                    if piece % 128 == 0:
                        to = pl.multiple_of(k * fast * piece + other * piece, 128)
                        ref[at, pl.ds(to, piece)] = value
                    else:
                        for l in range(fast):

                            @pl.when(other == l)
                            def _():
                                ref[at, (k * fast + l) * piece : (k * fast + l + 1) * piece] = value

            at = pl.ds(pl.multiple_of((place_ref[0] ^ LOW_ORDER[d]) * rows, 8), rows)
            pack_ref[at, :] = low_refs[j][d].astype(WIDE)
        for r, c, to_r, to_c, n, w in packing(piece, rows * GROUPS):
            at = pl.ds(pl.multiple_of(other * piece + r, 8), n)
            down_ref[at, c : c + w] = pack_ref[to_r : to_r + n, to_c : to_c + w]


def feed_finish(place, pair_packs, low_packs, parts_f):
    fast = len(pair_packs)
    _, rows, double = pair_packs[0].shape
    cols = double // 2
    piece = cols // parts_f
    return call(
        functools.partial(feed_finish_kernel, parts_f, fast),
        "feed_finish",
        place,
        [*pair_packs, *low_packs],
        [
            shaped(rows * GROUPS, cols * fast, dtype=WIDE),
            shaped(rows * GROUPS, cols * fast, dtype=WIDE),
            shaped(piece * fast, rows * GROUPS * parts_f, dtype=WIDE),
        ],
        [pltpu.VMEM((rows * GROUPS, cols), WIDE)],
    )


def input_finish_kernel(fast, place_ref, *refs):
    pack_refs, out_refs = refs[:fast], refs[fast : 2 * fast]
    query_ref, key_ref, value_ref, out_ref = refs[2 * fast :]
    rows = pack_refs[0].shape[0]
    for j in range(fast):
        value = out_refs[j][...].astype(WIDE)

        def place_out(at):
            out_ref[at, :] = value

        with_rows(place_ref[1] ^ j, rows, fast, place_out)
    for h in range(GROUPS):

        @pl.when(place_ref[0] == h)
        def _():
            for j in range(fast):
                starts = [(h - g) % GROUPS * 640 for g in range(GROUPS)]
                part = lambda a, b: pack_refs[j][:, a:b].astype(WIDE)
                query = jnp.concatenate([part(s, s + 192) for s in starts], axis=1)
                key = jnp.concatenate([part(s + 256, s + 448) for s in starts], axis=1)
                value = jnp.concatenate([p for s in starts for p in (part(s + 512, s + 640), part(s + 448, s + 512))], axis=1)

                def place_in(at):
                    query_ref[at, :] = query
                    key_ref[at, :] = key
                    value_ref[at, :] = value

                with_rows(place_ref[1] ^ j, rows, fast, place_in)


def input_finish(place, packs, out_all, width):
    fast = len(packs)
    return call(
        functools.partial(input_finish_kernel, fast),
        "input_finish",
        place,
        [*packs, *out_all],
        [shaped(packs[0].shape[0] * fast, width, dtype=WIDE)] * 4,
    )


def spread_groups(v):
    return [v] + [shift(v, d) for d in range(1, GROUPS)]


def gather_pack(pack, fast):
    slots = {0: pack}
    for bit in bits_down(fast):
        for j in list(slots):
            slots[j ^ bit] = hop(slots[j], "ctx", bit)
    return [slots[j] for j in range(fast)]


def after(value, *others):
    return lax.optimization_barrier((value, *others))[0]


def body(
    tokens,
    offsets,
    norm1_gain,
    norm2_gain,
    bias_table,
    w_query,
    w_key,
    w_value,
    w_out,
    w_gate,
    w_up,
    w_down,
    cotangent,
):
    micro, _, block_rows, width = tokens.shape
    blocks = lax.axis_size("ctx")
    parts_f = lax.axis_size("fsdp")
    fast = blocks // GROUPS
    ctx = lax.axis_index("ctx")
    f = lax.axis_index("fsdp")
    hi, lo = ctx // fast, ctx % fast
    group_cols = w_query.shape[1] // GROUPS
    own_rows = micro * block_rows
    hidden = w_gate.shape[1]
    piece = hidden // (parts_f * fast)
    part_rows = w_query.shape[0]
    gain_one = norm1_gain.reshape(1, width)
    gain_two = norm2_gain.reshape(1, width)
    place = jnp.stack([hi, lo, f]).astype(jnp.int32)

    own_x = tokens[:, 0]
    g_low = cotangent[:, 0].reshape(own_rows, width)
    x_slots = spread_groups(own_x)

    def group_of(matrix):
        return lax.dynamic_slice_in_dim(matrix, hi * group_cols, group_cols, axis=1)

    q_part, k_part, v_part = group_of(w_query), group_of(w_key), group_of(w_value)
    gap = jnp.zeros((part_rows, 64), LOW)
    qkv_part = jnp.concatenate([q_part, gap, k_part, v_part[:, 128:], v_part[:, :128]], axis=1)
    qkv_slots = slots_out(qkv_part, "fsdp", parts_f)

    def pieces(matrix):
        return [
            lax.dynamic_slice_in_dim(matrix, (k * fast + lo) * piece, piece, axis=1) for k in range(parts_f)
        ]

    pair_part = jnp.concatenate(pieces(w_gate) + pieces(w_up), axis=1)
    down_part = lax.dynamic_slice_in_dim(w_down, lo * piece, piece, axis=0)

    starts = offsets[:, 0]
    group_ids = (hi + GROUPS - jnp.arange(GROUPS, dtype=jnp.int32)) % GROUPS
    slot_ids = lo ^ jnp.arange(fast, dtype=jnp.int32)
    kplace = jnp.take(starts, group_ids[None, :] * fast + slot_ids[:, None], axis=1)
    table_group = lax.dynamic_slice_in_dim(bias_table, hi * 3, 3, axis=1)
    strip = make_strip(table_group, blocks)

    tick = [place]

    def fence(*values):
        tick[0], *values = lax.optimization_barrier((tick[0], *values))
        return values[0] if len(values) == 1 else values

    def shifted(parts, sign):
        return [shift(v, sign * d) for d, v in enumerate(parts, 1)]

    def to_f(parts):
        return [hop(v, "fsdp", j) for j, v in enumerate(parts, 1)]

    def groups_sum(own, parts):
        return (own + sum(v.astype(WIDE) for v in parts)).astype(LOW)

    def far_places(v):
        have = {0: v}
        for bit in bits_down(fast // 2):
            for j in list(have):
                have[j ^ (2 * bit)] = hop(have[j], "ctx", 2 * bit)
        return have

    def both_cores(have):
        return [v for j in range(0, fast, 2) for v in (have[j], hop(have[j], "ctx", 1))]

    strip, kplace = fence(strip, kplace)
    places = (kplace[:, 0], kplace)
    out_w, pair_w, x_slots, qkv_slots = fence(w_out, pair_part, x_slots, qkv_slots)
    act_one, q, kv = project(tick[0], gain_one, x_slots, qkv_slots)
    kv_slots = slots_out(kv, "ctx", fast)
    out_w_slots = slots_out(out_w, "fsdp", parts_f)
    pair_slots = slots_out(pair_w, "fsdp", parts_f)
    g_low, kv_slots = fence(g_low, kv_slots)
    g_have = {0: g_low, 1: hop(g_low, "ctx", 1)}
    for bit in bits_down(fast // 2):
        for j in [j for j in g_have if j % 2 == 0]:
            g_have[j ^ (2 * bit)] = hop(g_have[j], "ctx", 2 * bit)
    o_group, lse = attention_forward(places, strip, q, kv_slots, blocks)
    o_group, g_have, out_w_slots, down_w = fence(o_group, g_have, out_w_slots, down_part)
    o_slots = [o_group[0]] + shifted(o_group[1:], -1)
    down_slots = slots_out(down_w, "fsdp", parts_f)
    for j in range(2, fast, 2):
        g_have[j + 1] = hop(g_have[j], "ctx", 1)
    g_slots = [g_have[j] for j in range(fast)]
    resid, act_two = joined(tick[0], gain_two, own_x, o_slots, out_w_slots)
    act_two, g_slots = fence(act_two, g_slots)
    act_slots = slots_out(act_two, "ctx", fast)
    two_parts, out_parts, hid, grads = feed(tick[0], act_slots, g_slots, pair_slots, down_slots)
    two_parts, out_parts = fence(two_parts, out_parts)

    two_odd = two_parts[2]
    two_got = hop(two_odd, "ctx", 1)
    pair_keep, *pair_sends = pair_grads(tick[0], act_slots, grads, parts_f)
    two_got, pair_keep, pair_sends = fence(two_got, pair_keep, pair_sends)
    pair_got = to_f(pair_sends)
    two_list, sent = pairs_on(two_parts, two_got, fast)
    low_keep, *low_sends = down_grads(fence(tick[0], sent)[0], g_slots, hid, parts_f)
    got, low_keep, low_sends = fence([v for v, _ in two_list], low_keep, low_sends)
    two_list = [(v, first) for v, (_, first) in zip(got, two_list)]
    grad_resid, grad_low, gain_two_part, do_own = branch(
        tick[0], gain_two, resid, g_low, two_list, out_w_slots, micro
    )
    do_own = fence(*do_own)
    do_slots = [do_own[0]] + shifted(do_own[1:], 1)
    out_keep, out_send = out_grads(tick[0], grad_low, o_slots, parts_f, fast)
    out_send, pair_got = fence(out_send, pair_got)
    pair_own, pair_sends = group_split(tick[0], [pair_keep, *pair_got])
    pair_own, pair_sends, low_sends, do_slots = fence(pair_own, pair_sends, low_sends, do_slots)

    pair_parts = shifted(pair_sends, 1)
    low_got = to_f(low_sends)
    out_got = hop(out_send, "ctx", 1)
    dq, dkv_parts, table_part = attention_backward(
        places, tick[0], strip, q, kv_slots, do_slots, lse, blocks
    )
    dq, dkv_parts, pair_parts, low_got, out_got = fence(dq, dkv_parts, pair_parts, low_got, out_got)
    dkv_list, sent = pairs_on(dkv_parts, hop(dkv_parts[2], "ctx", 1), fast)
    pair_chunk, out_chunk, _ = fence(groups_sum(pair_own, pair_parts), out_keep + out_got.astype(WIDE), sent)
    pair_spread = spread_groups(pair_chunk)
    out_chunk = halve(out_chunk, "fsdp", 1)
    low_keep, low_send = group_halves(tick[0], [low_keep, *low_got])
    got, pair_spread, out_chunk, low_send = fence([v for v, _ in dkv_list], pair_spread, out_chunk, low_send)
    dkv_list = [(v, first) for v, (_, first) in zip(got, dkv_list)]

    low_got = hop(low_send, "ctx", fast)
    out_chunk = halve(out_chunk, "ctx", 2)
    one_keep, one_send, gain_one_part, in_keep, in_send = input_grads(
        tick[0], act_one, dq, x_slots, dkv_list, qkv_slots, fast
    )
    one_keep, one_send, in_keep, in_send, low_got, out_chunk = fence(
        one_keep, one_send, in_keep, in_send, low_got, out_chunk
    )
    in_got = hop(in_send, "ctx", 1)
    pair_have = far_places(jnp.stack(pair_spread))
    one_got = hop(one_send, "ctx", fast)
    in_total = fence(in_keep + in_got.astype(WIDE))
    low_sum = low_keep + low_got.astype(WIDE)
    low_got = hop(low_sum[1].astype(LOW), "ctx", 2 * fast)
    in_total, low_got = fence(halve(in_total, "fsdp", 1), low_got)
    low_two = (low_sum[0] + low_got.astype(WIDE)).astype(LOW)
    low_two = jnp.stack([low_two, hop(low_two, "ctx", 2 * fast)])
    in_chunk, pair_have, one_got, low_two = fence(
        halve(in_total, "ctx", 2).astype(LOW), pair_have, one_got, low_two
    )
    in_spread = spread_groups(in_chunk)
    low_got = hop(low_two, "ctx", fast)
    small = jnp.concatenate([gain_one_part.reshape(-1, 128), gain_two_part.reshape(-1, 128), table_part], axis=0)
    for bit in bits_up(parts_f):
        small = small + hop(small, "fsdp", bit)
    small = small + hop(small, "ctx", 1)
    in_pack, low_pack, small, one_sum, out_low, out_parts = fence(
        jnp.concatenate(in_spread, axis=1),
        jnp.concatenate([low_two, low_got]),
        small,
        one_keep + one_got.astype(WIDE),
        out_chunk.astype(LOW),
        out_parts,
    )
    in_have = far_places(in_pack)
    out_got = hop(out_low, "ctx", fast)
    small = small + hop(small, "ctx", fast)
    low_have = far_places(low_pack)
    out_low, small, one_send = fence(
        (out_low.astype(WIDE) + out_got.astype(WIDE)).astype(LOW), small, one_sum[1].astype(LOW)
    )
    out_got = hop(out_low, "ctx", 2 * fast)
    small = small + hop(small, "ctx", 2 * fast)
    one_got = hop(one_send, "ctx", 2 * fast)
    pair_packs = both_cores(pair_have)
    out_chunk, small, in_have, low_have, pair_packs = fence(
        (out_low.astype(WIDE) + out_got.astype(WIDE)).astype(LOW), small, in_have, low_have, pair_packs
    )
    low_packs = both_cores(low_have)
    in_packs = both_cores(in_have)
    out_have = far_places(out_chunk)
    for bit in bits_down(fast // 2):
        small = small + hop(small, "ctx", 2 * bit)
    w_gate_grad, w_up_grad, w_down_grad = feed_finish(tick[0], pair_packs, low_packs, parts_f)
    w_gate_grad, in_packs, out_have, small, one_got = fence(w_gate_grad, in_packs, out_have, small, one_got)
    out_all = both_cores(out_have)
    out_list, _ = pairs_back(*out_parts, fast)
    x_grad, result = last(tick[0], gain_one, own_x, grad_resid, resid, one_sum[0], one_got, out_list)
    x_grad, out_all = fence(x_grad, out_all)
    w_query_grad, w_key_grad, w_value_grad, w_out_grad = input_finish(tick[0], in_packs, out_all, width)
    head_count = bias_table.shape[1]

    lines = width // 128
    gain_rows = width // parts_f
    table_rows = bias_table.shape[0] // parts_f
    gain_one_grad = lax.dynamic_slice_in_dim(small[:lines].reshape(width), f * gain_rows, gain_rows)
    gain_two_grad = lax.dynamic_slice_in_dim(small[lines : 2 * lines].reshape(width), f * gain_rows, gain_rows)
    table_grad = lax.dynamic_slice(small, (2 * lines + f * table_rows, 0), (table_rows, head_count))

    return (
        result.reshape(micro, 1, block_rows, width),
        x_grad.reshape(micro, 1, block_rows, width),
        gain_one_grad,
        gain_two_grad,
        table_grad,
        w_query_grad,
        w_key_grad,
        w_value_grad,
        w_out_grad,
        w_gate_grad,
        w_up_grad,
        w_down_grad,
    )


def solution(mesh):
    in_specs = (
        P(None, "fsdp", "ctx", None),
        P(None, "fsdp", None),
        P(),
        P(),
        P(),
        P("fsdp", None),
        P("fsdp", None),
        P("fsdp", None),
        P("fsdp", None),
        P("fsdp", None),
        P("fsdp", None),
        P("fsdp", None),
        P(None, "fsdp", "ctx", None),
    )
    out_specs = (
        P(None, "fsdp", "ctx", None),
        P(None, "fsdp", "ctx", None),
        P("fsdp"),
        P("fsdp"),
        P("fsdp", None),
        P("fsdp", None),
        P("fsdp", None),
        P("fsdp", None),
        P("fsdp", None),
        P("fsdp", None),
        P("fsdp", None),
        P("fsdp", None),
    )
    return jax.shard_map(body, mesh=mesh, in_specs=in_specs, out_specs=out_specs, check_vma=False)
```

```python
import functools

import jax
import jax.numpy as jnp
from jax import lax
from jax.experimental import pallas as pl
from jax.experimental.pallas import tpu as pltpu
from jax.sharding import PartitionSpec as P

EPSILON = 1e-06
GROUPS = 4
WIDE = jnp.float32
LOW = jnp.bfloat16
FAR = 91
NEAR_LEAD = 96
VMEM_LIMIT = 60 * 1024 * 1024


def dot(a, b):
    return jnp.dot(a, b, preferred_element_type=WIDE)


def dot_t(a, b):
    return lax.dot_general(a, b, (((1,), (1,)), ((), ())), preferred_element_type=WIDE)


def t_dot(a, b):
    return lax.dot_general(a, b, (((0,), (0,)), ((), ())), preferred_element_type=WIDE)


def bucket_of(relative):
    distance = jnp.abs(relative)
    squared = distance * distance
    counted = jnp.zeros_like(relative)
    for exponent in range(1, 8):
        counted = counted + (squared >= 64 * 2**exponent).astype(jnp.int32)
    within = jnp.where(distance < 8, distance, 8 + counted)
    return jnp.where(relative > 0, 16, 0).astype(jnp.int32) + within


def hop(v, axis, bit):
    size = lax.axis_size(axis)
    return lax.ppermute(v, axis, [(i, i ^ bit) for i in range(size)])


def bits_down(size):
    bit = size // 2
    while bit >= 1:
        yield bit
        bit //= 2


def bits_up(size):
    return reversed(list(bits_down(size)))


def shift(v, steps):
    size = lax.axis_size("ctx")
    stride = size // GROUPS
    return lax.ppermute(v, "ctx", [(i, (i + steps * stride) % size) for i in range(size)])


def slots_out(v, axis, count):
    slots = {0: v}
    for bit in bits_down(count):
        for j in list(slots):
            slots[j ^ bit] = hop(slots[j], axis, bit)
    return [slots[j] for j in range(count)]


def pairs_on(parts, got, count):
    own, evens, _ = parts
    have = {k: evens[k - 1].astype(WIDE) + got[k].astype(WIDE) for k in range(1, count // 2)}
    mine, sent = [(own, False), (got, True)], []
    for bit in bits_up(count // 2):
        for k in sorted(have):
            if k & bit:
                sent.append(have[k].astype(LOW))
                part = hop(sent[-1], "ctx", 2 * bit)
                if k ^ bit:
                    have[k ^ bit] = have[k ^ bit] + part.astype(WIDE)
                else:
                    mine.append((part, False))
                del have[k]
    return mine, sent


def pairs_back(own, evens, odds, count):
    return pairs_on((own, evens, odds), hop(odds, "ctx", 1), count)


def halve(v, axis, unit):
    count = v.shape[0]
    for bit in bits_down(count):
        v = v[:bit] + hop(v[bit:].astype(LOW), axis, bit * unit).astype(WIDE)
    return v[0]


def strip_kernel(blocks, table_ref, strip_ref):
    centre = 64 * (blocks - 1)
    rows = 2 * 64 * blocks
    near = 256
    start = centre - NEAR_LEAD
    chunk = 128
    heads = table_ref.shape[1]

    def relative(first, count):
        u = lax.broadcasted_iota(jnp.int32, (count, 128), 0) + first
        i = lax.broadcasted_iota(jnp.int32, (count, 128), 1)
        return u - centre - jnp.where(i >= 64, i - 64, i)

    for h in range(heads):
        strip_ref[h, : start, :] = jnp.full((start, 128), table_ref[15, h], WIDE)
        strip_ref[h, start + near :, :] = jnp.full((rows - start - near, 128), table_ref[31, h], WIDE)
    for first in range(start, start + near, chunk):
        label = bucket_of(relative(first, chunk))
        for h in range(heads):
            value = jnp.zeros((chunk, 128), WIDE)
            for b in range(32):
                value = jnp.where(label == b, table_ref[b, h], value)
            strip_ref[h, first : first + chunk, :] = value


def make_strip(table_group, blocks):
    heads = table_group.shape[1]
    return pl.pallas_call(
        functools.partial(strip_kernel, blocks),
        out_shape=jax.ShapeDtypeStruct((heads, 2 * 64 * blocks, 128), WIDE),
        in_specs=[pl.BlockSpec(memory_space=pltpu.SMEM)],
        out_specs=pl.BlockSpec(memory_space=pltpu.VMEM),
        compiler_params=pltpu.CompilerParams(vmem_limit_bytes=VMEM_LIMIT),
        name="bias_strip",
    )(table_group)


def split_heads(wide, second_upper):
    lane = lax.broadcasted_iota(jnp.int32, (wide.shape[0], 128), 1)
    low = lane < 64
    zero = jnp.zeros((wide.shape[0], 128), wide.dtype)
    first, second = wide[:, :128], wide[:, 128:]
    third = jnp.where(low, zero, second) if second_upper else jnp.where(low, second, zero)
    return [jnp.where(low, first, zero), jnp.where(low, zero, first), third]


KEY_COLS = (0, 0, 128)
VALUE_COLS = (256, 256, 128)


def sort_blocks(count, m, kplace_ref, kv_refs, sorted_ref):
    for j in range(count):
        for e in range(GROUPS):
            to = pl.multiple_of(kplace_ref[m, j, e] * 64, 64)
            sorted_ref[pl.ds(to, 64), :] = kv_refs[j][e, 0]


def rows_sum(value):
    return jnp.sum(value.reshape(value.shape[0] // 8, 8, value.shape[1]), axis=0)


CHUNK = 128


def chunk_scores(strip_ref, sorted_ref, query, h, start, offs, low):
    scores = dot_t(sorted_ref[start : start + CHUNK, KEY_COLS[h] : KEY_COLS[h] + 128], query)
    parts = []
    for half in range(2):
        a = strip_ref[h, pl.ds(offs[2 * half] + start, CHUNK), :]
        b = strip_ref[h, pl.ds(offs[2 * half + 1] + start, CHUNK), :]
        parts.append(scores[:, half * 128 : half * 128 + 128] + jnp.where(low, a, b))
    return jnp.concatenate(parts, axis=1)


def forward_kernel(count, blocks, qplace_ref, kplace_ref, strip_ref, q_ref, *refs):
    kv_refs = refs[:count]
    o_refs = refs[count : count + GROUPS]
    lse_ref, sorted_ref, score_ref, weight_ref = refs[count + GROUPS :]
    m = pl.program_id(0)
    rows = 64 * blocks
    sort_blocks(count, m, kplace_ref, kv_refs, sorted_ref)
    offs = [pl.multiple_of((blocks - 1 - qplace_ref[m, e]) * 64, 64) for e in range(GROUPS)]
    queries = split_heads(q_ref[:, 0].reshape(GROUPS * 64, 256), False)
    low = lax.broadcasted_iota(jnp.int32, (CHUNK, 128), 1) < 64
    mixed = []
    for h in range(3):
        top = jnp.full((8, GROUPS * 64), -jnp.inf, WIDE)
        for start in range(0, rows, CHUNK):
            s = chunk_scores(strip_ref, sorted_ref, queries[h], h, start, offs, low)
            score_ref[start : start + CHUNK, :] = s
            top = jnp.maximum(top, jnp.max(s.reshape(CHUNK // 8, 8, GROUPS * 64), axis=0))
        top = jnp.max(top, axis=0, keepdims=True)
        total = jnp.zeros((8, GROUPS * 64), WIDE)
        for start in range(0, rows, CHUNK):
            e = jnp.exp(score_ref[start : start + CHUNK, :] - top)
            score_ref[start : start + CHUNK, :] = e
            total = total + rows_sum(e)
        total = jnp.sum(total, axis=0, keepdims=True)
        lse_ref[0, h : h + 1, :] = top + jnp.log(total)
        scale = 1.0 / total
        for start in range(0, rows, CHUNK):
            weight_ref[start : start + CHUNK, :] = (score_ref[start : start + CHUNK, :] * scale).astype(LOW)
        mixed.append(t_dot(sorted_ref[:, VALUE_COLS[h] : VALUE_COLS[h] + 128], weight_ref[...]))
    sub = lax.broadcasted_iota(jnp.int32, (128, GROUPS * 64), 0) < 64
    first = jnp.where(sub, mixed[0], mixed[1]).T
    second = jnp.where(sub, 0.0, mixed[2]).T
    out = jnp.concatenate([first, second], axis=1).astype(LOW)
    for d in range(GROUPS):
        o_refs[d][0] = out[d * 64 : d * 64 + 64]


def attention_forward(places, strip, q, kv_slots, blocks):
    qplace, kplace = places
    count = len(kv_slots)
    micro = q.shape[1]
    rows = 64 * blocks
    kv_cols = kv_slots[0].shape[-1]
    by_micro = lambda width: pl.BlockSpec((GROUPS, 1, 64, width), lambda m, *_: (0, m, 0, 0))
    results = pl.pallas_call(
        functools.partial(forward_kernel, count, blocks),
        out_shape=(jax.ShapeDtypeStruct((micro, 64, 256), LOW),) * GROUPS
        + (jax.ShapeDtypeStruct((micro, 3, GROUPS * 64), WIDE),),
        grid_spec=pltpu.PrefetchScalarGridSpec(
            num_scalar_prefetch=2,
            grid=(micro,),
            in_specs=[pl.BlockSpec(strip.shape, lambda m, *_: (0, 0, 0)), by_micro(256)] + [by_micro(kv_cols)] * count,
            out_specs=(pl.BlockSpec((1, 64, 256), lambda m, *_: (m, 0, 0)),) * GROUPS
            + (pl.BlockSpec((1, 3, GROUPS * 64), lambda m, *_: (m, 0, 0)),),
            scratch_shapes=[
                pltpu.VMEM((rows, kv_cols), LOW),
                pltpu.VMEM((rows, GROUPS * 64), WIDE),
                pltpu.VMEM((rows, GROUPS * 64), LOW),
            ],
        ),
        compiler_params=pltpu.CompilerParams(vmem_limit_bytes=VMEM_LIMIT),
        cost_estimate=pl.CostEstimate(
            flops=micro * 3 * 2 * 2 * rows * GROUPS * 64 * 128 * 2,
            bytes_accessed=micro * rows * kv_cols * 4,
            transcendentals=micro * 3 * rows * GROUPS * 64,
        ),
        name="attention_forward",
    )(qplace, kplace, strip, q, *kv_slots)
    return list(results[:GROUPS]), results[GROUPS]


def backward_kernel(count, blocks, qplace_ref, kplace_ref, place_ref, strip_ref, q_ref, lse_ref, *refs):
    do_refs, refs = refs[:GROUPS], refs[GROUPS:]
    kv_refs = refs[:count]
    dq_ref = refs[count]
    own_ref, even_ref, odd_ref, table_ref = refs[count + 1 : count + 5]
    sorted_ref, grad_ref, p_ref, dp_ref, soft_ref, ds_ref, wide_ref, near_ref, far_ref = refs[count + 5 :]
    m = pl.program_id(0)
    rows = 64 * blocks
    queue = GROUPS * 64
    near = near_ref.shape[1]
    lead = 128

    @pl.when(m == 0)
    def _():
        near_ref[...] = jnp.zeros_like(near_ref)
        far_ref[...] = jnp.zeros_like(far_ref)
        wide_ref[:lead, :] = jnp.zeros((lead, queue), WIDE)
        wide_ref[lead + rows :, :] = jnp.zeros((wide_ref.shape[0] - lead - rows, queue), WIDE)

    sort_blocks(count, m, kplace_ref, kv_refs, sorted_ref)
    offs = [pl.multiple_of((blocks - 1 - qplace_ref[m, e]) * 64, 64) for e in range(GROUPS)]
    queries = split_heads(q_ref[:, 0].reshape(queue, 256), False)
    grads = split_heads(jnp.concatenate([r[0] for r in do_refs], axis=0), True)
    low = lax.broadcasted_iota(jnp.int32, (CHUNK, 128), 1) < 64
    lane_block = lax.broadcasted_iota(jnp.int32, (8, queue), 1) // 64
    own_place = jnp.zeros((8, queue), jnp.int32)
    for e in range(GROUPS):
        own_place = jnp.where(lane_block == e, qplace_ref[m, e], own_place)
    near_low = lax.broadcasted_iota(jnp.int32, (near, 128), 1) < 64
    query_grads = []
    for h in range(3):
        delta = jnp.zeros((8, queue), WIDE)
        lse = lse_ref[0, h : h + 1, :]
        for start in range(0, rows, CHUNK):
            at = slice(start, start + CHUNK)
            p = jnp.exp(chunk_scores(strip_ref, sorted_ref, queries[h], h, start, offs, low) - lse)
            dp = dot_t(sorted_ref[at, VALUE_COLS[h] : VALUE_COLS[h] + 128], grads[h])
            p_ref[at, :] = p
            dp_ref[at, :] = dp
            soft_ref[h, at, :] = p.astype(LOW)
            delta = delta + rows_sum(p * dp)
        delta = jnp.sum(delta, axis=0, keepdims=True)
        before = jnp.zeros((8, queue), WIDE)
        after = jnp.zeros((8, queue), WIDE)
        for start in range(0, rows, CHUNK):
            at = slice(start, start + CHUNK)
            ds = (p_ref[at, :] * (dp_ref[at, :] - delta)).astype(LOW)
            ds_ref[h, at, :] = ds
            wide = ds.astype(WIDE)
            wide_ref[lead + start : lead + start + CHUNK, :] = wide
            for k in range(CHUNK // 64):
                block = start // 64 + k
                part = rows_sum(wide[k * 64 : k * 64 + 64])
                before = before + jnp.where(own_place >= block + 3, part, 0.0)
                after = after + jnp.where(own_place <= block - 3, part, 0.0)
        far_ref[h, 0] += before
        far_ref[h, 1] += after
        for half in range(2):
            cols = slice(half * 128, half * 128 + 128)
            a = wide_ref[pl.ds(pl.multiple_of(qplace_ref[m, 2 * half] * 64, 64), near), cols]
            b = wide_ref[pl.ds(pl.multiple_of(qplace_ref[m, 2 * half + 1] * 64, 64), near), cols]
            near_ref[h] += jnp.where(near_low, a, b)
        query_grads.append(t_dot(sorted_ref[:, KEY_COLS[h] : KEY_COLS[h] + 128], ds_ref[h]))
    sub = lax.broadcasted_iota(jnp.int32, (128, queue), 0) < 64
    first = jnp.where(sub, query_grads[0], query_grads[1]).T
    second = jnp.where(sub, query_grads[2], 0.0).T
    dq_ref[:, 0] = jnp.concatenate([first, second], axis=1).astype(LOW).reshape(GROUPS, 64, 256)
    grad_ref[:, 0:128] = dot(ds_ref[0], queries[0]) + dot(ds_ref[1], queries[1])
    grad_ref[:, 128:256] = dot(ds_ref[2], queries[2]) + dot(soft_ref[2], grads[2])
    grad_ref[:, 256:384] = dot(soft_ref[0], grads[0]) + dot(soft_ref[1], grads[1])
    for j in range(count):
        for e in range(GROUPS):
            at = pl.multiple_of(kplace_ref[m, j, e] * 64, 64)
            value = grad_ref[pl.ds(at, 64), :]
            if j == 0:
                own_ref[e, 0] = value
            elif j % 2:
                odd_ref[j // 2, e, 0] = value.astype(LOW)
            else:
                even_ref[j // 2 - 1, e, 0] = value.astype(LOW)

    @pl.when(m == pl.num_programs(0) - 1)
    def _():
        sums_row = lax.broadcasted_iota(jnp.int32, (32, 128), 0)
        lanes = lax.broadcasted_iota(jnp.int32, (32, 128), 1)
        side = lax.broadcasted_iota(jnp.int32, (near, 128), 1)
        rel = lax.broadcasted_iota(jnp.int32, (near, 128), 0) - lead - jnp.where(side >= 64, side - 64, side)
        label = bucket_of(rel)
        table = jnp.zeros((32, 128), WIDE)
        for h in range(3):
            far = [jnp.sum(far_ref[h, k][:, :128] + far_ref[h, k][:, 128:], axis=0, keepdims=True) for k in range(2)]
            result = jnp.where(sums_row == 15, far[0], jnp.where(sums_row == 31, far[1], 0.0))
            window = near_ref[h]
            for b in range(32):
                part = jnp.sum(jnp.where(label == b, window, 0.0), axis=0, keepdims=True)
                result = result + jnp.where(sums_row == b, part, 0.0)
            total = jnp.sum(result, axis=1, keepdims=True)
            table = jnp.where(lanes == place_ref[0] * 3 + h, total, table)
        table_ref[...] = table


def attention_backward(places, place, strip, q, kv_slots, do_slots, lse, blocks):
    qplace, kplace = places
    count = len(kv_slots)
    micro = q.shape[1]
    rows = 64 * blocks
    kv_cols = kv_slots[0].shape[-1]
    by_micro = lambda width: pl.BlockSpec((GROUPS, 1, 64, width), lambda m, *_: (0, m, 0, 0))
    kv_shape = kv_slots[0].shape
    by_part = lambda n: pl.BlockSpec((n, GROUPS, 1, 64, kv_cols), lambda m, *_: (0, 0, m, 0, 0))
    results = pl.pallas_call(
        functools.partial(backward_kernel, count, blocks),
        out_shape=(jax.ShapeDtypeStruct(q.shape, LOW),)
        + (
            jax.ShapeDtypeStruct(kv_shape, WIDE),
            jax.ShapeDtypeStruct((count // 2 - 1,) + kv_shape, LOW),
            jax.ShapeDtypeStruct((count // 2,) + kv_shape, LOW),
        )
        + (jax.ShapeDtypeStruct((32, 128), WIDE),),
        grid_spec=pltpu.PrefetchScalarGridSpec(
            num_scalar_prefetch=3,
            grid=(micro,),
            in_specs=[
                pl.BlockSpec(strip.shape, lambda m, *_: (0, 0, 0)),
                by_micro(256),
                pl.BlockSpec((1, 3, GROUPS * 64), lambda m, *_: (m, 0, 0)),
            ]
            + [pl.BlockSpec((1, 64, 256), lambda m, *_: (m, 0, 0))] * GROUPS
            + [by_micro(kv_cols)] * count,
            out_specs=(by_micro(256),)
            + (by_micro(kv_cols), by_part(count // 2 - 1), by_part(count // 2))
            + (pl.BlockSpec((32, 128), lambda m, *_: (0, 0)),),
            scratch_shapes=[
                pltpu.VMEM((rows, kv_cols), LOW),
                pltpu.VMEM((rows, kv_cols), WIDE),
                pltpu.VMEM((rows, GROUPS * 64), WIDE),
                pltpu.VMEM((rows, GROUPS * 64), WIDE),
                pltpu.VMEM((3, rows, GROUPS * 64), LOW),
                pltpu.VMEM((3, rows, GROUPS * 64), LOW),
                pltpu.VMEM((rows + 256, GROUPS * 64), WIDE),
                pltpu.VMEM((3, 320, 128), WIDE),
                pltpu.VMEM((3, 2, 8, GROUPS * 64), WIDE),
            ],
        ),
        compiler_params=pltpu.CompilerParams(vmem_limit_bytes=VMEM_LIMIT),
        cost_estimate=pl.CostEstimate(
            flops=micro * 3 * 5 * 2 * rows * GROUPS * 64 * 128 * 2,
            bytes_accessed=micro * rows * kv_cols * 8,
            transcendentals=micro * 3 * rows * GROUPS * 64,
        ),
        name="attention_backward",
    )(qplace, kplace, place, strip, q, lse, *do_slots, *kv_slots)
    return results[0], results[1:4], results[4]


PLACE = pl.BlockSpec(memory_space=pltpu.SMEM)


def whole(count):
    return [pl.BlockSpec(memory_space=pltpu.VMEM)] * count


def first_entry(v):
    return pl.BlockSpec((1,) + v.shape[1:], lambda _: (0,) * v.ndim)


def call(kernel, name, place, operands, out_shape, scratch=(), flops=0):
    operands = [v if isinstance(v, tuple) else (v, False) for v in operands]
    grid = {"grid": (1,)} if any(first for _, first in operands) else {}
    specs = [PLACE] + [first_entry(v) if first else whole(1)[0] for v, first in operands]
    operands = [v for v, _ in operands]
    size = sum(v.size * v.dtype.itemsize for v in operands) + sum(
        v.size * jnp.dtype(v.dtype).itemsize for v in out_shape
    )
    return pl.pallas_call(
        kernel,
        out_shape=tuple(out_shape),
        **grid,
        in_specs=specs,
        out_specs=tuple(whole(len(out_shape))),
        scratch_shapes=list(scratch),
        compiler_params=pltpu.CompilerParams(vmem_limit_bytes=VMEM_LIMIT),
        cost_estimate=pl.CostEstimate(flops=flops, bytes_accessed=size, transcendentals=0),
        name=name,
    )(place, *operands)


def shaped(*shape, dtype=LOW):
    return jax.ShapeDtypeStruct(shape, dtype)


def place_rows(full_ref, slot_refs, index):
    rows = slot_refs[0].shape[0]
    for j, ref in enumerate(slot_refs):
        full_ref[pl.ds(pl.multiple_of((index ^ j) * rows, rows), rows), :] = ref[...]


def rms_scale(values):
    return lax.rsqrt(jnp.mean(values * values, axis=-1, keepdims=True) + EPSILON)


def norm_back(grad_normed, normed, scale):
    return scale * (grad_normed - normed * jnp.mean(grad_normed * normed, axis=-1, keepdims=True))


def project_kernel(parts_f, place_ref, gain_ref, *refs):
    x_refs, w_refs = refs[:GROUPS], refs[GROUPS : GROUPS + parts_f]
    act_ref, q_ref, kv_ref, full_ref = refs[GROUPS + parts_f :]
    place_rows(full_ref, w_refs, place_ref[2])
    micro, rows, width = x_refs[0].shape
    for d in range(GROUPS):
        x = x_refs[d][...].reshape(micro * rows, width).astype(WIDE)
        act_ref[d] = (x * rms_scale(x) * gain_ref[...]).astype(LOW)
    both = dot(act_ref[...].reshape(GROUPS * micro * rows, width), full_ref[...]).astype(LOW)
    q_ref[...] = both[:, :256].reshape(GROUPS, micro, rows, 256)
    kv_ref[...] = both[:, 256:].reshape(GROUPS, micro, rows, 384)


def project(place, gain, x_slots, w_slots):
    micro, rows, width = x_slots[0].shape
    return call(
        functools.partial(project_kernel, len(w_slots)),
        "project",
        place,
        [gain, *x_slots, *w_slots],
        [
            shaped(GROUPS, micro * rows, width),
            shaped(GROUPS, micro, rows, 256),
            shaped(GROUPS, micro, rows, 384),
        ],
        [pltpu.VMEM((width, 640), LOW)],
        flops=2 * GROUPS * micro * rows * width * 640,
    )


def group_rows(place_ref, d):
    return lax.rem(place_ref[0] + d, GROUPS) * 192


def arrange_kernel(parts_f, place_ref, *refs):
    w_refs, (out_ref, full_ref) = refs[:parts_f], refs[parts_f:]
    place_rows(full_ref, w_refs, place_ref[2])
    for d in range(GROUPS):
        at = group_rows(place_ref, d)
        out_ref[d * 256 : d * 256 + 128, :] = full_ref[pl.ds(pl.multiple_of(at, 64), 128), :]
        out_ref[d * 256 + 128 : d * 256 + 256, :] = full_ref[pl.ds(pl.multiple_of(at + 64, 64), 128), :]


def arrange(place, w_slots):
    width = w_slots[0].shape[1]
    return call(
        functools.partial(arrange_kernel, len(w_slots)),
        "arrange",
        place,
        w_slots,
        [shaped(GROUPS * 256, width)],
        [pltpu.VMEM((width, width), LOW)],
    )[0]


def joined_kernel(place_ref, gain_ref, x_ref, w_ref, *refs):
    o_refs, (resid_ref, act_ref) = refs[:GROUPS], refs[GROUPS:]
    micro, rows, width = x_ref.shape
    o = jnp.concatenate([r[...].reshape(micro * rows, 256) for r in o_refs], axis=1)
    total = x_ref[...].reshape(micro * rows, width).astype(WIDE) + dot(o, w_ref[...])
    resid_ref[...] = total
    act_ref[...] = (total * rms_scale(total) * gain_ref[...]).astype(LOW)


def joined(place, gain, x, o_slots, w_rel):
    micro, rows, width = x.shape
    return call(
        joined_kernel,
        "joined",
        place,
        [gain, x, w_rel, *o_slots],
        [shaped(micro * rows, width, dtype=WIDE), shaped(micro * rows, width)],
        flops=2 * micro * rows * width * 1024,
    )


GELU_A = 0.7978845608028654
GELU_B = 0.044715


def put_part(refs, j, value):
    own_ref, even_ref, odd_ref = refs
    if j == 0:
        own_ref[...] = value
    elif j % 2:
        odd_ref[j // 2] = value.astype(odd_ref.dtype)
    else:
        even_ref[j // 2 - 1] = value.astype(even_ref.dtype)


def part_shapes(shape, fast):
    return [
        shaped(*shape, dtype=WIDE),
        shaped(fast // 2 - 1, *shape),
        shaped(fast // 2, *shape),
    ]


def feed_kernel(parts_f, fast, place_ref, *refs):
    act_refs, refs = refs[:fast], refs[fast:]
    g_refs, refs = refs[:fast], refs[fast:]
    pair_refs, refs = refs[:parts_f], refs[parts_f:]
    down_refs, refs = refs[:parts_f], refs[parts_f:]
    two_refs, out_refs, refs = refs[:3], refs[3:6], refs[6:]
    hid_ref, grad_ref, pair_ref, down_ref = refs
    place_rows(pair_ref, pair_refs, place_ref[2])
    place_rows(down_ref, down_refs, place_ref[2])
    cols = hid_ref.shape[-1]
    rows = act_refs[0].shape[0]
    act = jnp.concatenate([r[...] for r in act_refs], axis=0)
    g = jnp.concatenate([r[...] for r in g_refs], axis=0)
    both = dot(act, pair_ref[...])
    dh = dot_t(g, down_ref[...])
    for j in range(fast):
        at = slice(j * rows, j * rows + rows)
        z, up = both[at, :cols], both[at, cols:]
        square = z * z
        t = jnp.tanh(GELU_A * (z + GELU_B * square * z))
        half = 0.5 * (1.0 + t)
        gelu = z * half
        slope = half + (0.5 * z) * (1.0 - t * t) * (GELU_A * (1.0 + 3.0 * GELU_B * square))
        hid_ref[j] = (gelu * up).astype(LOW)
        grad_ref[j, :, :cols] = (dh[at] * up * slope).astype(LOW)
        grad_ref[j, :, cols:] = (dh[at] * gelu).astype(LOW)
    two = dot_t(grad_ref[...].reshape(fast * rows, 2 * cols), pair_ref[...])
    out = dot(hid_ref[...].reshape(fast * rows, cols), down_ref[...])
    for j in range(fast):
        put_part(two_refs, j, two[j * rows : j * rows + rows])
        put_part(out_refs, j, out[j * rows : j * rows + rows])


def feed(place, act_slots, g_slots, pair_slots, down_slots):
    fast, parts_f = len(act_slots), len(pair_slots)
    rows, width = act_slots[0].shape
    cols = down_slots[0].shape[0] * parts_f
    results = call(
        functools.partial(feed_kernel, parts_f, fast),
        "feed",
        place,
        [*act_slots, *g_slots, *pair_slots, *down_slots],
        part_shapes((rows, width), fast) * 2 + [shaped(fast, rows, cols), shaped(fast, rows, 2 * cols)],
        [pltpu.VMEM((width, 2 * cols), LOW), pltpu.VMEM((cols, width), LOW)],
        flops=2 * fast * rows * width * cols * 6,
    )
    return results[:3], results[3:6], results[-2], results[-1]


def packing(piece, rows):
    if rows == 3 * piece:
        return [(0, k * 256, k * piece, 0, piece, 256) for k in range(3)]
    half = piece // 2
    return [
        (0, 0, 0, 0, piece, 512),
        (0, 512, piece, 0, half, 256),
        (half, 512, piece, 256, half, 256),
    ]


def pair_grads_kernel(fast, place_ref, *refs):
    act_refs, grad_ref, refs = refs[:fast], refs[fast], refs[fast + 1 :]
    outs, full_ref = refs[:-1], refs[-1]
    act = jnp.concatenate([r[...] for r in act_refs], axis=0)
    full_ref[...] = t_dot(act, grad_ref[...].reshape(act.shape[0], -1))
    rows = outs[0].shape[0]
    for j, out in enumerate(outs):
        at = pl.multiple_of((place_ref[2] ^ j) * rows, rows)
        out[...] = full_ref[pl.ds(at, rows), :].astype(out.dtype)


def pair_grads(place, act_slots, grads, parts_f):
    fast, rows, double = grads.shape
    width = act_slots[0].shape[1]
    types = [WIDE] + [LOW] * (parts_f - 1)
    return call(
        functools.partial(pair_grads_kernel, fast),
        "pair_grads",
        place,
        [*act_slots, grads],
        [shaped(width // parts_f, double, dtype=t) for t in types],
        [pltpu.VMEM((width, double), WIDE)],
        flops=2 * fast * rows * width * double,
    )


def down_grads_kernel(fast, place_ref, *refs):
    g_refs, hid_ref, refs = refs[:fast], refs[fast], refs[fast + 1 :]
    outs, full_ref = refs[:-1], refs[-1]
    g = jnp.concatenate([r[...] for r in g_refs], axis=0)
    full_ref[...] = t_dot(hid_ref[...].reshape(g.shape[0], -1), g)
    rows = outs[0].shape[0]
    piece = full_ref.shape[0] // len(outs)
    for j, out in enumerate(outs):
        for r, c, to_r, to_c, n, w in packing(piece, rows):
            at = pl.multiple_of((place_ref[2] ^ j) * piece + r, 8)
            out[to_r : to_r + n, to_c : to_c + w] = full_ref[pl.ds(at, n), c : c + w].astype(out.dtype)


def down_grads(place, g_slots, hid, parts_f):
    fast, rows, cols = hid.shape
    width = g_slots[0].shape[1]
    types = [WIDE] + [LOW] * (parts_f - 1)
    return call(
        functools.partial(down_grads_kernel, fast),
        "down_grads",
        place,
        [*g_slots, hid],
        [shaped(width // parts_f, cols, dtype=t) for t in types],
        [pltpu.VMEM((cols, width), WIDE)],
        flops=2 * fast * rows * width * cols,
    )


def group_split_kernel(count, place_ref, *refs):
    own_ref, send_refs = refs[count], refs[count + 1 :]
    rows = own_ref.shape[0]

    def part(d):
        at = pl.ds(pl.multiple_of(lax.rem(place_ref[0] + d, GROUPS) * rows, 8), rows)
        return sum(r[at, :].astype(WIDE) for r in refs[:count])

    own_ref[...] = part(0)
    for d, ref in enumerate(send_refs, 1):
        ref[...] = part(d).astype(ref.dtype)


def group_split(place, parts):
    rows, cols = parts[0].shape
    cut = rows // GROUPS
    results = call(
        functools.partial(group_split_kernel, len(parts)),
        "group_split",
        place,
        parts,
        [shaped(cut, cols, dtype=WIDE)] + [shaped(cut, cols)] * (GROUPS - 1),
    )
    return results[0], list(results[1:])


def group_halves_kernel(count, place_ref, *refs):
    keep_ref, send_ref = refs[count:]
    rows = keep_ref.shape[1]
    for d in range(GROUPS):
        at = pl.ds(pl.multiple_of((place_ref[0] ^ d) * rows, 8), rows)
        total = sum(r[at, :].astype(WIDE) for r in refs[:count])
        if d % 2:
            send_ref[d // 2] = total.astype(send_ref.dtype)
        else:
            keep_ref[d // 2] = total


def group_halves(place, parts):
    rows, cols = parts[0].shape
    cut = (GROUPS // 2, rows // GROUPS, cols)
    return call(
        functools.partial(group_halves_kernel, len(parts)),
        "group_halves",
        place,
        parts,
        [shaped(*cut, dtype=WIDE), shaped(*cut)],
    )


def summed(refs):
    return sum((r[0] if len(r.shape) == 3 else r[...]).astype(WIDE) for r in refs)


def branch_kernel(count, place_ref, gain_ref, resid_ref, g_ref, w_ref, *refs):
    two_refs, refs = refs[:count], refs[count:]
    grad_ref, low_ref, gain_out = refs[:3]
    do_refs = refs[3:]
    micro, rows, _ = do_refs[0].shape
    grad_two = summed(two_refs)
    resid = resid_ref[...]
    scale = rms_scale(resid)
    normed = resid * scale
    gain_out[...] = jnp.sum(grad_two * normed, axis=0, keepdims=True)
    grad = g_ref[...].astype(WIDE) + norm_back(grad_two * gain_ref[...], normed, scale)
    grad_ref[...] = grad
    low = grad.astype(LOW)
    low_ref[...] = low
    both = dot_t(low, w_ref[...]).astype(LOW)
    for d in range(GROUPS):
        do_refs[d][...] = both[:, d * 256 : d * 256 + 256].reshape(micro, rows, 256)


def branch(place, gain, resid, g, two_list, w_rel, micro):
    rows, width = resid.shape
    results = call(
        functools.partial(branch_kernel, len(two_list)),
        "branch",
        place,
        [gain, resid, g, w_rel, *two_list],
        [shaped(rows, width, dtype=WIDE), shaped(rows, width), shaped(1, width, dtype=WIDE)]
        + [shaped(micro, rows // micro, 256)] * GROUPS,
        flops=2 * rows * width * 1024,
    )
    return results[0], results[1], results[2], list(results[3:])


def with_rows(index, rows, count, action):
    if rows % 8 == 0:
        action(pl.ds(pl.multiple_of(index * rows, 8), rows))
        return
    for known in range(count):

        @pl.when(index == known)
        def _():
            action(slice(known * rows, known * rows + rows))


def write_chunks(place_ref, full_ref, keep_ref, send_ref):
    parts_f, halves, rows, _ = keep_ref.shape
    for i in range(parts_f):
        for k in range(halves):
            for odd, ref in ((0, keep_ref), (1, send_ref)):
                index = (place_ref[2] ^ i) * (2 * halves) + (place_ref[1] ^ (2 * k + odd))

                def copy(at):
                    ref[i, k] = full_ref[at, :].astype(ref.dtype)

                with_rows(index, rows, 2 * halves * parts_f, copy)


def out_grads_kernel(place_ref, low_ref, *refs):
    o_refs = refs[:GROUPS]
    keep_ref, send_ref, full_ref = refs[GROUPS:]
    micro, rows, _ = o_refs[0].shape
    low = low_ref[...]
    for d in range(GROUPS):
        both = t_dot(o_refs[d][...].reshape(micro * rows, 256), low)
        at = group_rows(place_ref, d)
        full_ref[pl.ds(pl.multiple_of(at, 64), 128), :] = both[:128]
        full_ref[pl.ds(pl.multiple_of(at + 128, 64), 64), :] = both[192:]
    write_chunks(place_ref, full_ref, keep_ref, send_ref)


def out_grads(place, low, o_slots, parts_f, fast):
    rows, width = low.shape
    chunk = (parts_f, fast // 2, width // (parts_f * fast), width)
    return call(
        out_grads_kernel,
        "out_grads",
        place,
        [low, *o_slots],
        [shaped(*chunk, dtype=WIDE), shaped(*chunk)],
        [pltpu.VMEM((width, width), WIDE)],
        flops=2 * rows * width * 1024,
    )


def input_grads_kernel(parts_f, count, place_ref, act_ref, dq_ref, *refs):
    x_refs, refs = refs[:GROUPS], refs[GROUPS:]
    dkv_refs, refs = refs[:count], refs[count:]
    w_refs, refs = refs[:parts_f], refs[parts_f:]
    one_keep, one_send, gain_out, keep_ref, send_ref, full_ref, sums_ref, both_ref, one_ref = refs
    place_rows(full_ref, w_refs, place_ref[2])
    groups, rows, width = act_ref.shape
    micro = dq_ref.shape[1]
    gain_total = jnp.zeros((1, width), WIDE)
    for d in range(GROUPS):
        dkv = sum((r[0, d] if len(r.shape) == 5 else r[d]).astype(WIDE) for r in dkv_refs)
        dkv = dkv.astype(LOW).reshape(rows, 384)
        both = jnp.concatenate([dq_ref[d].reshape(rows, 256), dkv], axis=1)
        both_ref[d] = both
        one = dot_t(both, full_ref[...])
        x = x_refs[d][...].reshape(rows, width).astype(WIDE)
        gain_total = gain_total + jnp.sum(one * (x * rms_scale(x)), axis=0, keepdims=True)
        one_ref[lax.rem(place_ref[0] + GROUPS - d, GROUPS)] = one
    for d in range(GROUPS):
        value = one_ref[place_ref[0] ^ d]
        if d % 2:
            one_send[d // 2] = value.astype(LOW)
        else:
            one_keep[d // 2] = value
    gain_out[...] = gain_total
    sums_ref[...] = t_dot(act_ref[...].reshape(groups * rows, width), both_ref[...].reshape(groups * rows, 640))
    write_chunks(place_ref, sums_ref, keep_ref, send_ref)


def input_grads(place, act, dq, x_slots, dkv_list, w_slots, fast):
    groups, rows, width = act.shape
    micro = dq.shape[1]
    parts_f = len(w_slots)
    chunk = (parts_f, fast // 2, width // (parts_f * fast), 640)
    return call(
        functools.partial(input_grads_kernel, parts_f, len(dkv_list)),
        "input_grads",
        place,
        [act, dq, *x_slots, *dkv_list, *w_slots],
        [shaped(GROUPS // 2, rows, width, dtype=WIDE), shaped(GROUPS // 2, rows, width)]
        + [shaped(1, width, dtype=WIDE), shaped(*chunk, dtype=WIDE), shaped(*chunk)],
        [
            pltpu.VMEM((width, 640), LOW),
            pltpu.VMEM((width, 640), WIDE),
            pltpu.VMEM((groups, rows, 640), LOW),
            pltpu.VMEM((groups, rows, width), WIDE),
        ],
        flops=4 * groups * rows * width * 640,
    )


def last_kernel(count, place_ref, gain_ref, x_ref, grad_ref, resid_ref, *refs):
    one_ref, got_ref, refs = refs[0], refs[1], refs[2:]
    out_refs, refs = refs[:count], refs[count:]
    x_grad_ref, out_ref = refs
    micro, rows, width = x_ref.shape
    grad_one = one_ref[...] + got_ref[: micro * rows, :].astype(WIDE)
    x = x_ref[...].reshape(micro * rows, width).astype(WIDE)
    scale = rms_scale(x)
    normed = x * scale
    x_grad_ref[...] = grad_ref[...] + norm_back(grad_one * gain_ref[...], normed, scale)
    parts = [(r[0] if len(r.shape) == 3 else r[r.shape[0] - micro * rows :, :]).astype(WIDE) for r in out_refs]
    out_ref[...] = (resid_ref[...] + sum(parts)).astype(LOW)


def last(place, gain, x, grad, resid, one, one_got, out_list):
    rows, width = resid.shape
    return call(
        functools.partial(last_kernel, len(out_list)),
        "last",
        place,
        [gain, x, grad, resid, one, one_got, *out_list],
        [shaped(rows, width, dtype=WIDE), shaped(rows, width)],
    )


def pair_finish_kernel(parts_f, fast, place_ref, *refs):
    pair_refs, (gate_ref, up_ref) = refs[:fast], refs[fast:]
    _, rows, double = pair_refs[0].shape
    cols = double // 2
    piece = cols // parts_f
    for j in range(fast):
        other = place_ref[1] ^ j
        for d in range(GROUPS):
            at = pl.ds(pl.multiple_of(lax.rem(place_ref[0] + GROUPS - d, GROUPS) * rows, 8), rows)
            for start, ref in ((0, gate_ref), (cols, up_ref)):
                for k in range(parts_f):
                    value = pair_refs[j][d, :, start + k * piece : start + (k + 1) * piece].astype(WIDE)
                    if piece % 128 == 0:
                        to = pl.multiple_of(k * fast * piece + other * piece, 128)
                        ref[at, pl.ds(to, piece)] = value
                    else:
                        for l in range(fast):

                            @pl.when(other == l)
                            def _():
                                ref[at, (k * fast + l) * piece : (k * fast + l + 1) * piece] = value


def low_finish_kernel(parts_f, fast, place_ref, *refs):
    low_refs, (down_ref, pack_ref) = refs[:fast], refs[fast:]
    _, rows, cols = low_refs[0].shape
    piece = cols // parts_f
    for j in range(fast):
        for d in range(GROUPS):
            at = pl.ds(pl.multiple_of(lax.rem(place_ref[0] + GROUPS - d, GROUPS) * rows, 8), rows)
            pack_ref[at, :] = low_refs[j][d].astype(WIDE)
        for r, c, to_r, to_c, n, w in packing(piece, rows * GROUPS):
            at = pl.ds(pl.multiple_of((place_ref[1] ^ j) * piece + r, 8), n)
            down_ref[at, c : c + w] = pack_ref[to_r : to_r + n, to_c : to_c + w]


def low_finish(place, packs, parts_f):
    fast = len(packs)
    _, rows, cols = packs[0].shape
    return call(
        functools.partial(low_finish_kernel, parts_f, fast),
        "low_finish",
        place,
        packs,
        [shaped(cols // parts_f * fast, rows * GROUPS * parts_f, dtype=WIDE)],
        [pltpu.VMEM((rows * GROUPS, cols), WIDE)],
    )[0]


def input_finish_kernel(fast, place_ref, *refs):
    pack_refs = refs[:fast]
    query_ref, key_ref, value_ref, out_ref = refs[fast:]
    rows = pack_refs[0].shape[0]
    for j in range(fast):
        value = pack_refs[j][:, GROUPS * 640 :].astype(WIDE)

        def place_out(at):
            out_ref[at, :] = value

        with_rows(place_ref[1] ^ j, rows, fast, place_out)
    for h in range(GROUPS):

        @pl.when(place_ref[0] == h)
        def _():
            for j in range(fast):
                starts = [(h - g) % GROUPS * 640 for g in range(GROUPS)]
                part = lambda a, b: pack_refs[j][:, a:b].astype(WIDE)
                query = jnp.concatenate([part(s, s + 192) for s in starts], axis=1)
                key = jnp.concatenate([part(s + 256, s + 448) for s in starts], axis=1)
                value = jnp.concatenate([p for s in starts for p in (part(s + 512, s + 640), part(s + 448, s + 512))], axis=1)

                def place_in(at):
                    query_ref[at, :] = query
                    key_ref[at, :] = key
                    value_ref[at, :] = value

                with_rows(place_ref[1] ^ j, rows, fast, place_in)


def most_finish_kernel(parts_f, fast, place_ref, *refs):
    pair_refs, pack_refs, refs = refs[:fast], refs[fast : 2 * fast], refs[2 * fast :]
    pair_finish_kernel(parts_f, fast, place_ref, *pair_refs, *refs[:2])
    input_finish_kernel(fast, place_ref, *pack_refs, *refs[2:])


def most_finish(place, pair_packs, packs, parts_f, width):
    fast = len(packs)
    _, rows, double = pair_packs[0].shape
    return call(
        functools.partial(most_finish_kernel, parts_f, fast),
        "most_finish",
        place,
        [*pair_packs, *packs],
        [shaped(rows * GROUPS, double // 2 * fast, dtype=WIDE)] * 2
        + [shaped(packs[0].shape[0] * fast, width, dtype=WIDE)] * 4,
    )


def spread_groups(v):
    return [v] + [shift(v, d) for d in range(1, GROUPS)]


def gather_pack(pack, fast):
    slots = {0: pack}
    for bit in bits_down(fast):
        for j in list(slots):
            slots[j ^ bit] = hop(slots[j], "ctx", bit)
    return [slots[j] for j in range(fast)]


def after(value, *others):
    return lax.optimization_barrier((value, *others))[0]


def body(
    tokens,
    offsets,
    norm1_gain,
    norm2_gain,
    bias_table,
    w_query,
    w_key,
    w_value,
    w_out,
    w_gate,
    w_up,
    w_down,
    cotangent,
):
    micro, _, block_rows, width = tokens.shape
    blocks = lax.axis_size("ctx")
    parts_f = lax.axis_size("fsdp")
    fast = blocks // GROUPS
    ctx = lax.axis_index("ctx")
    f = lax.axis_index("fsdp")
    hi, lo = ctx // fast, ctx % fast
    group_cols = w_query.shape[1] // GROUPS
    own_rows = micro * block_rows
    hidden = w_gate.shape[1]
    piece = hidden // (parts_f * fast)
    part_rows = w_query.shape[0]
    gain_one = norm1_gain.reshape(1, width)
    gain_two = norm2_gain.reshape(1, width)
    place = jnp.stack([hi, lo, f]).astype(jnp.int32)

    own_x = tokens[:, 0]
    g_low = cotangent[:, 0].reshape(own_rows, width)
    x_slots = spread_groups(own_x)

    def group_of(matrix):
        return lax.dynamic_slice_in_dim(matrix, hi * group_cols, group_cols, axis=1)

    q_part, k_part, v_part = group_of(w_query), group_of(w_key), group_of(w_value)
    gap = jnp.zeros((part_rows, 64), LOW)
    qkv_part = jnp.concatenate([q_part, gap, k_part, v_part[:, 128:], v_part[:, :128]], axis=1)
    qkv_slots = slots_out(qkv_part, "fsdp", parts_f)

    def pieces(matrix):
        return [
            lax.dynamic_slice_in_dim(matrix, (k * fast + lo) * piece, piece, axis=1) for k in range(parts_f)
        ]

    pair_part = jnp.concatenate(pieces(w_gate) + pieces(w_up), axis=1)
    down_part = lax.dynamic_slice_in_dim(w_down, lo * piece, piece, axis=0)

    starts = offsets[:, 0]
    group_ids = (hi + GROUPS - jnp.arange(GROUPS, dtype=jnp.int32)) % GROUPS
    slot_ids = lo ^ jnp.arange(fast, dtype=jnp.int32)
    kplace = jnp.take(starts, group_ids[None, :] * fast + slot_ids[:, None], axis=1)
    table_group = lax.dynamic_slice_in_dim(bias_table, hi * 3, 3, axis=1)
    strip = make_strip(table_group, blocks)

    tick = [place]

    def fence(*values):
        tick[0], *values = lax.optimization_barrier((tick[0], *values))
        return values[0] if len(values) == 1 else values

    def shifted(parts, sign):
        return [shift(v, sign * d) for d, v in enumerate(parts, 1)]

    def to_f(parts):
        return [hop(v, "fsdp", j) for j, v in enumerate(parts, 1)]

    def groups_sum(own, parts):
        return (own + sum(v.astype(WIDE) for v in parts)).astype(LOW)

    def far_places(v):
        have = {0: v}
        for bit in bits_down(fast // 2):
            for j in list(have):
                have[j ^ (2 * bit)] = hop(have[j], "ctx", 2 * bit)
        return have

    def both_cores(have):
        return [v for j in range(0, fast, 2) for v in (have[j], hop(have[j], "ctx", 1))]

    strip, kplace = fence(strip, kplace)
    places = (kplace[:, 0], kplace)
    out_w, pair_w, x_slots, qkv_slots = fence(w_out, pair_part, x_slots, qkv_slots)
    act_one, q, kv = project(tick[0], gain_one, x_slots, qkv_slots)
    kv_slots = slots_out(kv, "ctx", fast)
    out_w_slots = slots_out(out_w, "fsdp", parts_f)
    pair_slots = slots_out(pair_w, "fsdp", parts_f)
    g_low, kv_slots = fence(g_low, kv_slots)
    g_have = {0: g_low, 1: hop(g_low, "ctx", 1)}
    for bit in bits_down(fast // 2):
        for j in [j for j in g_have if j % 2 == 0]:
            g_have[j ^ (2 * bit)] = hop(g_have[j], "ctx", 2 * bit)
    o_group, lse = attention_forward(places, strip, q, kv_slots, blocks)
    o_group, g_have, out_w_slots, down_w = fence(o_group, g_have, out_w_slots, down_part)
    o_slots = [o_group[0]] + shifted(o_group[1:], -1)
    down_slots = slots_out(down_w, "fsdp", parts_f)
    for j in range(2, fast, 2):
        g_have[j + 1] = hop(g_have[j], "ctx", 1)
    g_slots = [g_have[j] for j in range(fast)]
    w_rel = arrange(tick[0], out_w_slots)
    o_slots, w_rel = fence(o_slots, w_rel)
    resid, act_two = joined(tick[0], gain_two, own_x, o_slots, w_rel)
    act_two, g_slots = fence(act_two, g_slots)
    act_slots = slots_out(act_two, "ctx", fast)
    two_parts, out_parts, hid, grads = feed(tick[0], act_slots, g_slots, pair_slots, down_slots)
    two_parts, out_parts = fence(two_parts, out_parts)

    two_odd = two_parts[2]
    two_got = hop(two_odd, "ctx", 1)
    pair_keep, *pair_sends = pair_grads(tick[0], act_slots, grads, parts_f)
    out_got_one = hop(out_parts[2], "ctx", 1)
    two_got, pair_keep, pair_sends, out_got_one = fence(two_got, pair_keep, pair_sends, out_got_one)
    pair_got = to_f(pair_sends)
    two_list, sent = pairs_on(two_parts, two_got, fast)
    low_keep, *low_sends = down_grads(fence(tick[0], sent)[0], g_slots, hid, parts_f)
    got, low_keep, low_sends = fence([v for v, _ in two_list], low_keep, low_sends)
    two_list = [(v, first) for v, (_, first) in zip(got, two_list)]
    grad_resid, grad_low, gain_two_part, do_own = branch(
        tick[0], gain_two, resid, g_low, two_list, w_rel, micro
    )
    do_own = fence(*do_own)
    do_slots = [do_own[0]] + shifted(do_own[1:], 1)
    out_keep, out_send = out_grads(tick[0], grad_low, o_slots, parts_f, fast)
    out_keep, out_send, do_slots, pair_got = fence(out_keep, out_send, do_slots, pair_got)
    out_got = hop(out_send, "ctx", 1)
    pair_own, pair_sends = group_split(tick[0], [pair_keep, *pair_got])
    pair_own, pair_sends, low_sends, out_total = fence(
        pair_own, pair_sends, low_sends, out_keep + out_got.astype(WIDE)
    )

    pair_parts = shifted(pair_sends, 1)
    low_got = to_f(low_sends)
    out_total = halve(out_total, "fsdp", 1)
    dq, dkv_parts, table_part = attention_backward(
        places, tick[0], strip, q, kv_slots, do_slots, lse, blocks
    )
    dq, dkv_parts, pair_parts, low_got, out_total = fence(dq, dkv_parts, pair_parts, low_got, out_total)
    dkv_list, sent = pairs_on(dkv_parts, hop(dkv_parts[2], "ctx", 1), fast)
    low_keep, low_send = group_halves(tick[0], [low_keep, *low_got])
    pair_chunk, low_send, out_total, _ = fence(groups_sum(pair_own, pair_parts), low_send, out_total, sent)
    pair_spread = spread_groups(pair_chunk)
    if fast == 4:
        out_far = (out_parts[1][0].astype(WIDE) + out_got_one[1].astype(WIDE)).astype(LOW)
        far = jnp.concatenate([out_total[1].astype(LOW), out_far])
        far = hop(far, "ctx", 2)
    got = fence([v for v, _ in dkv_list])
    dkv_list = [(v, first) for v, (_, first) in zip(got, dkv_list)]
    one_keep, one_send, gain_one_part, in_keep, in_send = input_grads(
        tick[0], act_one, dq, x_slots, dkv_list, qkv_slots, fast
    )
    one_keep, one_send, in_keep, in_send, low_send, pair_spread = fence(
        one_keep, one_send, in_keep, in_send, low_send, pair_spread
    )
    if fast == 4:
        far = fence(far)
        chunk = out_total.shape[1]
        out_low = (out_total[0] + far[:chunk].astype(WIDE)).astype(LOW)
        out_list = [(out_parts[0], False), (out_got_one, True), (far, False)]
    else:
        out_low = halve(out_total, "ctx", 2).astype(LOW)
        out_list, _ = pairs_on(out_parts, out_got_one, fast)

    def send_small(v, small, bit):
        high = small.astype(LOW)
        rest = (small - high.astype(WIDE)).astype(LOW)
        return hop(jnp.concatenate([v, high, rest]), "ctx", bit), high.astype(WIDE) + rest.astype(WIDE)

    def take_small(got, own):
        lines = own.shape[0]
        count = got.shape[0] - 2 * lines
        return got[:count], own + got[count : count + lines].astype(WIDE) + got[count + lines :].astype(WIDE)

    def two_hops(a, b, bit):
        if a.shape[:-1] != b.shape[:-1]:
            return hop(a, "ctx", bit), hop(b, "ctx", bit)
        got = hop(jnp.concatenate([a, b], axis=-1), "ctx", bit)
        return got[..., : a.shape[-1]], got[..., a.shape[-1] :]

    head_count = bias_table.shape[1]
    table_row = table_part[:, :head_count].reshape(1, -1)
    table_row = jnp.pad(table_row, ((0, 5), (0, width - table_row.shape[1])))
    small = jnp.concatenate([gain_one_part, gain_two_part, table_row])
    in_got = hop(in_send, "ctx", 1)
    out_two = jnp.stack([out_low[:, : width // 2], out_low[:, width // 2 :]])
    low_got, out_got = two_hops(low_send, out_two, fast)
    small = small + hop(small, "ctx", 1)
    in_total, pair_send, small = fence(in_keep + in_got.astype(WIDE), jnp.stack(pair_spread), small)
    in_total = halve(jnp.swapaxes(in_total, 0, 1), "ctx", 2)
    for bit in bits_down(fast // 2):
        small = small + hop(small, "ctx", 2 * bit)
    in_total, low_got, out_got, small = fence(in_total, low_got, out_got, small)
    low_sum = low_keep + low_got.astype(WIDE)
    out_two = (out_two.astype(WIDE) + out_got.astype(WIDE)).astype(LOW)
    out_low = jnp.concatenate([out_two[0], out_two[1]], axis=1)
    low_got, out_got = two_hops(low_sum[1].astype(LOW), out_low, 2 * fast)
    pair_have = far_places(pair_send)
    for bit in bits_up(parts_f):
        small = small + hop(small, "fsdp", bit)
    in_chunk, small = fence(halve(in_total, "fsdp", 1).astype(LOW), small)
    in_spread = spread_groups(in_chunk)
    in_spread, low_got, out_got, pair_have = fence(in_spread, low_got, out_got, pair_have)
    low_spread = spread_groups((low_sum[0] + low_got.astype(WIDE)).astype(LOW))
    out_low = (out_low.astype(WIDE) + out_got.astype(WIDE)).astype(LOW)
    in_pack, one_send = fence(jnp.concatenate([*in_spread, out_low], axis=1), one_send)
    in_have = far_places(in_pack)
    one_got, small = send_small(one_send.reshape(-1, width), small, fast)
    low_spread, one_got, pair_have, in_have = fence(low_spread, one_got, pair_have, in_have)
    one_got, small = take_small(one_got, small)
    one_got = one_got.reshape(one_keep.shape)
    one_sum = one_keep[0] + one_got[0].astype(WIDE)
    one_got, small = send_small((one_keep[1] + one_got[1].astype(WIDE)).astype(LOW), small, 2 * fast)
    low_have = far_places(jnp.stack(low_spread))
    pair_packs = both_cores(pair_have)
    in_packs, pair_packs = fence(both_cores(in_have), pair_packs)
    w_gate_grad, w_up_grad, w_query_grad, w_key_grad, w_value_grad, w_out_grad = most_finish(
        tick[0], pair_packs, in_packs, parts_f, width
    )
    w_query_grad, one_got, low_have = fence(w_query_grad, one_got, low_have)
    low_packs = both_cores(low_have)
    x_grad, result = last(tick[0], gain_one, own_x, grad_resid, resid, one_sum, one_got, out_list)
    x_grad, low_packs = fence(x_grad, low_packs)
    w_down_grad = low_finish(tick[0], low_packs, parts_f)
    small = take_small(one_got, small)[1]

    gain_rows = width // parts_f
    table_rows = bias_table.shape[0] // parts_f
    gain_one_grad = lax.dynamic_slice_in_dim(small[0], f * gain_rows, gain_rows)
    gain_two_grad = lax.dynamic_slice_in_dim(small[1], f * gain_rows, gain_rows)
    table_grad = small[2, : bias_table.size].reshape(bias_table.shape)
    table_grad = lax.dynamic_slice_in_dim(table_grad, f * table_rows, table_rows)

    return (
        result.reshape(micro, 1, block_rows, width),
        x_grad.reshape(micro, 1, block_rows, width),
        gain_one_grad,
        gain_two_grad,
        table_grad,
        w_query_grad,
        w_key_grad,
        w_value_grad,
        w_out_grad,
        w_gate_grad,
        w_up_grad,
        w_down_grad,
    )


def solution(mesh):
    in_specs = (
        P(None, "fsdp", "ctx", None),
        P(None, "fsdp", None),
        P(),
        P(),
        P(),
        P("fsdp", None),
        P("fsdp", None),
        P("fsdp", None),
        P("fsdp", None),
        P("fsdp", None),
        P("fsdp", None),
        P("fsdp", None),
        P(None, "fsdp", "ctx", None),
    )
    out_specs = (
        P(None, "fsdp", "ctx", None),
        P(None, "fsdp", "ctx", None),
        P("fsdp"),
        P("fsdp"),
        P("fsdp", None),
        P("fsdp", None),
        P("fsdp", None),
        P("fsdp", None),
        P("fsdp", None),
        P("fsdp", None),
        P("fsdp", None),
        P("fsdp", None),
    )
    return jax.shard_map(body, mesh=mesh, in_specs=in_specs, out_specs=out_specs, check_vma=False)
```

```python
import functools

import jax
import jax.numpy as jnp
from jax import lax
from jax.experimental import pallas as pl
from jax.experimental.pallas import tpu as pltpu
from jax.sharding import PartitionSpec as P

EPSILON = 1e-06
GROUPS = 4
WIDE = jnp.float32
LOW = jnp.bfloat16
FAR = 91
NEAR_LEAD = 96
VMEM_LIMIT = 60 * 1024 * 1024


def dot(a, b):
    return jnp.dot(a, b, preferred_element_type=WIDE)


def dot_t(a, b):
    return lax.dot_general(a, b, (((1,), (1,)), ((), ())), preferred_element_type=WIDE)


def t_dot(a, b):
    return lax.dot_general(a, b, (((0,), (0,)), ((), ())), preferred_element_type=WIDE)


def bucket_of(relative):
    distance = jnp.abs(relative)
    squared = distance * distance
    counted = jnp.zeros_like(relative)
    for exponent in range(1, 8):
        counted = counted + (squared >= 64 * 2**exponent).astype(jnp.int32)
    within = jnp.where(distance < 8, distance, 8 + counted)
    return jnp.where(relative > 0, 16, 0).astype(jnp.int32) + within


def hop(v, axis, bit):
    size = lax.axis_size(axis)
    return lax.ppermute(v, axis, [(i, i ^ bit) for i in range(size)])


def bits_down(size):
    bit = size // 2
    while bit >= 1:
        yield bit
        bit //= 2


def bits_up(size):
    return reversed(list(bits_down(size)))


def shift(v, steps):
    size = lax.axis_size("ctx")
    stride = size // GROUPS
    return lax.ppermute(v, "ctx", [(i, (i + steps * stride) % size) for i in range(size)])


def slots_out(v, axis, count):
    slots = {0: v}
    for bit in bits_down(count):
        for j in list(slots):
            slots[j ^ bit] = hop(slots[j], axis, bit)
    return [slots[j] for j in range(count)]


def pairs_on(parts, got, count):
    own, evens, _ = parts
    have = {k: evens[k - 1].astype(WIDE) + got[k].astype(WIDE) for k in range(1, count // 2)}
    mine, sent = [(own, False), (got, True)], []
    for bit in bits_up(count // 2):
        for k in sorted(have):
            if k & bit:
                sent.append(have[k].astype(LOW))
                part = hop(sent[-1], "ctx", 2 * bit)
                if k ^ bit:
                    have[k ^ bit] = have[k ^ bit] + part.astype(WIDE)
                else:
                    mine.append((part, False))
                del have[k]
    return mine, sent


def pairs_back(own, evens, odds, count):
    return pairs_on((own, evens, odds), hop(odds, "ctx", 1), count)


def halve(v, axis, unit):
    count = v.shape[0]
    for bit in bits_down(count):
        v = v[:bit] + hop(v[bit:].astype(LOW), axis, bit * unit).astype(WIDE)
    return v[0]


def strip_kernel(blocks, table_ref, strip_ref):
    centre = 64 * (blocks - 1)
    rows = 2 * 64 * blocks
    near = 256
    start = centre - NEAR_LEAD
    chunk = 128
    heads = table_ref.shape[1]

    def relative(first, count):
        u = lax.broadcasted_iota(jnp.int32, (count, 128), 0) + first
        i = lax.broadcasted_iota(jnp.int32, (count, 128), 1)
        return u - centre - jnp.where(i >= 64, i - 64, i)

    for h in range(heads):
        strip_ref[h, : start, :] = jnp.full((start, 128), table_ref[15, h], WIDE)
        strip_ref[h, start + near :, :] = jnp.full((rows - start - near, 128), table_ref[31, h], WIDE)
    for first in range(start, start + near, chunk):
        label = bucket_of(relative(first, chunk))
        for h in range(heads):
            value = jnp.zeros((chunk, 128), WIDE)
            for b in range(32):
                value = jnp.where(label == b, table_ref[b, h], value)
            strip_ref[h, first : first + chunk, :] = value


def make_strip(table_group, blocks):
    heads = table_group.shape[1]
    return pl.pallas_call(
        functools.partial(strip_kernel, blocks),
        out_shape=jax.ShapeDtypeStruct((heads, 2 * 64 * blocks, 128), WIDE),
        in_specs=[pl.BlockSpec(memory_space=pltpu.SMEM)],
        out_specs=pl.BlockSpec(memory_space=pltpu.VMEM),
        compiler_params=pltpu.CompilerParams(vmem_limit_bytes=VMEM_LIMIT),
        name="bias_strip",
    )(table_group)


def split_heads(wide, second_upper):
    lane = lax.broadcasted_iota(jnp.int32, (wide.shape[0], 128), 1)
    low = lane < 64
    zero = jnp.zeros((wide.shape[0], 128), wide.dtype)
    first, second = wide[:, :128], wide[:, 128:]
    third = jnp.where(low, zero, second) if second_upper else jnp.where(low, second, zero)
    return [jnp.where(low, first, zero), jnp.where(low, zero, first), third]


KEY_COLS = (0, 0, 128)
VALUE_COLS = (256, 256, 128)


def sort_blocks(count, m, kplace_ref, kv_refs, sorted_ref):
    for j in range(count):
        for e in range(GROUPS):
            to = pl.multiple_of(kplace_ref[m, j, e] * 64, 64)
            sorted_ref[pl.ds(to, 64), :] = kv_refs[j][e, 0]


def rows_sum(value):
    return jnp.sum(value.reshape(value.shape[0] // 8, 8, value.shape[1]), axis=0)


CHUNK = 128


def chunk_scores(strip_ref, sorted_ref, query, h, start, offs, low):
    scores = dot_t(sorted_ref[start : start + CHUNK, KEY_COLS[h] : KEY_COLS[h] + 128], query)
    parts = []
    for half in range(2):
        a = strip_ref[h, pl.ds(offs[2 * half] + start, CHUNK), :]
        b = strip_ref[h, pl.ds(offs[2 * half + 1] + start, CHUNK), :]
        parts.append(scores[:, half * 128 : half * 128 + 128] + jnp.where(low, a, b))
    return jnp.concatenate(parts, axis=1)


def forward_kernel(count, blocks, qplace_ref, kplace_ref, strip_ref, q_ref, *refs):
    kv_refs = refs[:count]
    o_refs = refs[count : count + GROUPS]
    lse_ref, sorted_ref, score_ref, weight_ref = refs[count + GROUPS :]
    m = pl.program_id(0)
    rows = 64 * blocks
    sort_blocks(count, m, kplace_ref, kv_refs, sorted_ref)
    offs = [pl.multiple_of((blocks - 1 - qplace_ref[m, e]) * 64, 64) for e in range(GROUPS)]
    queries = split_heads(q_ref[:, 0].reshape(GROUPS * 64, 256), False)
    low = lax.broadcasted_iota(jnp.int32, (CHUNK, 128), 1) < 64
    mixed = []
    for h in range(3):
        top = jnp.full((8, GROUPS * 64), -jnp.inf, WIDE)
        for start in range(0, rows, CHUNK):
            s = chunk_scores(strip_ref, sorted_ref, queries[h], h, start, offs, low)
            score_ref[start : start + CHUNK, :] = s
            top = jnp.maximum(top, jnp.max(s.reshape(CHUNK // 8, 8, GROUPS * 64), axis=0))
        top = jnp.max(top, axis=0, keepdims=True)
        total = jnp.zeros((8, GROUPS * 64), WIDE)
        for start in range(0, rows, CHUNK):
            e = jnp.exp(score_ref[start : start + CHUNK, :] - top)
            score_ref[start : start + CHUNK, :] = e
            total = total + rows_sum(e)
        total = jnp.sum(total, axis=0, keepdims=True)
        lse_ref[0, h : h + 1, :] = top + jnp.log(total)
        scale = 1.0 / total
        for start in range(0, rows, CHUNK):
            weight_ref[start : start + CHUNK, :] = (score_ref[start : start + CHUNK, :] * scale).astype(LOW)
        mixed.append(t_dot(sorted_ref[:, VALUE_COLS[h] : VALUE_COLS[h] + 128], weight_ref[...]))
    sub = lax.broadcasted_iota(jnp.int32, (128, GROUPS * 64), 0) < 64
    first = jnp.where(sub, mixed[0], mixed[1]).T
    second = jnp.where(sub, 0.0, mixed[2]).T
    out = jnp.concatenate([first, second], axis=1).astype(LOW)
    for d in range(GROUPS):
        o_refs[d][0] = out[d * 64 : d * 64 + 64]


def attention_forward(places, strip, q, kv_slots, blocks):
    qplace, kplace = places
    count = len(kv_slots)
    micro = q.shape[1]
    rows = 64 * blocks
    kv_cols = kv_slots[0].shape[-1]
    by_micro = lambda width: pl.BlockSpec((GROUPS, 1, 64, width), lambda m, *_: (0, m, 0, 0))
    results = pl.pallas_call(
        functools.partial(forward_kernel, count, blocks),
        out_shape=(jax.ShapeDtypeStruct((micro, 64, 256), LOW),) * GROUPS
        + (jax.ShapeDtypeStruct((micro, 3, GROUPS * 64), WIDE),),
        grid_spec=pltpu.PrefetchScalarGridSpec(
            num_scalar_prefetch=2,
            grid=(micro,),
            in_specs=[pl.BlockSpec(strip.shape, lambda m, *_: (0, 0, 0)), by_micro(256)] + [by_micro(kv_cols)] * count,
            out_specs=(pl.BlockSpec((1, 64, 256), lambda m, *_: (m, 0, 0)),) * GROUPS
            + (pl.BlockSpec((1, 3, GROUPS * 64), lambda m, *_: (m, 0, 0)),),
            scratch_shapes=[
                pltpu.VMEM((rows, kv_cols), LOW),
                pltpu.VMEM((rows, GROUPS * 64), WIDE),
                pltpu.VMEM((rows, GROUPS * 64), LOW),
            ],
        ),
        compiler_params=pltpu.CompilerParams(vmem_limit_bytes=VMEM_LIMIT),
        cost_estimate=pl.CostEstimate(
            flops=micro * 3 * 2 * 2 * rows * GROUPS * 64 * 128 * 2,
            bytes_accessed=micro * rows * kv_cols * 4,
            transcendentals=micro * 3 * rows * GROUPS * 64,
        ),
        name="attention_forward",
    )(qplace, kplace, strip, q, *kv_slots)
    return list(results[:GROUPS]), results[GROUPS]


def backward_kernel(count, blocks, qplace_ref, kplace_ref, place_ref, strip_ref, q_ref, lse_ref, *refs):
    do_refs, refs = refs[:GROUPS], refs[GROUPS:]
    kv_refs = refs[:count]
    dq_ref = refs[count]
    own_ref, even_ref, odd_ref, table_ref = refs[count + 1 : count + 5]
    sorted_ref, grad_ref, p_ref, dp_ref, soft_ref, ds_ref, wide_ref, near_ref, far_ref = refs[count + 5 :]
    m = pl.program_id(0)
    rows = 64 * blocks
    queue = GROUPS * 64
    near = near_ref.shape[1]
    lead = 128

    @pl.when(m == 0)
    def _():
        near_ref[...] = jnp.zeros_like(near_ref)
        far_ref[...] = jnp.zeros_like(far_ref)
        wide_ref[:lead, :] = jnp.zeros((lead, queue), WIDE)
        wide_ref[lead + rows :, :] = jnp.zeros((wide_ref.shape[0] - lead - rows, queue), WIDE)

    sort_blocks(count, m, kplace_ref, kv_refs, sorted_ref)
    offs = [pl.multiple_of((blocks - 1 - qplace_ref[m, e]) * 64, 64) for e in range(GROUPS)]
    queries = split_heads(q_ref[:, 0].reshape(queue, 256), False)
    grads = split_heads(jnp.concatenate([r[0] for r in do_refs], axis=0), True)
    low = lax.broadcasted_iota(jnp.int32, (CHUNK, 128), 1) < 64
    lane_block = lax.broadcasted_iota(jnp.int32, (8, queue), 1) // 64
    own_place = jnp.zeros((8, queue), jnp.int32)
    for e in range(GROUPS):
        own_place = jnp.where(lane_block == e, qplace_ref[m, e], own_place)
    near_low = lax.broadcasted_iota(jnp.int32, (near, 128), 1) < 64
    query_grads = []
    for h in range(3):
        delta = jnp.zeros((8, queue), WIDE)
        lse = lse_ref[0, h : h + 1, :]
        for start in range(0, rows, CHUNK):
            at = slice(start, start + CHUNK)
            p = jnp.exp(chunk_scores(strip_ref, sorted_ref, queries[h], h, start, offs, low) - lse)
            dp = dot_t(sorted_ref[at, VALUE_COLS[h] : VALUE_COLS[h] + 128], grads[h])
            p_ref[at, :] = p
            dp_ref[at, :] = dp
            soft_ref[h, at, :] = p.astype(LOW)
            delta = delta + rows_sum(p * dp)
        delta = jnp.sum(delta, axis=0, keepdims=True)
        before = jnp.zeros((8, queue), WIDE)
        after = jnp.zeros((8, queue), WIDE)
        for start in range(0, rows, CHUNK):
            at = slice(start, start + CHUNK)
            ds = (p_ref[at, :] * (dp_ref[at, :] - delta)).astype(LOW)
            ds_ref[h, at, :] = ds
            wide = ds.astype(WIDE)
            wide_ref[lead + start : lead + start + CHUNK, :] = wide
            for k in range(CHUNK // 64):
                block = start // 64 + k
                part = rows_sum(wide[k * 64 : k * 64 + 64])
                before = before + jnp.where(own_place >= block + 3, part, 0.0)
                after = after + jnp.where(own_place <= block - 3, part, 0.0)
        far_ref[h, 0] += before
        far_ref[h, 1] += after
        for half in range(2):
            cols = slice(half * 128, half * 128 + 128)
            a = wide_ref[pl.ds(pl.multiple_of(qplace_ref[m, 2 * half] * 64, 64), near), cols]
            b = wide_ref[pl.ds(pl.multiple_of(qplace_ref[m, 2 * half + 1] * 64, 64), near), cols]
            near_ref[h] += jnp.where(near_low, a, b)
        query_grads.append(t_dot(sorted_ref[:, KEY_COLS[h] : KEY_COLS[h] + 128], ds_ref[h]))
    sub = lax.broadcasted_iota(jnp.int32, (128, queue), 0) < 64
    first = jnp.where(sub, query_grads[0], query_grads[1]).T
    second = jnp.where(sub, query_grads[2], 0.0).T
    dq_ref[:, 0] = jnp.concatenate([first, second], axis=1).astype(LOW).reshape(GROUPS, 64, 256)
    grad_ref[:, 0:128] = dot(ds_ref[0], queries[0]) + dot(ds_ref[1], queries[1])
    grad_ref[:, 128:256] = dot(ds_ref[2], queries[2]) + dot(soft_ref[2], grads[2])
    grad_ref[:, 256:384] = dot(soft_ref[0], grads[0]) + dot(soft_ref[1], grads[1])
    for j in range(count):
        for e in range(GROUPS):
            at = pl.multiple_of(kplace_ref[m, j, e] * 64, 64)
            value = grad_ref[pl.ds(at, 64), :]
            if j == 0:
                own_ref[e, 0] = value
            elif j % 2:
                odd_ref[j // 2, e, 0] = value.astype(LOW)
            else:
                even_ref[j // 2 - 1, e, 0] = value.astype(LOW)

    @pl.when(m == pl.num_programs(0) - 1)
    def _():
        sums_row = lax.broadcasted_iota(jnp.int32, (32, 128), 0)
        lanes = lax.broadcasted_iota(jnp.int32, (32, 128), 1)
        side = lax.broadcasted_iota(jnp.int32, (near, 128), 1)
        rel = lax.broadcasted_iota(jnp.int32, (near, 128), 0) - lead - jnp.where(side >= 64, side - 64, side)
        label = bucket_of(rel)
        table = jnp.zeros((32, 128), WIDE)
        for h in range(3):
            far = [jnp.sum(far_ref[h, k][:, :128] + far_ref[h, k][:, 128:], axis=0, keepdims=True) for k in range(2)]
            result = jnp.where(sums_row == 15, far[0], jnp.where(sums_row == 31, far[1], 0.0))
            window = near_ref[h]
            for b in range(32):
                part = jnp.sum(jnp.where(label == b, window, 0.0), axis=0, keepdims=True)
                result = result + jnp.where(sums_row == b, part, 0.0)
            total = jnp.sum(result, axis=1, keepdims=True)
            table = jnp.where(lanes == place_ref[0] * 3 + h, total, table)
        table_ref[...] = table


def attention_backward(places, place, strip, q, kv_slots, do_slots, lse, blocks):
    qplace, kplace = places
    count = len(kv_slots)
    micro = q.shape[1]
    rows = 64 * blocks
    kv_cols = kv_slots[0].shape[-1]
    by_micro = lambda width: pl.BlockSpec((GROUPS, 1, 64, width), lambda m, *_: (0, m, 0, 0))
    kv_shape = kv_slots[0].shape
    by_part = lambda n: pl.BlockSpec((n, GROUPS, 1, 64, kv_cols), lambda m, *_: (0, 0, m, 0, 0))
    results = pl.pallas_call(
        functools.partial(backward_kernel, count, blocks),
        out_shape=(jax.ShapeDtypeStruct(q.shape, LOW),)
        + (
            jax.ShapeDtypeStruct(kv_shape, WIDE),
            jax.ShapeDtypeStruct((count // 2 - 1,) + kv_shape, LOW),
            jax.ShapeDtypeStruct((count // 2,) + kv_shape, LOW),
        )
        + (jax.ShapeDtypeStruct((32, 128), WIDE),),
        grid_spec=pltpu.PrefetchScalarGridSpec(
            num_scalar_prefetch=3,
            grid=(micro,),
            in_specs=[
                pl.BlockSpec(strip.shape, lambda m, *_: (0, 0, 0)),
                by_micro(256),
                pl.BlockSpec((1, 3, GROUPS * 64), lambda m, *_: (m, 0, 0)),
            ]
            + [pl.BlockSpec((1, 64, 256), lambda m, *_: (m, 0, 0))] * GROUPS
            + [by_micro(kv_cols)] * count,
            out_specs=(by_micro(256),)
            + (by_micro(kv_cols), by_part(count // 2 - 1), by_part(count // 2))
            + (pl.BlockSpec((32, 128), lambda m, *_: (0, 0)),),
            scratch_shapes=[
                pltpu.VMEM((rows, kv_cols), LOW),
                pltpu.VMEM((rows, kv_cols), WIDE),
                pltpu.VMEM((rows, GROUPS * 64), WIDE),
                pltpu.VMEM((rows, GROUPS * 64), WIDE),
                pltpu.VMEM((3, rows, GROUPS * 64), LOW),
                pltpu.VMEM((3, rows, GROUPS * 64), LOW),
                pltpu.VMEM((rows + 256, GROUPS * 64), WIDE),
                pltpu.VMEM((3, 320, 128), WIDE),
                pltpu.VMEM((3, 2, 8, GROUPS * 64), WIDE),
            ],
        ),
        compiler_params=pltpu.CompilerParams(vmem_limit_bytes=VMEM_LIMIT),
        cost_estimate=pl.CostEstimate(
            flops=micro * 3 * 5 * 2 * rows * GROUPS * 64 * 128 * 2,
            bytes_accessed=micro * rows * kv_cols * 8,
            transcendentals=micro * 3 * rows * GROUPS * 64,
        ),
        name="attention_backward",
    )(qplace, kplace, place, strip, q, lse, *do_slots, *kv_slots)
    return results[0], results[1:4], results[4]


PLACE = pl.BlockSpec(memory_space=pltpu.SMEM)


def whole(count):
    return [pl.BlockSpec(memory_space=pltpu.VMEM)] * count


def first_entry(v):
    return pl.BlockSpec((1,) + v.shape[1:], lambda _: (0,) * v.ndim)


def call(kernel, name, place, operands, out_shape, scratch=(), flops=0):
    operands = [v if isinstance(v, tuple) else (v, False) for v in operands]
    grid = {"grid": (1,)} if any(first for _, first in operands) else {}
    specs = [PLACE] + [first_entry(v) if first else whole(1)[0] for v, first in operands]
    operands = [v for v, _ in operands]
    size = sum(v.size * v.dtype.itemsize for v in operands) + sum(
        v.size * jnp.dtype(v.dtype).itemsize for v in out_shape
    )
    return pl.pallas_call(
        kernel,
        out_shape=tuple(out_shape),
        **grid,
        in_specs=specs,
        out_specs=tuple(whole(len(out_shape))),
        scratch_shapes=list(scratch),
        compiler_params=pltpu.CompilerParams(vmem_limit_bytes=VMEM_LIMIT),
        cost_estimate=pl.CostEstimate(flops=flops, bytes_accessed=size, transcendentals=0),
        name=name,
    )(place, *operands)


def shaped(*shape, dtype=LOW):
    return jax.ShapeDtypeStruct(shape, dtype)


def place_rows(full_ref, slot_refs, index):
    rows = slot_refs[0].shape[0]
    for j, ref in enumerate(slot_refs):
        full_ref[pl.ds(pl.multiple_of((index ^ j) * rows, rows), rows), :] = ref[...]


def rms_scale(values):
    return lax.rsqrt(jnp.mean(values * values, axis=-1, keepdims=True) + EPSILON)


def norm_back(grad_normed, normed, scale):
    return scale * (grad_normed - normed * jnp.mean(grad_normed * normed, axis=-1, keepdims=True))


def project_kernel(parts_f, place_ref, gain_ref, *refs):
    x_refs, w_refs = refs[:GROUPS], refs[GROUPS : GROUPS + parts_f]
    act_ref, q_ref, kv_ref, full_ref = refs[GROUPS + parts_f :]
    place_rows(full_ref, w_refs, place_ref[2])
    micro, rows, width = x_refs[0].shape
    for d in range(GROUPS):
        x = x_refs[d][...].reshape(micro * rows, width).astype(WIDE)
        act_ref[d] = (x * rms_scale(x) * gain_ref[...]).astype(LOW)
    both = dot(act_ref[...].reshape(GROUPS * micro * rows, width), full_ref[...]).astype(LOW)
    q_ref[...] = both[:, :256].reshape(GROUPS, micro, rows, 256)
    kv_ref[...] = both[:, 256:].reshape(GROUPS, micro, rows, 384)


def project(place, gain, x_slots, w_slots):
    micro, rows, width = x_slots[0].shape
    return call(
        functools.partial(project_kernel, len(w_slots)),
        "project",
        place,
        [gain, *x_slots, *w_slots],
        [
            shaped(GROUPS, micro * rows, width),
            shaped(GROUPS, micro, rows, 256),
            shaped(GROUPS, micro, rows, 384),
        ],
        [pltpu.VMEM((width, 640), LOW)],
        flops=2 * GROUPS * micro * rows * width * 640,
    )


def group_rows(place_ref, d):
    return lax.rem(place_ref[0] + d, GROUPS) * 192


def arrange_kernel(parts_f, place_ref, *refs):
    w_refs, (out_ref, full_ref) = refs[:parts_f], refs[parts_f:]
    place_rows(full_ref, w_refs, place_ref[2])
    for d in range(GROUPS):
        at = group_rows(place_ref, d)
        out_ref[d * 256 : d * 256 + 128, :] = full_ref[pl.ds(pl.multiple_of(at, 64), 128), :]
        out_ref[d * 256 + 128 : d * 256 + 256, :] = full_ref[pl.ds(pl.multiple_of(at + 64, 64), 128), :]


def arrange(place, w_slots):
    width = w_slots[0].shape[1]
    return call(
        functools.partial(arrange_kernel, len(w_slots)),
        "arrange",
        place,
        w_slots,
        [shaped(GROUPS * 256, width)],
        [pltpu.VMEM((width, width), LOW)],
    )[0]


def joined_kernel(place_ref, gain_ref, x_ref, w_ref, *refs):
    o_refs, (resid_ref, act_ref) = refs[:GROUPS], refs[GROUPS:]
    micro, rows, width = x_ref.shape
    o = jnp.concatenate([r[...].reshape(micro * rows, 256) for r in o_refs], axis=1)
    total = x_ref[...].reshape(micro * rows, width).astype(WIDE) + dot(o, w_ref[...])
    resid_ref[...] = total
    act_ref[...] = (total * rms_scale(total) * gain_ref[...]).astype(LOW)


def joined(place, gain, x, o_slots, w_rel):
    micro, rows, width = x.shape
    return call(
        joined_kernel,
        "joined",
        place,
        [gain, x, w_rel, *o_slots],
        [shaped(micro * rows, width, dtype=WIDE), shaped(micro * rows, width)],
        flops=2 * micro * rows * width * 1024,
    )


GELU_A = 0.7978845608028654
GELU_B = 0.044715


def put_part(refs, j, value):
    own_ref, even_ref, odd_ref = refs
    if j == 0:
        own_ref[...] = value
    elif j % 2:
        odd_ref[j // 2] = value.astype(odd_ref.dtype)
    else:
        even_ref[j // 2 - 1] = value.astype(even_ref.dtype)


def part_shapes(shape, fast):
    return [
        shaped(*shape, dtype=WIDE),
        shaped(fast // 2 - 1, *shape),
        shaped(fast // 2, *shape),
    ]


def feed_kernel(parts_f, fast, place_ref, *refs):
    act_refs, refs = refs[:fast], refs[fast:]
    g_refs, refs = refs[:fast], refs[fast:]
    pair_refs, refs = refs[:parts_f], refs[parts_f:]
    down_refs, refs = refs[:parts_f], refs[parts_f:]
    two_refs, out_refs, refs = refs[:3], refs[3:6], refs[6:]
    hid_ref, grad_ref, pair_ref, down_ref = refs
    place_rows(pair_ref, pair_refs, place_ref[2])
    place_rows(down_ref, down_refs, place_ref[2])
    cols = hid_ref.shape[-1]
    rows = act_refs[0].shape[0]
    act = jnp.concatenate([r[...] for r in act_refs], axis=0)
    g = jnp.concatenate([r[...] for r in g_refs], axis=0)
    both = dot(act, pair_ref[...])
    dh = dot_t(g, down_ref[...])
    for j in range(fast):
        at = slice(j * rows, j * rows + rows)
        z, up = both[at, :cols], both[at, cols:]
        square = z * z
        t = jnp.tanh(GELU_A * (z + GELU_B * square * z))
        half = 0.5 * (1.0 + t)
        gelu = z * half
        slope = half + (0.5 * z) * (1.0 - t * t) * (GELU_A * (1.0 + 3.0 * GELU_B * square))
        hid_ref[j] = (gelu * up).astype(LOW)
        grad_ref[j, :, :cols] = (dh[at] * up * slope).astype(LOW)
        grad_ref[j, :, cols:] = (dh[at] * gelu).astype(LOW)
    two = dot_t(grad_ref[...].reshape(fast * rows, 2 * cols), pair_ref[...])
    out = dot(hid_ref[...].reshape(fast * rows, cols), down_ref[...])
    for j in range(fast):
        put_part(two_refs, j, two[j * rows : j * rows + rows])
        put_part(out_refs, j, out[j * rows : j * rows + rows])


def feed(place, act_slots, g_slots, pair_slots, down_slots):
    fast, parts_f = len(act_slots), len(pair_slots)
    rows, width = act_slots[0].shape
    cols = down_slots[0].shape[0] * parts_f
    results = call(
        functools.partial(feed_kernel, parts_f, fast),
        "feed",
        place,
        [*act_slots, *g_slots, *pair_slots, *down_slots],
        part_shapes((rows, width), fast) * 2 + [shaped(fast, rows, cols), shaped(fast, rows, 2 * cols)],
        [pltpu.VMEM((width, 2 * cols), LOW), pltpu.VMEM((cols, width), LOW)],
        flops=2 * fast * rows * width * cols * 6,
    )
    return results[:3], results[3:6], results[-2], results[-1]


def packing(piece, rows):
    if rows == 3 * piece:
        return [(0, k * 256, k * piece, 0, piece, 256) for k in range(3)]
    half = piece // 2
    return [
        (0, 0, 0, 0, piece, 512),
        (0, 512, piece, 0, half, 256),
        (half, 512, piece, 256, half, 256),
    ]


def pair_grads_kernel(fast, place_ref, *refs):
    act_refs, grad_ref, refs = refs[:fast], refs[fast], refs[fast + 1 :]
    outs, full_ref = refs[:-1], refs[-1]
    act = jnp.concatenate([r[...] for r in act_refs], axis=0)
    full_ref[...] = t_dot(act, grad_ref[...].reshape(act.shape[0], -1))
    rows = outs[0].shape[0]
    for j, out in enumerate(outs):
        at = pl.multiple_of((place_ref[2] ^ j) * rows, rows)
        out[...] = full_ref[pl.ds(at, rows), :].astype(out.dtype)


def pair_grads(place, act_slots, grads, parts_f):
    fast, rows, double = grads.shape
    width = act_slots[0].shape[1]
    types = [WIDE] + [LOW] * (parts_f - 1)
    return call(
        functools.partial(pair_grads_kernel, fast),
        "pair_grads",
        place,
        [*act_slots, grads],
        [shaped(width // parts_f, double, dtype=t) for t in types],
        [pltpu.VMEM((width, double), WIDE)],
        flops=2 * fast * rows * width * double,
    )


def down_grads_kernel(fast, place_ref, *refs):
    g_refs, hid_ref, refs = refs[:fast], refs[fast], refs[fast + 1 :]
    outs, full_ref = refs[:-1], refs[-1]
    g = jnp.concatenate([r[...] for r in g_refs], axis=0)
    full_ref[...] = t_dot(hid_ref[...].reshape(g.shape[0], -1), g)
    rows = outs[0].shape[0]
    piece = full_ref.shape[0] // len(outs)
    for j, out in enumerate(outs):
        for r, c, to_r, to_c, n, w in packing(piece, rows):
            at = pl.multiple_of((place_ref[2] ^ j) * piece + r, 8)
            out[to_r : to_r + n, to_c : to_c + w] = full_ref[pl.ds(at, n), c : c + w].astype(out.dtype)


def down_grads(place, g_slots, hid, parts_f):
    fast, rows, cols = hid.shape
    width = g_slots[0].shape[1]
    types = [WIDE] + [LOW] * (parts_f - 1)
    return call(
        functools.partial(down_grads_kernel, fast),
        "down_grads",
        place,
        [*g_slots, hid],
        [shaped(width // parts_f, cols, dtype=t) for t in types],
        [pltpu.VMEM((cols, width), WIDE)],
        flops=2 * fast * rows * width * cols,
    )


def group_split_kernel(count, place_ref, *refs):
    own_ref, send_refs = refs[count], refs[count + 1 :]
    rows = own_ref.shape[0]

    def part(d):
        at = pl.ds(pl.multiple_of(lax.rem(place_ref[0] + d, GROUPS) * rows, 8), rows)
        return sum(r[at, :].astype(WIDE) for r in refs[:count])

    own_ref[...] = part(0)
    for d, ref in enumerate(send_refs, 1):
        ref[...] = part(d).astype(ref.dtype)


def group_split(place, parts):
    rows, cols = parts[0].shape
    cut = rows // GROUPS
    results = call(
        functools.partial(group_split_kernel, len(parts)),
        "group_split",
        place,
        parts,
        [shaped(cut, cols, dtype=WIDE)] + [shaped(cut, cols)] * (GROUPS - 1),
    )
    return results[0], list(results[1:])


def group_halves_kernel(count, place_ref, *refs):
    keep_ref, send_ref = refs[count:]
    rows = keep_ref.shape[1]
    for d in range(GROUPS):
        at = pl.ds(pl.multiple_of((place_ref[0] ^ d) * rows, 8), rows)
        total = sum(r[at, :].astype(WIDE) for r in refs[:count])
        if d % 2:
            send_ref[d // 2] = total.astype(send_ref.dtype)
        else:
            keep_ref[d // 2] = total


def group_halves(place, parts):
    rows, cols = parts[0].shape
    cut = (GROUPS // 2, rows // GROUPS, cols)
    return call(
        functools.partial(group_halves_kernel, len(parts)),
        "group_halves",
        place,
        parts,
        [shaped(*cut, dtype=WIDE), shaped(*cut)],
    )


def summed(refs):
    return sum((r[0] if len(r.shape) == 3 else r[...]).astype(WIDE) for r in refs)


def branch_kernel(count, place_ref, gain_ref, resid_ref, g_ref, w_ref, *refs):
    two_refs, refs = refs[:count], refs[count:]
    grad_ref, low_ref, gain_out = refs[:3]
    do_refs = refs[3:]
    micro, rows, _ = do_refs[0].shape
    grad_two = summed(two_refs)
    resid = resid_ref[...]
    scale = rms_scale(resid)
    normed = resid * scale
    gain_out[...] = jnp.sum(grad_two * normed, axis=0, keepdims=True)
    grad = g_ref[...].astype(WIDE) + norm_back(grad_two * gain_ref[...], normed, scale)
    grad_ref[...] = grad
    low = grad.astype(LOW)
    low_ref[...] = low
    both = dot_t(low, w_ref[...]).astype(LOW)
    for d in range(GROUPS):
        do_refs[d][...] = both[:, d * 256 : d * 256 + 256].reshape(micro, rows, 256)


def branch(place, gain, resid, g, two_list, w_rel, micro):
    rows, width = resid.shape
    results = call(
        functools.partial(branch_kernel, len(two_list)),
        "branch",
        place,
        [gain, resid, g, w_rel, *two_list],
        [shaped(rows, width, dtype=WIDE), shaped(rows, width), shaped(1, width, dtype=WIDE)]
        + [shaped(micro, rows // micro, 256)] * GROUPS,
        flops=2 * rows * width * 1024,
    )
    return results[0], results[1], results[2], list(results[3:])


def with_rows(index, rows, count, action):
    if rows % 8 == 0:
        action(pl.ds(pl.multiple_of(index * rows, 8), rows))
        return
    for known in range(count):

        @pl.when(index == known)
        def _():
            action(slice(known * rows, known * rows + rows))


def write_chunks(place_ref, full_ref, keep_ref, send_ref):
    parts_f, halves, rows, _ = keep_ref.shape
    for i in range(parts_f):
        for k in range(halves):
            for odd, ref in ((0, keep_ref), (1, send_ref)):
                index = (place_ref[2] ^ i) * (2 * halves) + (place_ref[1] ^ (2 * k + odd))

                def copy(at):
                    ref[i, k] = full_ref[at, :].astype(ref.dtype)

                with_rows(index, rows, 2 * halves * parts_f, copy)


def out_grads_kernel(place_ref, low_ref, *refs):
    o_refs = refs[:GROUPS]
    keep_ref, send_ref, full_ref = refs[GROUPS:]
    micro, rows, _ = o_refs[0].shape
    low = low_ref[...]
    for d in range(GROUPS):
        both = t_dot(o_refs[d][...].reshape(micro * rows, 256), low)
        at = group_rows(place_ref, d)
        full_ref[pl.ds(pl.multiple_of(at, 64), 128), :] = both[:128]
        full_ref[pl.ds(pl.multiple_of(at + 128, 64), 64), :] = both[192:]
    write_chunks(place_ref, full_ref, keep_ref, send_ref)


def out_grads(place, low, o_slots, parts_f, fast):
    rows, width = low.shape
    chunk = (parts_f, fast // 2, width // (parts_f * fast), width)
    return call(
        out_grads_kernel,
        "out_grads",
        place,
        [low, *o_slots],
        [shaped(*chunk, dtype=WIDE), shaped(*chunk)],
        [pltpu.VMEM((width, width), WIDE)],
        flops=2 * rows * width * 1024,
    )


def input_grads_kernel(parts_f, count, place_ref, act_ref, dq_ref, *refs):
    x_refs, refs = refs[:GROUPS], refs[GROUPS:]
    dkv_refs, refs = refs[:count], refs[count:]
    w_refs, refs = refs[:parts_f], refs[parts_f:]
    one_keep, one_send, gain_out, keep_ref, send_ref, full_ref, sums_ref, both_ref, one_ref = refs
    place_rows(full_ref, w_refs, place_ref[2])
    groups, rows, width = act_ref.shape
    micro = dq_ref.shape[1]
    gain_total = jnp.zeros((1, width), WIDE)
    for d in range(GROUPS):
        dkv = sum((r[0, d] if len(r.shape) == 5 else r[d]).astype(WIDE) for r in dkv_refs)
        dkv = dkv.astype(LOW).reshape(rows, 384)
        both = jnp.concatenate([dq_ref[d].reshape(rows, 256), dkv], axis=1)
        both_ref[d] = both
        one = dot_t(both, full_ref[...])
        x = x_refs[d][...].reshape(rows, width).astype(WIDE)
        gain_total = gain_total + jnp.sum(one * (x * rms_scale(x)), axis=0, keepdims=True)
        one_ref[lax.rem(place_ref[0] + GROUPS - d, GROUPS)] = one
    for d in range(GROUPS):
        value = one_ref[place_ref[0] ^ d]
        if d % 2:
            one_send[d // 2] = value.astype(LOW)
        else:
            one_keep[d // 2] = value
    gain_out[...] = gain_total
    sums_ref[...] = t_dot(act_ref[...].reshape(groups * rows, width), both_ref[...].reshape(groups * rows, 640))
    write_chunks(place_ref, sums_ref, keep_ref, send_ref)


def input_grads(place, act, dq, x_slots, dkv_list, w_slots, fast):
    groups, rows, width = act.shape
    micro = dq.shape[1]
    parts_f = len(w_slots)
    chunk = (parts_f, fast // 2, width // (parts_f * fast), 640)
    return call(
        functools.partial(input_grads_kernel, parts_f, len(dkv_list)),
        "input_grads",
        place,
        [act, dq, *x_slots, *dkv_list, *w_slots],
        [shaped(GROUPS // 2, rows, width, dtype=WIDE), shaped(GROUPS // 2, rows, width)]
        + [shaped(1, width, dtype=WIDE), shaped(*chunk, dtype=WIDE), shaped(*chunk)],
        [
            pltpu.VMEM((width, 640), LOW),
            pltpu.VMEM((width, 640), WIDE),
            pltpu.VMEM((groups, rows, 640), LOW),
            pltpu.VMEM((groups, rows, width), WIDE),
        ],
        flops=4 * groups * rows * width * 640,
    )


def last_kernel(count, place_ref, gain_ref, x_ref, grad_ref, resid_ref, *refs):
    one_ref, got_ref, refs = refs[0], refs[1], refs[2:]
    out_refs, refs = refs[:count], refs[count:]
    x_grad_ref, out_ref = refs
    micro, rows, width = x_ref.shape
    grad_one = one_ref[...] + got_ref[: micro * rows, :].astype(WIDE)
    x = x_ref[...].reshape(micro * rows, width).astype(WIDE)
    scale = rms_scale(x)
    normed = x * scale
    x_grad_ref[...] = grad_ref[...] + norm_back(grad_one * gain_ref[...], normed, scale)
    parts = [(r[0] if len(r.shape) == 3 else r[r.shape[0] - micro * rows :, :]).astype(WIDE) for r in out_refs]
    out_ref[...] = (resid_ref[...] + sum(parts)).astype(LOW)


def last(place, gain, x, grad, resid, one, one_got, out_list):
    rows, width = resid.shape
    return call(
        functools.partial(last_kernel, len(out_list)),
        "last",
        place,
        [gain, x, grad, resid, one, one_got, *out_list],
        [shaped(rows, width, dtype=WIDE), shaped(rows, width)],
    )


def pair_finish_kernel(parts_f, fast, place_ref, *refs):
    pair_refs, (gate_ref, up_ref) = refs[:fast], refs[fast:]
    _, rows, double = pair_refs[0].shape
    cols = double // 2
    piece = cols // parts_f
    for j in range(fast):
        other = place_ref[1] ^ j
        for d in range(GROUPS):
            at = pl.ds(pl.multiple_of(lax.rem(place_ref[0] + GROUPS - d, GROUPS) * rows, 8), rows)
            for start, ref in ((0, gate_ref), (cols, up_ref)):
                for k in range(parts_f):
                    value = pair_refs[j][d, :, start + k * piece : start + (k + 1) * piece].astype(WIDE)
                    if piece % 128 == 0:
                        to = pl.multiple_of(k * fast * piece + other * piece, 128)
                        ref[at, pl.ds(to, piece)] = value
                    else:
                        for l in range(fast):

                            @pl.when(other == l)
                            def _():
                                ref[at, (k * fast + l) * piece : (k * fast + l + 1) * piece] = value


def low_finish_kernel(parts_f, fast, place_ref, *refs):
    low_refs, (down_ref, pack_ref) = refs[:fast], refs[fast:]
    _, rows, cols = low_refs[0].shape
    piece = cols // parts_f
    for j in range(fast):
        for d in range(GROUPS):
            at = pl.ds(pl.multiple_of(lax.rem(place_ref[0] + GROUPS - d, GROUPS) * rows, 8), rows)
            pack_ref[at, :] = low_refs[j][d].astype(WIDE)
        for r, c, to_r, to_c, n, w in packing(piece, rows * GROUPS):
            at = pl.ds(pl.multiple_of((place_ref[1] ^ j) * piece + r, 8), n)
            down_ref[at, c : c + w] = pack_ref[to_r : to_r + n, to_c : to_c + w]


def low_finish(place, packs, parts_f):
    fast = len(packs)
    _, rows, cols = packs[0].shape
    return call(
        functools.partial(low_finish_kernel, parts_f, fast),
        "low_finish",
        place,
        packs,
        [shaped(cols // parts_f * fast, rows * GROUPS * parts_f, dtype=WIDE)],
        [pltpu.VMEM((rows * GROUPS, cols), WIDE)],
    )[0]


def input_finish_kernel(fast, place_ref, *refs):
    pack_refs = refs[:fast]
    query_ref, key_ref, value_ref, out_ref = refs[fast:]
    rows = pack_refs[0].shape[0]
    for j in range(fast):
        value = pack_refs[j][:, GROUPS * 640 :].astype(WIDE)

        def place_out(at):
            out_ref[at, :] = value

        with_rows(place_ref[1] ^ j, rows, fast, place_out)
    for h in range(GROUPS):

        @pl.when(place_ref[0] == h)
        def _():
            for j in range(fast):
                starts = [(h - g) % GROUPS * 640 for g in range(GROUPS)]
                part = lambda a, b: pack_refs[j][:, a:b].astype(WIDE)
                query = jnp.concatenate([part(s, s + 192) for s in starts], axis=1)
                key = jnp.concatenate([part(s + 256, s + 448) for s in starts], axis=1)
                value = jnp.concatenate([p for s in starts for p in (part(s + 512, s + 640), part(s + 448, s + 512))], axis=1)

                def place_in(at):
                    query_ref[at, :] = query
                    key_ref[at, :] = key
                    value_ref[at, :] = value

                with_rows(place_ref[1] ^ j, rows, fast, place_in)


def most_finish_kernel(parts_f, fast, place_ref, *refs):
    pair_refs, pack_refs, refs = refs[:fast], refs[fast : 2 * fast], refs[2 * fast :]
    pair_finish_kernel(parts_f, fast, place_ref, *pair_refs, *refs[:2])
    input_finish_kernel(fast, place_ref, *pack_refs, *refs[2:])


def most_finish(place, pair_packs, packs, parts_f, width):
    fast = len(packs)
    _, rows, double = pair_packs[0].shape
    return call(
        functools.partial(most_finish_kernel, parts_f, fast),
        "most_finish",
        place,
        [*pair_packs, *packs],
        [shaped(rows * GROUPS, double // 2 * fast, dtype=WIDE)] * 2
        + [shaped(packs[0].shape[0] * fast, width, dtype=WIDE)] * 4,
    )


def spread_groups(v):
    return [v] + [shift(v, d) for d in range(1, GROUPS)]


def gather_pack(pack, fast):
    slots = {0: pack}
    for bit in bits_down(fast):
        for j in list(slots):
            slots[j ^ bit] = hop(slots[j], "ctx", bit)
    return [slots[j] for j in range(fast)]


def after(value, *others):
    return lax.optimization_barrier((value, *others))[0]


def body(
    tokens,
    offsets,
    norm1_gain,
    norm2_gain,
    bias_table,
    w_query,
    w_key,
    w_value,
    w_out,
    w_gate,
    w_up,
    w_down,
    cotangent,
):
    micro, _, block_rows, width = tokens.shape
    blocks = lax.axis_size("ctx")
    parts_f = lax.axis_size("fsdp")
    fast = blocks // GROUPS
    ctx = lax.axis_index("ctx")
    f = lax.axis_index("fsdp")
    hi, lo = ctx // fast, ctx % fast
    group_cols = w_query.shape[1] // GROUPS
    own_rows = micro * block_rows
    hidden = w_gate.shape[1]
    piece = hidden // (parts_f * fast)
    part_rows = w_query.shape[0]
    gain_one = norm1_gain.reshape(1, width)
    gain_two = norm2_gain.reshape(1, width)
    place = jnp.stack([hi, lo, f]).astype(jnp.int32)

    own_x = tokens[:, 0]
    g_low = cotangent[:, 0].reshape(own_rows, width)
    x_slots = spread_groups(own_x)

    def group_of(matrix):
        return lax.dynamic_slice_in_dim(matrix, hi * group_cols, group_cols, axis=1)

    q_part, k_part, v_part = group_of(w_query), group_of(w_key), group_of(w_value)
    gap = jnp.zeros((part_rows, 64), LOW)
    qkv_part = jnp.concatenate([q_part, gap, k_part, v_part[:, 128:], v_part[:, :128]], axis=1)
    qkv_slots = slots_out(qkv_part, "fsdp", parts_f)

    def pieces(matrix):
        return [
            lax.dynamic_slice_in_dim(matrix, (k * fast + lo) * piece, piece, axis=1) for k in range(parts_f)
        ]

    pair_part = jnp.concatenate(pieces(w_gate) + pieces(w_up), axis=1)
    down_part = lax.dynamic_slice_in_dim(w_down, lo * piece, piece, axis=0)

    starts = offsets[:, 0]
    group_ids = (hi + GROUPS - jnp.arange(GROUPS, dtype=jnp.int32)) % GROUPS
    slot_ids = lo ^ jnp.arange(fast, dtype=jnp.int32)
    kplace = jnp.take(starts, group_ids[None, :] * fast + slot_ids[:, None], axis=1)
    table_group = lax.dynamic_slice_in_dim(bias_table, hi * 3, 3, axis=1)
    strip = make_strip(table_group, blocks)

    tick = [place]

    def fence(*values):
        tick[0], *values = lax.optimization_barrier((tick[0], *values))
        return values[0] if len(values) == 1 else values

    def shifted(parts, sign):
        return [shift(v, sign * d) for d, v in enumerate(parts, 1)]

    def to_f(parts):
        return [hop(v, "fsdp", j) for j, v in enumerate(parts, 1)]

    def groups_sum(own, parts):
        return (own + sum(v.astype(WIDE) for v in parts)).astype(LOW)

    def far_places(v):
        have = {0: v}
        for bit in bits_down(fast // 2):
            for j in list(have):
                have[j ^ (2 * bit)] = hop(have[j], "ctx", 2 * bit)
        return have

    def both_cores(have):
        return [v for j in range(0, fast, 2) for v in (have[j], hop(have[j], "ctx", 1))]

    strip, kplace = fence(strip, kplace)
    places = (kplace[:, 0], kplace)
    out_w, pair_w, x_slots, qkv_slots = fence(w_out, pair_part, x_slots, qkv_slots)
    act_one, q, kv = project(tick[0], gain_one, x_slots, qkv_slots)
    kv_slots = slots_out(kv, "ctx", fast)
    out_w_slots = slots_out(out_w, "fsdp", parts_f)
    pair_slots = slots_out(pair_w, "fsdp", parts_f)
    g_low, kv_slots = fence(g_low, kv_slots)
    g_have = {0: g_low, 1: hop(g_low, "ctx", 1)}
    for bit in bits_down(fast // 2):
        for j in [j for j in g_have if j % 2 == 0]:
            g_have[j ^ (2 * bit)] = hop(g_have[j], "ctx", 2 * bit)
    o_group, lse = attention_forward(places, strip, q, kv_slots, blocks)
    o_group, g_have, out_w_slots, down_w = fence(o_group, g_have, out_w_slots, down_part)
    o_slots = [o_group[0]] + shifted(o_group[1:], -1)
    down_slots = slots_out(down_w, "fsdp", parts_f)
    for j in range(2, fast, 2):
        g_have[j + 1] = hop(g_have[j], "ctx", 1)
    g_slots = [g_have[j] for j in range(fast)]
    w_rel = arrange(tick[0], out_w_slots)
    o_slots, w_rel = fence(o_slots, w_rel)
    resid, act_two = joined(tick[0], gain_two, own_x, o_slots, w_rel)
    act_two, g_slots = fence(act_two, g_slots)
    act_slots = slots_out(act_two, "ctx", fast)
    two_parts, out_parts, hid, grads = feed(tick[0], act_slots, g_slots, pair_slots, down_slots)
    two_parts, out_parts = fence(two_parts, out_parts)

    two_odd = two_parts[2]
    two_got = hop(two_odd, "ctx", 1)
    pair_keep, *pair_sends = pair_grads(tick[0], act_slots, grads, parts_f)
    out_got_one = hop(out_parts[2], "ctx", 1)
    two_got, pair_keep, pair_sends, out_got_one = fence(two_got, pair_keep, pair_sends, out_got_one)
    pair_got = to_f(pair_sends)
    two_list, sent = pairs_on(two_parts, two_got, fast)
    low_keep, *low_sends = down_grads(fence(tick[0], sent)[0], g_slots, hid, parts_f)
    got, low_keep, low_sends = fence([v for v, _ in two_list], low_keep, low_sends)
    two_list = [(v, first) for v, (_, first) in zip(got, two_list)]
    grad_resid, grad_low, gain_two_part, do_own = branch(
        tick[0], gain_two, resid, g_low, two_list, w_rel, micro
    )
    do_own = fence(*do_own)
    do_slots = [do_own[0]] + shifted(do_own[1:], 1)
    out_keep, out_send = out_grads(tick[0], grad_low, o_slots, parts_f, fast)
    out_keep, out_send, do_slots, pair_got = fence(out_keep, out_send, do_slots, pair_got)
    out_got = hop(out_send, "ctx", 1)
    pair_own, pair_sends = group_split(tick[0], [pair_keep, *pair_got])
    pair_own, pair_sends, low_sends, out_total = fence(
        pair_own, pair_sends, low_sends, out_keep + out_got.astype(WIDE)
    )

    pair_parts = shifted(pair_sends, 1)
    low_got = to_f(low_sends)
    out_total = halve(out_total, "fsdp", 1)
    dq, dkv_parts, table_part = attention_backward(
        places, tick[0], strip, q, kv_slots, do_slots, lse, blocks
    )
    dq, dkv_parts, pair_parts, low_got, out_total = fence(dq, dkv_parts, pair_parts, low_got, out_total)
    dkv_list, sent = pairs_on(dkv_parts, hop(dkv_parts[2], "ctx", 1), fast)
    low_keep, low_send = group_halves(tick[0], [low_keep, *low_got])
    pair_chunk, low_send, out_total, _ = fence(groups_sum(pair_own, pair_parts), low_send, out_total, sent)
    pair_spread = spread_groups(pair_chunk)
    if fast == 4:
        out_far = (out_parts[1][0].astype(WIDE) + out_got_one[1].astype(WIDE)).astype(LOW)
        far = jnp.concatenate([out_total[1].astype(LOW), out_far])
        far = hop(far, "ctx", 2)
    got = fence([v for v, _ in dkv_list])
    dkv_list = [(v, first) for v, (_, first) in zip(got, dkv_list)]
    one_keep, one_send, gain_one_part, in_keep, in_send = input_grads(
        tick[0], act_one, dq, x_slots, dkv_list, qkv_slots, fast
    )
    one_keep, one_send, in_keep, in_send, low_send, pair_spread = fence(
        one_keep, one_send, in_keep, in_send, low_send, pair_spread
    )
    if fast == 4:
        far = fence(far)
        chunk = out_total.shape[1]
        out_low = (out_total[0] + far[:chunk].astype(WIDE)).astype(LOW)
        out_list = [(out_parts[0], False), (out_got_one, True), (far, False)]
    else:
        out_low = halve(out_total, "ctx", 2).astype(LOW)
        out_list, _ = pairs_on(out_parts, out_got_one, fast)

    def send_small(v, small, bit):
        high = small.astype(LOW)
        rest = (small - high.astype(WIDE)).astype(LOW)
        return hop(jnp.concatenate([v, high, rest]), "ctx", bit), high.astype(WIDE) + rest.astype(WIDE)

    def take_small(got, own):
        lines = own.shape[0]
        count = got.shape[0] - 2 * lines
        return got[:count], own + got[count : count + lines].astype(WIDE) + got[count + lines :].astype(WIDE)

    def two_hops(a, b, bit):
        if a.shape[:-1] != b.shape[:-1]:
            return hop(a, "ctx", bit), hop(b, "ctx", bit)
        got = hop(jnp.concatenate([a, b], axis=-1), "ctx", bit)
        return got[..., : a.shape[-1]], got[..., a.shape[-1] :]

    head_count = bias_table.shape[1]
    table_row = table_part[:, :head_count].reshape(1, -1)
    table_row = jnp.pad(table_row, ((0, 5), (0, width - table_row.shape[1])))
    small = jnp.concatenate([gain_one_part, gain_two_part, table_row])
    in_got = hop(in_send, "ctx", 1)
    out_two = jnp.stack([out_low[:, : width // 2], out_low[:, width // 2 :]])
    low_got, out_got = two_hops(low_send, out_two, fast)
    pair_have = far_places(jnp.stack(pair_spread))
    one_got, small = send_small(one_send.reshape(-1, width), small, fast)
    in_total = fence(in_keep + in_got.astype(WIDE))
    in_total, low_got, out_got = fence(halve(in_total, "fsdp", 1), low_got, out_got)
    low_sum = low_keep + low_got.astype(WIDE)
    out_two = (out_two.astype(WIDE) + out_got.astype(WIDE)).astype(LOW)
    out_low = jnp.concatenate([out_two[0], out_two[1]], axis=1)
    low_got, out_got = two_hops(low_sum[1].astype(LOW), out_low, 2 * fast)
    in_chunk, pair_have = fence(halve(in_total, "ctx", 2).astype(LOW), pair_have)
    in_spread = spread_groups(in_chunk)
    in_spread, low_got, out_got, one_got = fence(in_spread, low_got, out_got, one_got)
    low_spread = spread_groups((low_sum[0] + low_got.astype(WIDE)).astype(LOW))
    out_low = (out_low.astype(WIDE) + out_got.astype(WIDE)).astype(LOW)
    in_have = far_places(jnp.concatenate([*in_spread, out_low], axis=1))
    one_got, small = take_small(one_got, small)
    one_got = one_got.reshape(one_keep.shape)
    one_sum = one_keep[0] + one_got[0].astype(WIDE)
    one_send = (one_keep[1] + one_got[1].astype(WIDE)).astype(LOW)
    small = small + hop(small, "ctx", 1)
    for bit in bits_up(parts_f):
        small = small + hop(small, "fsdp", bit)
    low_spread, one_send, pair_have, small = fence(low_spread, one_send, pair_have, small)
    low_have = far_places(jnp.stack(low_spread))
    one_got, small = send_small(one_send, small, 2 * fast)
    pair_packs = both_cores(pair_have)
    in_packs, pair_packs = fence(both_cores(in_have), pair_packs)
    w_gate_grad, w_up_grad, w_query_grad, w_key_grad, w_value_grad, w_out_grad = most_finish(
        tick[0], pair_packs, in_packs, parts_f, width
    )
    w_query_grad, one_got, low_have = fence(w_query_grad, one_got, low_have)
    low_packs = both_cores(low_have)
    small = take_small(one_got, small)[1]
    for bit in bits_down(fast // 2):
        small = small + hop(small, "ctx", 2 * bit)
    x_grad, result = last(tick[0], gain_one, own_x, grad_resid, resid, one_sum, one_got, out_list)
    x_grad, low_packs = fence(x_grad, low_packs)
    w_down_grad = low_finish(tick[0], low_packs, parts_f)

    gain_rows = width // parts_f
    table_rows = bias_table.shape[0] // parts_f
    gain_one_grad = lax.dynamic_slice_in_dim(small[0], f * gain_rows, gain_rows)
    gain_two_grad = lax.dynamic_slice_in_dim(small[1], f * gain_rows, gain_rows)
    table_grad = small[2, : bias_table.size].reshape(bias_table.shape)
    table_grad = lax.dynamic_slice_in_dim(table_grad, f * table_rows, table_rows)

    return (
        result.reshape(micro, 1, block_rows, width),
        x_grad.reshape(micro, 1, block_rows, width),
        gain_one_grad,
        gain_two_grad,
        table_grad,
        w_query_grad,
        w_key_grad,
        w_value_grad,
        w_out_grad,
        w_gate_grad,
        w_up_grad,
        w_down_grad,
    )


def solution(mesh):
    in_specs = (
        P(None, "fsdp", "ctx", None),
        P(None, "fsdp", None),
        P(),
        P(),
        P(),
        P("fsdp", None),
        P("fsdp", None),
        P("fsdp", None),
        P("fsdp", None),
        P("fsdp", None),
        P("fsdp", None),
        P("fsdp", None),
        P(None, "fsdp", "ctx", None),
    )
    out_specs = (
        P(None, "fsdp", "ctx", None),
        P(None, "fsdp", "ctx", None),
        P("fsdp"),
        P("fsdp"),
        P("fsdp", None),
        P("fsdp", None),
        P("fsdp", None),
        P("fsdp", None),
        P("fsdp", None),
        P("fsdp", None),
        P("fsdp", None),
        P("fsdp", None),
    )
    return jax.shard_map(body, mesh=mesh, in_specs=in_specs, out_specs=out_specs, check_vma=False)
```

```python
import functools

import jax
import jax.numpy as jnp
from jax import lax
from jax.experimental import pallas as pl
from jax.experimental.pallas import tpu as pltpu
from jax.sharding import PartitionSpec as P

EPSILON = 1e-06
GROUPS = 4
WIDE = jnp.float32
LOW = jnp.bfloat16
FAR = 91
NEAR_LEAD = 96
VMEM_LIMIT = 60 * 1024 * 1024


def dot(a, b):
    return jnp.dot(a, b, preferred_element_type=WIDE)


def dot_t(a, b):
    return lax.dot_general(a, b, (((1,), (1,)), ((), ())), preferred_element_type=WIDE)


def t_dot(a, b):
    return lax.dot_general(a, b, (((0,), (0,)), ((), ())), preferred_element_type=WIDE)


def bucket_of(relative):
    distance = jnp.abs(relative)
    squared = distance * distance
    counted = jnp.zeros_like(relative)
    for exponent in range(1, 8):
        counted = counted + (squared >= 64 * 2**exponent).astype(jnp.int32)
    within = jnp.where(distance < 8, distance, 8 + counted)
    return jnp.where(relative > 0, 16, 0).astype(jnp.int32) + within


def hop(v, axis, bit):
    size = lax.axis_size(axis)
    return lax.ppermute(v, axis, [(i, i ^ bit) for i in range(size)])


def bits_down(size):
    bit = size // 2
    while bit >= 1:
        yield bit
        bit //= 2


def bits_up(size):
    return reversed(list(bits_down(size)))


def shift(v, steps):
    size = lax.axis_size("ctx")
    stride = size // GROUPS
    return lax.ppermute(v, "ctx", [(i, (i + steps * stride) % size) for i in range(size)])


def slots_out(v, axis, count):
    slots = {0: v}
    for bit in bits_down(count):
        for j in list(slots):
            slots[j ^ bit] = hop(slots[j], axis, bit)
    return [slots[j] for j in range(count)]


def pairs_on(parts, got, count):
    own, evens, _ = parts
    have = {k: evens[k - 1].astype(WIDE) + got[k].astype(WIDE) for k in range(1, count // 2)}
    mine, sent = [(own, False), (got, True)], []
    for bit in bits_up(count // 2):
        for k in sorted(have):
            if k & bit:
                sent.append(have[k].astype(LOW))
                part = hop(sent[-1], "ctx", 2 * bit)
                if k ^ bit:
                    have[k ^ bit] = have[k ^ bit] + part.astype(WIDE)
                else:
                    mine.append((part, False))
                del have[k]
    return mine, sent


def pairs_back(own, evens, odds, count):
    return pairs_on((own, evens, odds), hop(odds, "ctx", 1), count)


def halve(v, axis, unit):
    count = v.shape[0]
    for bit in bits_down(count):
        v = v[:bit] + hop(v[bit:].astype(LOW), axis, bit * unit).astype(WIDE)
    return v[0]


def strip_kernel(blocks, table_ref, strip_ref):
    centre = 64 * (blocks - 1)
    rows = 2 * 64 * blocks
    near = 256
    start = centre - NEAR_LEAD
    chunk = 128
    heads = table_ref.shape[1]

    def relative(first, count):
        u = lax.broadcasted_iota(jnp.int32, (count, 128), 0) + first
        i = lax.broadcasted_iota(jnp.int32, (count, 128), 1)
        return u - centre - jnp.where(i >= 64, i - 64, i)

    for h in range(heads):
        strip_ref[h, : start, :] = jnp.full((start, 128), table_ref[15, h], WIDE)
        strip_ref[h, start + near :, :] = jnp.full((rows - start - near, 128), table_ref[31, h], WIDE)
    for first in range(start, start + near, chunk):
        label = bucket_of(relative(first, chunk))
        for h in range(heads):
            value = jnp.zeros((chunk, 128), WIDE)
            for b in range(32):
                value = jnp.where(label == b, table_ref[b, h], value)
            strip_ref[h, first : first + chunk, :] = value


def make_strip(table_group, blocks):
    heads = table_group.shape[1]
    return pl.pallas_call(
        functools.partial(strip_kernel, blocks),
        out_shape=jax.ShapeDtypeStruct((heads, 2 * 64 * blocks, 128), WIDE),
        in_specs=[pl.BlockSpec(memory_space=pltpu.SMEM)],
        out_specs=pl.BlockSpec(memory_space=pltpu.VMEM),
        compiler_params=pltpu.CompilerParams(vmem_limit_bytes=VMEM_LIMIT),
        name="bias_strip",
    )(table_group)


def split_heads(wide, second_upper):
    lane = lax.broadcasted_iota(jnp.int32, (wide.shape[0], 128), 1)
    low = lane < 64
    zero = jnp.zeros((wide.shape[0], 128), wide.dtype)
    first, second = wide[:, :128], wide[:, 128:]
    third = jnp.where(low, zero, second) if second_upper else jnp.where(low, second, zero)
    return [jnp.where(low, first, zero), jnp.where(low, zero, first), third]


KEY_COLS = (0, 0, 128)
VALUE_COLS = (256, 256, 128)


def sort_blocks(count, m, kplace_ref, kv_refs, sorted_ref):
    for j in range(count):
        for e in range(GROUPS):
            to = pl.multiple_of(kplace_ref[m, j, e] * 64, 64)
            sorted_ref[pl.ds(to, 64), :] = kv_refs[j][e, 0]


def rows_sum(value):
    return jnp.sum(value.reshape(value.shape[0] // 8, 8, value.shape[1]), axis=0)


CHUNK = 128


def chunk_scores(strip_ref, sorted_ref, query, h, start, offs, low):
    scores = dot_t(sorted_ref[start : start + CHUNK, KEY_COLS[h] : KEY_COLS[h] + 128], query)
    parts = []
    for half in range(2):
        a = strip_ref[h, pl.ds(offs[2 * half] + start, CHUNK), :]
        b = strip_ref[h, pl.ds(offs[2 * half + 1] + start, CHUNK), :]
        parts.append(scores[:, half * 128 : half * 128 + 128] + jnp.where(low, a, b))
    return jnp.concatenate(parts, axis=1)


def forward_kernel(count, blocks, qplace_ref, kplace_ref, strip_ref, q_ref, *refs):
    kv_refs = refs[:count]
    o_refs = refs[count : count + GROUPS]
    lse_ref, sorted_ref, score_ref, weight_ref = refs[count + GROUPS :]
    m = pl.program_id(0)
    rows = 64 * blocks
    sort_blocks(count, m, kplace_ref, kv_refs, sorted_ref)
    offs = [pl.multiple_of((blocks - 1 - qplace_ref[m, e]) * 64, 64) for e in range(GROUPS)]
    queries = split_heads(q_ref[:, 0].reshape(GROUPS * 64, 256), False)
    low = lax.broadcasted_iota(jnp.int32, (CHUNK, 128), 1) < 64
    mixed = []
    for h in range(3):
        top = jnp.full((8, GROUPS * 64), -jnp.inf, WIDE)
        for start in range(0, rows, CHUNK):
            s = chunk_scores(strip_ref, sorted_ref, queries[h], h, start, offs, low)
            score_ref[start : start + CHUNK, :] = s
            top = jnp.maximum(top, jnp.max(s.reshape(CHUNK // 8, 8, GROUPS * 64), axis=0))
        top = jnp.max(top, axis=0, keepdims=True)
        total = jnp.zeros((8, GROUPS * 64), WIDE)
        for start in range(0, rows, CHUNK):
            e = jnp.exp(score_ref[start : start + CHUNK, :] - top)
            score_ref[start : start + CHUNK, :] = e
            total = total + rows_sum(e)
        total = jnp.sum(total, axis=0, keepdims=True)
        lse_ref[0, h : h + 1, :] = top + jnp.log(total)
        scale = 1.0 / total
        for start in range(0, rows, CHUNK):
            weight_ref[start : start + CHUNK, :] = (score_ref[start : start + CHUNK, :] * scale).astype(LOW)
        mixed.append(t_dot(sorted_ref[:, VALUE_COLS[h] : VALUE_COLS[h] + 128], weight_ref[...]))
    sub = lax.broadcasted_iota(jnp.int32, (128, GROUPS * 64), 0) < 64
    first = jnp.where(sub, mixed[0], mixed[1]).T
    second = jnp.where(sub, 0.0, mixed[2]).T
    out = jnp.concatenate([first, second], axis=1).astype(LOW)
    for d in range(GROUPS):
        o_refs[d][0] = out[d * 64 : d * 64 + 64]


def attention_forward(places, strip, q, kv_slots, blocks):
    qplace, kplace = places
    count = len(kv_slots)
    micro = q.shape[1]
    rows = 64 * blocks
    kv_cols = kv_slots[0].shape[-1]
    by_micro = lambda width: pl.BlockSpec((GROUPS, 1, 64, width), lambda m, *_: (0, m, 0, 0))
    results = pl.pallas_call(
        functools.partial(forward_kernel, count, blocks),
        out_shape=(jax.ShapeDtypeStruct((micro, 64, 256), LOW),) * GROUPS
        + (jax.ShapeDtypeStruct((micro, 3, GROUPS * 64), WIDE),),
        grid_spec=pltpu.PrefetchScalarGridSpec(
            num_scalar_prefetch=2,
            grid=(micro,),
            in_specs=[pl.BlockSpec(strip.shape, lambda m, *_: (0, 0, 0)), by_micro(256)] + [by_micro(kv_cols)] * count,
            out_specs=(pl.BlockSpec((1, 64, 256), lambda m, *_: (m, 0, 0)),) * GROUPS
            + (pl.BlockSpec((1, 3, GROUPS * 64), lambda m, *_: (m, 0, 0)),),
            scratch_shapes=[
                pltpu.VMEM((rows, kv_cols), LOW),
                pltpu.VMEM((rows, GROUPS * 64), WIDE),
                pltpu.VMEM((rows, GROUPS * 64), LOW),
            ],
        ),
        compiler_params=pltpu.CompilerParams(vmem_limit_bytes=VMEM_LIMIT),
        cost_estimate=pl.CostEstimate(
            flops=micro * 3 * 2 * 2 * rows * GROUPS * 64 * 128 * 2,
            bytes_accessed=micro * rows * kv_cols * 4,
            transcendentals=micro * 3 * rows * GROUPS * 64,
        ),
        name="attention_forward",
    )(qplace, kplace, strip, q, *kv_slots)
    return list(results[:GROUPS]), results[GROUPS]


def backward_kernel(count, blocks, qplace_ref, kplace_ref, place_ref, strip_ref, q_ref, lse_ref, *refs):
    do_refs, refs = refs[:GROUPS], refs[GROUPS:]
    kv_refs = refs[:count]
    dq_ref = refs[count]
    own_ref, even_ref, odd_ref, table_ref = refs[count + 1 : count + 5]
    sorted_ref, grad_ref, p_ref, dp_ref, soft_ref, ds_ref, wide_ref, near_ref, far_ref = refs[count + 5 :]
    m = pl.program_id(0)
    rows = 64 * blocks
    queue = GROUPS * 64
    near = near_ref.shape[1]
    lead = 128

    @pl.when(m == 0)
    def _():
        near_ref[...] = jnp.zeros_like(near_ref)
        far_ref[...] = jnp.zeros_like(far_ref)
        wide_ref[:lead, :] = jnp.zeros((lead, queue), WIDE)
        wide_ref[lead + rows :, :] = jnp.zeros((wide_ref.shape[0] - lead - rows, queue), WIDE)

    sort_blocks(count, m, kplace_ref, kv_refs, sorted_ref)
    offs = [pl.multiple_of((blocks - 1 - qplace_ref[m, e]) * 64, 64) for e in range(GROUPS)]
    queries = split_heads(q_ref[:, 0].reshape(queue, 256), False)
    grads = split_heads(jnp.concatenate([r[0] for r in do_refs], axis=0), True)
    low = lax.broadcasted_iota(jnp.int32, (CHUNK, 128), 1) < 64
    lane_block = lax.broadcasted_iota(jnp.int32, (8, queue), 1) // 64
    own_place = jnp.zeros((8, queue), jnp.int32)
    for e in range(GROUPS):
        own_place = jnp.where(lane_block == e, qplace_ref[m, e], own_place)
    near_low = lax.broadcasted_iota(jnp.int32, (near, 128), 1) < 64
    query_grads = []
    for h in range(3):
        delta = jnp.zeros((8, queue), WIDE)
        lse = lse_ref[0, h : h + 1, :]
        for start in range(0, rows, CHUNK):
            at = slice(start, start + CHUNK)
            p = jnp.exp(chunk_scores(strip_ref, sorted_ref, queries[h], h, start, offs, low) - lse)
            dp = dot_t(sorted_ref[at, VALUE_COLS[h] : VALUE_COLS[h] + 128], grads[h])
            p_ref[at, :] = p
            dp_ref[at, :] = dp
            soft_ref[h, at, :] = p.astype(LOW)
            delta = delta + rows_sum(p * dp)
        delta = jnp.sum(delta, axis=0, keepdims=True)
        before = jnp.zeros((8, queue), WIDE)
        after = jnp.zeros((8, queue), WIDE)
        for start in range(0, rows, CHUNK):
            at = slice(start, start + CHUNK)
            ds = (p_ref[at, :] * (dp_ref[at, :] - delta)).astype(LOW)
            ds_ref[h, at, :] = ds
            wide = ds.astype(WIDE)
            wide_ref[lead + start : lead + start + CHUNK, :] = wide
            for k in range(CHUNK // 64):
                block = start // 64 + k
                part = rows_sum(wide[k * 64 : k * 64 + 64])
                before = before + jnp.where(own_place >= block + 3, part, 0.0)
                after = after + jnp.where(own_place <= block - 3, part, 0.0)
        far_ref[h, 0] += before
        far_ref[h, 1] += after
        for half in range(2):
            cols = slice(half * 128, half * 128 + 128)
            a = wide_ref[pl.ds(pl.multiple_of(qplace_ref[m, 2 * half] * 64, 64), near), cols]
            b = wide_ref[pl.ds(pl.multiple_of(qplace_ref[m, 2 * half + 1] * 64, 64), near), cols]
            near_ref[h] += jnp.where(near_low, a, b)
        query_grads.append(t_dot(sorted_ref[:, KEY_COLS[h] : KEY_COLS[h] + 128], ds_ref[h]))
    sub = lax.broadcasted_iota(jnp.int32, (128, queue), 0) < 64
    first = jnp.where(sub, query_grads[0], query_grads[1]).T
    second = jnp.where(sub, query_grads[2], 0.0).T
    dq_ref[:, 0] = jnp.concatenate([first, second], axis=1).astype(LOW).reshape(GROUPS, 64, 256)
    grad_ref[:, 0:128] = dot(ds_ref[0], queries[0]) + dot(ds_ref[1], queries[1])
    grad_ref[:, 128:256] = dot(ds_ref[2], queries[2]) + dot(soft_ref[2], grads[2])
    grad_ref[:, 256:384] = dot(soft_ref[0], grads[0]) + dot(soft_ref[1], grads[1])
    for j in range(count):
        for e in range(GROUPS):
            at = pl.multiple_of(kplace_ref[m, j, e] * 64, 64)
            value = grad_ref[pl.ds(at, 64), :]
            if j == 0:
                own_ref[e, 0] = value
            elif j % 2:
                odd_ref[j // 2, e, 0] = value.astype(LOW)
            else:
                even_ref[j // 2 - 1, e, 0] = value.astype(LOW)

    @pl.when(m == pl.num_programs(0) - 1)
    def _():
        sums_row = lax.broadcasted_iota(jnp.int32, (32, 128), 0)
        lanes = lax.broadcasted_iota(jnp.int32, (32, 128), 1)
        side = lax.broadcasted_iota(jnp.int32, (near, 128), 1)
        rel = lax.broadcasted_iota(jnp.int32, (near, 128), 0) - lead - jnp.where(side >= 64, side - 64, side)
        label = bucket_of(rel)
        table = jnp.zeros((32, 128), WIDE)
        for h in range(3):
            far = [jnp.sum(far_ref[h, k][:, :128] + far_ref[h, k][:, 128:], axis=0, keepdims=True) for k in range(2)]
            result = jnp.where(sums_row == 15, far[0], jnp.where(sums_row == 31, far[1], 0.0))
            window = near_ref[h]
            for b in range(32):
                part = jnp.sum(jnp.where(label == b, window, 0.0), axis=0, keepdims=True)
                result = result + jnp.where(sums_row == b, part, 0.0)
            total = jnp.sum(result, axis=1, keepdims=True)
            table = jnp.where(lanes == place_ref[0] * 3 + h, total, table)
        table_ref[...] = table


def attention_backward(places, place, strip, q, kv_slots, do_slots, lse, blocks):
    qplace, kplace = places
    count = len(kv_slots)
    micro = q.shape[1]
    rows = 64 * blocks
    kv_cols = kv_slots[0].shape[-1]
    by_micro = lambda width: pl.BlockSpec((GROUPS, 1, 64, width), lambda m, *_: (0, m, 0, 0))
    kv_shape = kv_slots[0].shape
    by_part = lambda n: pl.BlockSpec((n, GROUPS, 1, 64, kv_cols), lambda m, *_: (0, 0, m, 0, 0))
    results = pl.pallas_call(
        functools.partial(backward_kernel, count, blocks),
        out_shape=(jax.ShapeDtypeStruct(q.shape, LOW),)
        + (
            jax.ShapeDtypeStruct(kv_shape, WIDE),
            jax.ShapeDtypeStruct((count // 2 - 1,) + kv_shape, LOW),
            jax.ShapeDtypeStruct((count // 2,) + kv_shape, LOW),
        )
        + (jax.ShapeDtypeStruct((32, 128), WIDE),),
        grid_spec=pltpu.PrefetchScalarGridSpec(
            num_scalar_prefetch=3,
            grid=(micro,),
            in_specs=[
                pl.BlockSpec(strip.shape, lambda m, *_: (0, 0, 0)),
                by_micro(256),
                pl.BlockSpec((1, 3, GROUPS * 64), lambda m, *_: (m, 0, 0)),
            ]
            + [pl.BlockSpec((1, 64, 256), lambda m, *_: (m, 0, 0))] * GROUPS
            + [by_micro(kv_cols)] * count,
            out_specs=(by_micro(256),)
            + (by_micro(kv_cols), by_part(count // 2 - 1), by_part(count // 2))
            + (pl.BlockSpec((32, 128), lambda m, *_: (0, 0)),),
            scratch_shapes=[
                pltpu.VMEM((rows, kv_cols), LOW),
                pltpu.VMEM((rows, kv_cols), WIDE),
                pltpu.VMEM((rows, GROUPS * 64), WIDE),
                pltpu.VMEM((rows, GROUPS * 64), WIDE),
                pltpu.VMEM((3, rows, GROUPS * 64), LOW),
                pltpu.VMEM((3, rows, GROUPS * 64), LOW),
                pltpu.VMEM((rows + 256, GROUPS * 64), WIDE),
                pltpu.VMEM((3, 320, 128), WIDE),
                pltpu.VMEM((3, 2, 8, GROUPS * 64), WIDE),
            ],
        ),
        compiler_params=pltpu.CompilerParams(vmem_limit_bytes=VMEM_LIMIT),
        cost_estimate=pl.CostEstimate(
            flops=micro * 3 * 5 * 2 * rows * GROUPS * 64 * 128 * 2,
            bytes_accessed=micro * rows * kv_cols * 8,
            transcendentals=micro * 3 * rows * GROUPS * 64,
        ),
        name="attention_backward",
    )(qplace, kplace, place, strip, q, lse, *do_slots, *kv_slots)
    return results[0], results[1:4], results[4]


PLACE = pl.BlockSpec(memory_space=pltpu.SMEM)


def whole(count):
    return [pl.BlockSpec(memory_space=pltpu.VMEM)] * count


def first_entry(v):
    return pl.BlockSpec((1,) + v.shape[1:], lambda _: (0,) * v.ndim)


def call(kernel, name, place, operands, out_shape, scratch=(), flops=0):
    operands = [v if isinstance(v, tuple) else (v, False) for v in operands]
    grid = {"grid": (1,)} if any(first for _, first in operands) else {}
    specs = [PLACE] + [first_entry(v) if first else whole(1)[0] for v, first in operands]
    operands = [v for v, _ in operands]
    size = sum(v.size * v.dtype.itemsize for v in operands) + sum(
        v.size * jnp.dtype(v.dtype).itemsize for v in out_shape
    )
    return pl.pallas_call(
        kernel,
        out_shape=tuple(out_shape),
        **grid,
        in_specs=specs,
        out_specs=tuple(whole(len(out_shape))),
        scratch_shapes=list(scratch),
        compiler_params=pltpu.CompilerParams(vmem_limit_bytes=VMEM_LIMIT),
        cost_estimate=pl.CostEstimate(flops=flops, bytes_accessed=size, transcendentals=0),
        name=name,
    )(place, *operands)


def shaped(*shape, dtype=LOW):
    return jax.ShapeDtypeStruct(shape, dtype)


def place_rows(full_ref, slot_refs, index):
    rows = slot_refs[0].shape[0]
    for j, ref in enumerate(slot_refs):
        full_ref[pl.ds(pl.multiple_of((index ^ j) * rows, rows), rows), :] = ref[...]


def rms_scale(values):
    return lax.rsqrt(jnp.mean(values * values, axis=-1, keepdims=True) + EPSILON)


def norm_back(grad_normed, normed, scale):
    return scale * (grad_normed - normed * jnp.mean(grad_normed * normed, axis=-1, keepdims=True))


def project_kernel(parts_f, place_ref, gain_ref, *refs):
    x_refs, w_refs = refs[:GROUPS], refs[GROUPS : GROUPS + parts_f]
    act_ref, q_ref, kv_ref, full_ref = refs[GROUPS + parts_f :]
    place_rows(full_ref, w_refs, place_ref[2])
    micro, rows, width = x_refs[0].shape
    for d in range(GROUPS):
        x = x_refs[d][...].reshape(micro * rows, width).astype(WIDE)
        act_ref[d] = (x * rms_scale(x) * gain_ref[...]).astype(LOW)
    both = dot(act_ref[...].reshape(GROUPS * micro * rows, width), full_ref[...]).astype(LOW)
    q_ref[...] = both[:, :256].reshape(GROUPS, micro, rows, 256)
    kv_ref[...] = both[:, 256:].reshape(GROUPS, micro, rows, 384)


def project(place, gain, x_slots, w_slots):
    micro, rows, width = x_slots[0].shape
    return call(
        functools.partial(project_kernel, len(w_slots)),
        "project",
        place,
        [gain, *x_slots, *w_slots],
        [
            shaped(GROUPS, micro * rows, width),
            shaped(GROUPS, micro, rows, 256),
            shaped(GROUPS, micro, rows, 384),
        ],
        [pltpu.VMEM((width, 640), LOW)],
        flops=2 * GROUPS * micro * rows * width * 640,
    )


def group_rows(place_ref, d):
    return lax.rem(place_ref[0] + d, GROUPS) * 192


def arrange_kernel(parts_f, place_ref, *refs):
    w_refs, (out_ref, full_ref) = refs[:parts_f], refs[parts_f:]
    place_rows(full_ref, w_refs, place_ref[2])
    for d in range(GROUPS):
        at = group_rows(place_ref, d)
        out_ref[d * 256 : d * 256 + 128, :] = full_ref[pl.ds(pl.multiple_of(at, 64), 128), :]
        out_ref[d * 256 + 128 : d * 256 + 256, :] = full_ref[pl.ds(pl.multiple_of(at + 64, 64), 128), :]


def arrange(place, w_slots):
    width = w_slots[0].shape[1]
    return call(
        functools.partial(arrange_kernel, len(w_slots)),
        "arrange",
        place,
        w_slots,
        [shaped(GROUPS * 256, width)],
        [pltpu.VMEM((width, width), LOW)],
    )[0]


def joined_kernel(place_ref, gain_ref, x_ref, w_ref, *refs):
    o_refs, (resid_ref, act_ref) = refs[:GROUPS], refs[GROUPS:]
    micro, rows, width = x_ref.shape
    o = jnp.concatenate([r[...].reshape(micro * rows, 256) for r in o_refs], axis=1)
    total = x_ref[...].reshape(micro * rows, width).astype(WIDE) + dot(o, w_ref[...])
    resid_ref[...] = total
    act_ref[...] = (total * rms_scale(total) * gain_ref[...]).astype(LOW)


def joined(place, gain, x, o_slots, w_rel):
    micro, rows, width = x.shape
    return call(
        joined_kernel,
        "joined",
        place,
        [gain, x, w_rel, *o_slots],
        [shaped(micro * rows, width, dtype=WIDE), shaped(micro * rows, width)],
        flops=2 * micro * rows * width * 1024,
    )


GELU_A = 0.7978845608028654
GELU_B = 0.044715


def put_part(refs, j, value):
    own_ref, even_ref, odd_ref = refs
    if j == 0:
        own_ref[...] = value
    elif j % 2:
        odd_ref[j // 2] = value.astype(odd_ref.dtype)
    else:
        even_ref[j // 2 - 1] = value.astype(even_ref.dtype)


def part_shapes(shape, fast):
    return [
        shaped(*shape, dtype=WIDE),
        shaped(fast // 2 - 1, *shape),
        shaped(fast // 2, *shape),
    ]


def feed_kernel(parts_f, fast, place_ref, *refs):
    act_refs, refs = refs[:fast], refs[fast:]
    g_refs, refs = refs[:fast], refs[fast:]
    pair_refs, refs = refs[:parts_f], refs[parts_f:]
    down_refs, refs = refs[:parts_f], refs[parts_f:]
    two_refs, out_refs, refs = refs[:3], refs[3:6], refs[6:]
    hid_ref, grad_ref, pair_ref, down_ref = refs
    place_rows(pair_ref, pair_refs, place_ref[2])
    place_rows(down_ref, down_refs, place_ref[2])
    cols = hid_ref.shape[-1]
    rows = act_refs[0].shape[0]
    act = jnp.concatenate([r[...] for r in act_refs], axis=0)
    g = jnp.concatenate([r[...] for r in g_refs], axis=0)
    both = dot(act, pair_ref[...])
    dh = dot_t(g, down_ref[...])
    for j in range(fast):
        at = slice(j * rows, j * rows + rows)
        z, up = both[at, :cols], both[at, cols:]
        square = z * z
        t = jnp.tanh(GELU_A * (z + GELU_B * square * z))
        half = 0.5 * (1.0 + t)
        gelu = z * half
        slope = half + (0.5 * z) * (1.0 - t * t) * (GELU_A * (1.0 + 3.0 * GELU_B * square))
        hid_ref[j] = (gelu * up).astype(LOW)
        grad_ref[j, :, :cols] = (dh[at] * up * slope).astype(LOW)
        grad_ref[j, :, cols:] = (dh[at] * gelu).astype(LOW)
    two = dot_t(grad_ref[...].reshape(fast * rows, 2 * cols), pair_ref[...])
    out = dot(hid_ref[...].reshape(fast * rows, cols), down_ref[...])
    for j in range(fast):
        put_part(two_refs, j, two[j * rows : j * rows + rows])
        put_part(out_refs, j, out[j * rows : j * rows + rows])


def feed(place, act_slots, g_slots, pair_slots, down_slots):
    fast, parts_f = len(act_slots), len(pair_slots)
    rows, width = act_slots[0].shape
    cols = down_slots[0].shape[0] * parts_f
    results = call(
        functools.partial(feed_kernel, parts_f, fast),
        "feed",
        place,
        [*act_slots, *g_slots, *pair_slots, *down_slots],
        part_shapes((rows, width), fast) * 2 + [shaped(fast, rows, cols), shaped(fast, rows, 2 * cols)],
        [pltpu.VMEM((width, 2 * cols), LOW), pltpu.VMEM((cols, width), LOW)],
        flops=2 * fast * rows * width * cols * 6,
    )
    return results[:3], results[3:6], results[-2], results[-1]


def packing(piece, rows):
    if rows == 3 * piece:
        return [(0, k * 256, k * piece, 0, piece, 256) for k in range(3)]
    half = piece // 2
    return [
        (0, 0, 0, 0, piece, 512),
        (0, 512, piece, 0, half, 256),
        (half, 512, piece, 256, half, 256),
    ]


def pair_grads_kernel(fast, place_ref, *refs):
    act_refs, grad_ref, refs = refs[:fast], refs[fast], refs[fast + 1 :]
    outs, full_ref = refs[:-1], refs[-1]
    act = jnp.concatenate([r[...] for r in act_refs], axis=0)
    full_ref[...] = t_dot(act, grad_ref[...].reshape(act.shape[0], -1))
    rows = outs[0].shape[0]
    for j, out in enumerate(outs):
        at = pl.multiple_of((place_ref[2] ^ j) * rows, rows)
        out[...] = full_ref[pl.ds(at, rows), :].astype(out.dtype)


def pair_grads(place, act_slots, grads, parts_f):
    fast, rows, double = grads.shape
    width = act_slots[0].shape[1]
    types = [WIDE] + [LOW] * (parts_f - 1)
    return call(
        functools.partial(pair_grads_kernel, fast),
        "pair_grads",
        place,
        [*act_slots, grads],
        [shaped(width // parts_f, double, dtype=t) for t in types],
        [pltpu.VMEM((width, double), WIDE)],
        flops=2 * fast * rows * width * double,
    )


def down_grads_kernel(fast, place_ref, *refs):
    g_refs, hid_ref, refs = refs[:fast], refs[fast], refs[fast + 1 :]
    outs, full_ref = refs[:-1], refs[-1]
    g = jnp.concatenate([r[...] for r in g_refs], axis=0)
    full_ref[...] = t_dot(hid_ref[...].reshape(g.shape[0], -1), g)
    rows = outs[0].shape[0]
    piece = full_ref.shape[0] // len(outs)
    for j, out in enumerate(outs):
        for r, c, to_r, to_c, n, w in packing(piece, rows):
            at = pl.multiple_of((place_ref[2] ^ j) * piece + r, 8)
            out[to_r : to_r + n, to_c : to_c + w] = full_ref[pl.ds(at, n), c : c + w].astype(out.dtype)


def down_grads(place, g_slots, hid, parts_f):
    fast, rows, cols = hid.shape
    width = g_slots[0].shape[1]
    types = [WIDE] + [LOW] * (parts_f - 1)
    return call(
        functools.partial(down_grads_kernel, fast),
        "down_grads",
        place,
        [*g_slots, hid],
        [shaped(width // parts_f, cols, dtype=t) for t in types],
        [pltpu.VMEM((cols, width), WIDE)],
        flops=2 * fast * rows * width * cols,
    )


def group_split_kernel(count, place_ref, *refs):
    own_ref, send_refs = refs[count], refs[count + 1 :]
    rows = own_ref.shape[0]

    def part(d):
        at = pl.ds(pl.multiple_of(lax.rem(place_ref[0] + d, GROUPS) * rows, 8), rows)
        return sum(r[at, :].astype(WIDE) for r in refs[:count])

    own_ref[...] = part(0)
    for d, ref in enumerate(send_refs, 1):
        ref[...] = part(d).astype(ref.dtype)


def group_split(place, parts):
    rows, cols = parts[0].shape
    cut = rows // GROUPS
    results = call(
        functools.partial(group_split_kernel, len(parts)),
        "group_split",
        place,
        parts,
        [shaped(cut, cols, dtype=WIDE)] + [shaped(cut, cols)] * (GROUPS - 1),
    )
    return results[0], list(results[1:])


def group_halves_kernel(count, place_ref, *refs):
    keep_ref, send_ref = refs[count:]
    rows = keep_ref.shape[1]
    for d in range(GROUPS):
        at = pl.ds(pl.multiple_of((place_ref[0] ^ d) * rows, 8), rows)
        total = sum(r[at, :].astype(WIDE) for r in refs[:count])
        if d % 2:
            send_ref[d // 2] = total.astype(send_ref.dtype)
        else:
            keep_ref[d // 2] = total


def group_halves(place, parts):
    rows, cols = parts[0].shape
    cut = (GROUPS // 2, rows // GROUPS, cols)
    return call(
        functools.partial(group_halves_kernel, len(parts)),
        "group_halves",
        place,
        parts,
        [shaped(*cut, dtype=WIDE), shaped(*cut)],
    )


def summed(refs):
    return sum((r[0] if len(r.shape) == 3 else r[...]).astype(WIDE) for r in refs)


def branch_kernel(count, place_ref, gain_ref, resid_ref, g_ref, w_ref, *refs):
    two_refs, refs = refs[:count], refs[count:]
    grad_ref, low_ref, gain_out = refs[:3]
    do_refs = refs[3:]
    micro, rows, _ = do_refs[0].shape
    grad_two = summed(two_refs)
    resid = resid_ref[...]
    scale = rms_scale(resid)
    normed = resid * scale
    gain_out[...] = jnp.sum(grad_two * normed, axis=0, keepdims=True)
    grad = g_ref[...].astype(WIDE) + norm_back(grad_two * gain_ref[...], normed, scale)
    grad_ref[...] = grad
    low = grad.astype(LOW)
    low_ref[...] = low
    both = dot_t(low, w_ref[...]).astype(LOW)
    for d in range(GROUPS):
        do_refs[d][...] = both[:, d * 256 : d * 256 + 256].reshape(micro, rows, 256)


def branch(place, gain, resid, g, two_list, w_rel, micro):
    rows, width = resid.shape
    results = call(
        functools.partial(branch_kernel, len(two_list)),
        "branch",
        place,
        [gain, resid, g, w_rel, *two_list],
        [shaped(rows, width, dtype=WIDE), shaped(rows, width), shaped(1, width, dtype=WIDE)]
        + [shaped(micro, rows // micro, 256)] * GROUPS,
        flops=2 * rows * width * 1024,
    )
    return results[0], results[1], results[2], list(results[3:])


def with_rows(index, rows, count, action):
    if rows % 8 == 0:
        action(pl.ds(pl.multiple_of(index * rows, 8), rows))
        return
    for known in range(count):

        @pl.when(index == known)
        def _():
            action(slice(known * rows, known * rows + rows))


def write_chunks(place_ref, full_ref, keep_ref, send_ref):
    parts_f, halves, rows, _ = keep_ref.shape
    for i in range(parts_f):
        for k in range(halves):
            for odd, ref in ((0, keep_ref), (1, send_ref)):
                index = (place_ref[2] ^ i) * (2 * halves) + (place_ref[1] ^ (2 * k + odd))

                def copy(at):
                    ref[i, k] = full_ref[at, :].astype(ref.dtype)

                with_rows(index, rows, 2 * halves * parts_f, copy)


def out_grads_kernel(place_ref, low_ref, *refs):
    o_refs = refs[:GROUPS]
    keep_ref, send_ref, full_ref = refs[GROUPS:]
    micro, rows, _ = o_refs[0].shape
    low = low_ref[...]
    for d in range(GROUPS):
        both = t_dot(o_refs[d][...].reshape(micro * rows, 256), low)
        at = group_rows(place_ref, d)
        full_ref[pl.ds(pl.multiple_of(at, 64), 128), :] = both[:128]
        full_ref[pl.ds(pl.multiple_of(at + 128, 64), 64), :] = both[192:]
    write_chunks(place_ref, full_ref, keep_ref, send_ref)


def out_grads(place, low, o_slots, parts_f, fast):
    rows, width = low.shape
    chunk = (parts_f, fast // 2, width // (parts_f * fast), width)
    return call(
        out_grads_kernel,
        "out_grads",
        place,
        [low, *o_slots],
        [shaped(*chunk, dtype=WIDE), shaped(*chunk)],
        [pltpu.VMEM((width, width), WIDE)],
        flops=2 * rows * width * 1024,
    )


def input_grads_kernel(parts_f, count, place_ref, act_ref, dq_ref, *refs):
    x_refs, refs = refs[:GROUPS], refs[GROUPS:]
    dkv_refs, refs = refs[:count], refs[count:]
    w_refs, refs = refs[:parts_f], refs[parts_f:]
    one_keep, one_send, gain_out, keep_ref, send_ref, full_ref, sums_ref, both_ref, one_ref = refs
    place_rows(full_ref, w_refs, place_ref[2])
    groups, rows, width = act_ref.shape
    micro = dq_ref.shape[1]
    gain_total = jnp.zeros((1, width), WIDE)
    for d in range(GROUPS):
        dkv = sum((r[0, d] if len(r.shape) == 5 else r[d]).astype(WIDE) for r in dkv_refs)
        dkv = dkv.astype(LOW).reshape(rows, 384)
        both = jnp.concatenate([dq_ref[d].reshape(rows, 256), dkv], axis=1)
        both_ref[d] = both
        one = dot_t(both, full_ref[...])
        x = x_refs[d][...].reshape(rows, width).astype(WIDE)
        gain_total = gain_total + jnp.sum(one * (x * rms_scale(x)), axis=0, keepdims=True)
        one_ref[lax.rem(place_ref[0] + GROUPS - d, GROUPS)] = one
    for d in range(GROUPS):
        value = one_ref[place_ref[0] ^ d]
        if d % 2:
            one_send[d // 2] = value.astype(LOW)
        else:
            one_keep[d // 2] = value
    gain_out[...] = gain_total
    sums_ref[...] = t_dot(act_ref[...].reshape(groups * rows, width), both_ref[...].reshape(groups * rows, 640))
    write_chunks(place_ref, sums_ref, keep_ref, send_ref)


def input_grads(place, act, dq, x_slots, dkv_list, w_slots, fast):
    groups, rows, width = act.shape
    micro = dq.shape[1]
    parts_f = len(w_slots)
    chunk = (parts_f, fast // 2, width // (parts_f * fast), 640)
    return call(
        functools.partial(input_grads_kernel, parts_f, len(dkv_list)),
        "input_grads",
        place,
        [act, dq, *x_slots, *dkv_list, *w_slots],
        [shaped(GROUPS // 2, rows, width, dtype=WIDE), shaped(GROUPS // 2, rows, width)]
        + [shaped(1, width, dtype=WIDE), shaped(*chunk, dtype=WIDE), shaped(*chunk)],
        [
            pltpu.VMEM((width, 640), LOW),
            pltpu.VMEM((width, 640), WIDE),
            pltpu.VMEM((groups, rows, 640), LOW),
            pltpu.VMEM((groups, rows, width), WIDE),
        ],
        flops=4 * groups * rows * width * 640,
    )


def last_kernel(place_ref, gain_ref, x_ref, grad_ref, one_ref, got_ref, x_grad_ref):
    micro, rows, width = x_ref.shape
    grad_one = one_ref[...] + got_ref[: micro * rows, :].astype(WIDE)
    x = x_ref[...].reshape(micro * rows, width).astype(WIDE)
    scale = rms_scale(x)
    x_grad_ref[...] = grad_ref[...] + norm_back(grad_one * gain_ref[...], x * scale, scale)


def last(place, gain, x, grad, one, one_got):
    return call(
        last_kernel, "last", place, [gain, x, grad, one, one_got], [shaped(*grad.shape, dtype=WIDE)]
    )[0]


def pair_finish_kernel(parts_f, fast, place_ref, *refs):
    pair_refs, (gate_ref, up_ref) = refs[:fast], refs[fast:]
    _, rows, double = pair_refs[0].shape
    cols = double // 2
    piece = cols // parts_f
    for j in range(fast):
        other = place_ref[1] ^ j
        for d in range(GROUPS):
            at = pl.ds(pl.multiple_of(lax.rem(place_ref[0] + GROUPS - d, GROUPS) * rows, 8), rows)
            for start, ref in ((0, gate_ref), (cols, up_ref)):
                for k in range(parts_f):
                    value = pair_refs[j][d, :, start + k * piece : start + (k + 1) * piece].astype(WIDE)
                    if piece % 128 == 0:
                        to = pl.multiple_of(k * fast * piece + other * piece, 128)
                        ref[at, pl.ds(to, piece)] = value
                    else:
                        for l in range(fast):

                            @pl.when(other == l)
                            def _():
                                ref[at, (k * fast + l) * piece : (k * fast + l + 1) * piece] = value


def low_finish_kernel(parts_f, fast, place_ref, *refs):
    low_refs, (down_ref, pack_ref) = refs[:fast], refs[fast:]
    _, rows, cols = low_refs[0].shape
    piece = cols // parts_f
    for j in range(fast):
        for d in range(GROUPS):
            at = pl.ds(pl.multiple_of(lax.rem(place_ref[0] + GROUPS - d, GROUPS) * rows, 8), rows)
            pack_ref[at, :] = low_refs[j][d].astype(WIDE)
        for r, c, to_r, to_c, n, w in packing(piece, rows * GROUPS):
            at = pl.ds(pl.multiple_of((place_ref[1] ^ j) * piece + r, 8), n)
            down_ref[at, c : c + w] = pack_ref[to_r : to_r + n, to_c : to_c + w]


def low_finish(place, packs, parts_f):
    fast = len(packs)
    _, rows, cols = packs[0].shape
    return call(
        functools.partial(low_finish_kernel, parts_f, fast),
        "low_finish",
        place,
        packs,
        [shaped(cols // parts_f * fast, rows * GROUPS * parts_f, dtype=WIDE)],
        [pltpu.VMEM((rows * GROUPS, cols), WIDE)],
    )[0]


def input_finish_kernel(fast, place_ref, *refs):
    pack_refs = refs[:fast]
    query_ref, key_ref, value_ref, out_ref = refs[fast:]
    rows = pack_refs[0].shape[0]
    for j in range(fast):
        value = pack_refs[j][:, GROUPS * 640 :].astype(WIDE)

        def place_out(at):
            out_ref[at, :] = value

        with_rows(place_ref[1] ^ j, rows, fast, place_out)
    for h in range(GROUPS):

        @pl.when(place_ref[0] == h)
        def _():
            for j in range(fast):
                starts = [(h - g) % GROUPS * 640 for g in range(GROUPS)]
                part = lambda a, b: pack_refs[j][:, a:b].astype(WIDE)
                query = jnp.concatenate([part(s, s + 192) for s in starts], axis=1)
                key = jnp.concatenate([part(s + 256, s + 448) for s in starts], axis=1)
                value = jnp.concatenate([p for s in starts for p in (part(s + 512, s + 640), part(s + 448, s + 512))], axis=1)

                def place_in(at):
                    query_ref[at, :] = query
                    key_ref[at, :] = key
                    value_ref[at, :] = value

                with_rows(place_ref[1] ^ j, rows, fast, place_in)


def most_finish_kernel(parts_f, fast, place_ref, *refs):
    pair_refs, pack_refs, refs = refs[:fast], refs[fast : 2 * fast], refs[2 * fast :]
    pair_finish_kernel(parts_f, fast, place_ref, *pair_refs, *refs[-7:-5])
    input_finish_kernel(fast, place_ref, *pack_refs, *refs[-5:-1])
    resid_ref, out_refs, out_ref = refs[0], refs[1:-7], refs[-1]
    rows = resid_ref.shape[0]
    parts = [(r[0] if len(r.shape) == 3 else r[r.shape[0] - rows :, :]).astype(WIDE) for r in out_refs]
    out_ref[...] = (resid_ref[...] + sum(parts)).astype(LOW)


def most_finish(place, pair_packs, packs, resid, out_list, parts_f, width):
    fast = len(packs)
    _, rows, double = pair_packs[0].shape
    return call(
        functools.partial(most_finish_kernel, parts_f, fast),
        "most_finish",
        place,
        [*pair_packs, *packs, resid, *out_list],
        [shaped(rows * GROUPS, double // 2 * fast, dtype=WIDE)] * 2
        + [shaped(packs[0].shape[0] * fast, width, dtype=WIDE)] * 4
        + [shaped(*resid.shape)],
    )


def spread_groups(v):
    return [v] + [shift(v, d) for d in range(1, GROUPS)]


def gather_pack(pack, fast):
    slots = {0: pack}
    for bit in bits_down(fast):
        for j in list(slots):
            slots[j ^ bit] = hop(slots[j], "ctx", bit)
    return [slots[j] for j in range(fast)]


def after(value, *others):
    return lax.optimization_barrier((value, *others))[0]


def body(
    tokens,
    offsets,
    norm1_gain,
    norm2_gain,
    bias_table,
    w_query,
    w_key,
    w_value,
    w_out,
    w_gate,
    w_up,
    w_down,
    cotangent,
):
    micro, _, block_rows, width = tokens.shape
    blocks = lax.axis_size("ctx")
    parts_f = lax.axis_size("fsdp")
    fast = blocks // GROUPS
    ctx = lax.axis_index("ctx")
    f = lax.axis_index("fsdp")
    hi, lo = ctx // fast, ctx % fast
    group_cols = w_query.shape[1] // GROUPS
    own_rows = micro * block_rows
    hidden = w_gate.shape[1]
    piece = hidden // (parts_f * fast)
    part_rows = w_query.shape[0]
    gain_one = norm1_gain.reshape(1, width)
    gain_two = norm2_gain.reshape(1, width)
    place = jnp.stack([hi, lo, f]).astype(jnp.int32)

    own_x = tokens[:, 0]
    g_low = cotangent[:, 0].reshape(own_rows, width)
    x_slots = spread_groups(own_x)

    def group_of(matrix):
        return lax.dynamic_slice_in_dim(matrix, hi * group_cols, group_cols, axis=1)

    q_part, k_part, v_part = group_of(w_query), group_of(w_key), group_of(w_value)
    gap = jnp.zeros((part_rows, 64), LOW)
    qkv_part = jnp.concatenate([q_part, gap, k_part, v_part[:, 128:], v_part[:, :128]], axis=1)
    qkv_slots = slots_out(qkv_part, "fsdp", parts_f)

    def pieces(matrix):
        return [
            lax.dynamic_slice_in_dim(matrix, (k * fast + lo) * piece, piece, axis=1) for k in range(parts_f)
        ]

    pair_part = jnp.concatenate(pieces(w_gate) + pieces(w_up), axis=1)
    down_part = lax.dynamic_slice_in_dim(w_down, lo * piece, piece, axis=0)

    starts = offsets[:, 0]
    group_ids = (hi + GROUPS - jnp.arange(GROUPS, dtype=jnp.int32)) % GROUPS
    slot_ids = lo ^ jnp.arange(fast, dtype=jnp.int32)
    kplace = jnp.take(starts, group_ids[None, :] * fast + slot_ids[:, None], axis=1)
    table_group = lax.dynamic_slice_in_dim(bias_table, hi * 3, 3, axis=1)
    strip = make_strip(table_group, blocks)

    tick = [place]

    def fence(*values):
        tick[0], *values = lax.optimization_barrier((tick[0], *values))
        return values[0] if len(values) == 1 else values

    def shifted(parts, sign):
        return [shift(v, sign * d) for d, v in enumerate(parts, 1)]

    def to_f(parts):
        return [hop(v, "fsdp", j) for j, v in enumerate(parts, 1)]

    def groups_sum(own, parts):
        return (own + sum(v.astype(WIDE) for v in parts)).astype(LOW)

    def far_places(v):
        have = {0: v}
        for bit in bits_down(fast // 2):
            for j in list(have):
                have[j ^ (2 * bit)] = hop(have[j], "ctx", 2 * bit)
        return have

    def both_cores(have):
        return [v for j in range(0, fast, 2) for v in (have[j], hop(have[j], "ctx", 1))]

    strip, kplace = fence(strip, kplace)
    places = (kplace[:, 0], kplace)
    g_have = far_places(g_low)
    out_w, pair_w, x_slots, qkv_slots, g_have = fence(w_out, pair_part, x_slots, qkv_slots, g_have)
    act_one, q, kv = project(tick[0], gain_one, x_slots, qkv_slots)
    kv_slots = slots_out(kv, "ctx", fast)
    out_w_slots = slots_out(out_w, "fsdp", parts_f)
    g_slots = both_cores(g_have)
    g_low, kv_slots, out_w_slots, g_slots, pair_w = fence(g_low, kv_slots, out_w_slots, g_slots, pair_w)
    pair_slots = slots_out(pair_w, "fsdp", parts_f)
    o_group, lse = attention_forward(places, strip, q, kv_slots, blocks)
    o_group, down_w = fence(o_group, down_part)
    o_slots = [o_group[0]] + shifted(o_group[1:], -1)
    down_slots = slots_out(down_w, "fsdp", parts_f)
    w_rel = arrange(tick[0], out_w_slots)
    o_slots, w_rel = fence(o_slots, w_rel)
    resid, act_two = joined(tick[0], gain_two, own_x, o_slots, w_rel)
    act_two = fence(act_two)
    act_slots = slots_out(act_two, "ctx", fast)
    two_parts, out_parts, hid, grads = feed(tick[0], act_slots, g_slots, pair_slots, down_slots)
    two_parts, out_parts = fence(two_parts, out_parts)

    two_odd = two_parts[2]
    two_got = hop(two_odd, "ctx", 1)
    pair_keep, *pair_sends = pair_grads(tick[0], act_slots, grads, parts_f)
    out_got_one = hop(out_parts[2], "ctx", 1)
    two_got, pair_keep, pair_sends, out_got_one = fence(two_got, pair_keep, pair_sends, out_got_one)
    pair_got = to_f(pair_sends)
    two_list, sent = pairs_on(two_parts, two_got, fast)
    low_keep, *low_sends = down_grads(fence(tick[0], sent)[0], g_slots, hid, parts_f)
    got, low_keep, low_sends = fence([v for v, _ in two_list], low_keep, low_sends)
    two_list = [(v, first) for v, (_, first) in zip(got, two_list)]
    grad_resid, grad_low, gain_two_part, do_own = branch(
        tick[0], gain_two, resid, g_low, two_list, w_rel, micro
    )
    do_own = fence(*do_own)
    do_slots = [do_own[0]] + shifted(do_own[1:], 1)
    out_keep, out_send = out_grads(tick[0], grad_low, o_slots, parts_f, fast)
    out_keep, out_send, do_slots, pair_got = fence(out_keep, out_send, do_slots, pair_got)
    out_got = hop(out_send, "ctx", 1)
    pair_own, pair_sends = group_split(tick[0], [pair_keep, *pair_got])
    pair_own, pair_sends, low_sends, out_total = fence(
        pair_own, pair_sends, low_sends, out_keep + out_got.astype(WIDE)
    )

    pair_parts = shifted(pair_sends, 1)
    low_got = to_f(low_sends)
    out_total = halve(out_total, "fsdp", 1)
    dq, dkv_parts, table_part = attention_backward(
        places, tick[0], strip, q, kv_slots, do_slots, lse, blocks
    )
    dq, dkv_parts, pair_parts, low_got, out_total = fence(dq, dkv_parts, pair_parts, low_got, out_total)
    dkv_list, sent = pairs_on(dkv_parts, hop(dkv_parts[2], "ctx", 1), fast)
    low_keep, low_send = group_halves(tick[0], [low_keep, *low_got])
    pair_chunk, low_send, out_total, _ = fence(groups_sum(pair_own, pair_parts), low_send, out_total, sent)
    pair_spread = spread_groups(pair_chunk)
    if fast == 4:
        out_far = (out_parts[1][0].astype(WIDE) + out_got_one[1].astype(WIDE)).astype(LOW)
        far = jnp.concatenate([out_total[1].astype(LOW), out_far])
        far = hop(far, "ctx", 2)
    got = fence([v for v, _ in dkv_list])
    dkv_list = [(v, first) for v, (_, first) in zip(got, dkv_list)]
    one_keep, one_send, gain_one_part, in_keep, in_send = input_grads(
        tick[0], act_one, dq, x_slots, dkv_list, qkv_slots, fast
    )
    one_keep, one_send, in_keep, in_send, low_send, pair_spread = fence(
        one_keep, one_send, in_keep, in_send, low_send, pair_spread
    )
    if fast == 4:
        far = fence(far)
        chunk = out_total.shape[1]
        out_low = (out_total[0] + far[:chunk].astype(WIDE)).astype(LOW)
        out_list = [(out_parts[0], False), (out_got_one, True), (far, False)]
    else:
        out_low = halve(out_total, "ctx", 2).astype(LOW)
        out_list, _ = pairs_on(out_parts, out_got_one, fast)

    def send_small(v, small, bit):
        high = small.astype(LOW)
        rest = (small - high.astype(WIDE)).astype(LOW)
        return hop(jnp.concatenate([v, high, rest]), "ctx", bit), high.astype(WIDE) + rest.astype(WIDE)

    def take_small(got, own):
        lines = own.shape[0]
        count = got.shape[0] - 2 * lines
        return got[:count], own + got[count : count + lines].astype(WIDE) + got[count + lines :].astype(WIDE)

    def two_hops(a, b, bit):
        if a.shape[:-1] != b.shape[:-1]:
            return hop(a, "ctx", bit), hop(b, "ctx", bit)
        got = hop(jnp.concatenate([a, b], axis=-1), "ctx", bit)
        return got[..., : a.shape[-1]], got[..., a.shape[-1] :]

    head_count = bias_table.shape[1]
    table_row = table_part[:, :head_count].reshape(1, -1)
    table_row = jnp.pad(table_row, ((0, 5), (0, width - table_row.shape[1])))
    small = jnp.concatenate([gain_one_part, gain_two_part, table_row])
    in_got = hop(in_send, "ctx", 1)
    out_two = jnp.stack([out_low[:, : width // 2], out_low[:, width // 2 :]])
    low_got, out_got = two_hops(low_send, out_two, fast)
    pair_have = far_places(jnp.stack(pair_spread))
    one_got, small = send_small(one_send.reshape(-1, width), small, fast)
    in_total = fence(in_keep + in_got.astype(WIDE))
    in_total, low_got, out_got = fence(halve(in_total, "fsdp", 1), low_got, out_got)
    low_sum = low_keep + low_got.astype(WIDE)
    out_two = (out_two.astype(WIDE) + out_got.astype(WIDE)).astype(LOW)
    out_low = jnp.concatenate([out_two[0], out_two[1]], axis=1)
    low_got, out_got = two_hops(low_sum[1].astype(LOW), out_low, 2 * fast)
    in_chunk, pair_have = fence(halve(in_total, "ctx", 2).astype(LOW), pair_have)
    in_spread = spread_groups(in_chunk)
    in_spread, low_got, out_got, one_got = fence(in_spread, low_got, out_got, one_got)
    low_spread = spread_groups((low_sum[0] + low_got.astype(WIDE)).astype(LOW))
    out_low = (out_low.astype(WIDE) + out_got.astype(WIDE)).astype(LOW)
    in_have = far_places(jnp.concatenate([*in_spread, out_low], axis=1))
    one_got, small = take_small(one_got, small)
    one_got = one_got.reshape(one_keep.shape)
    one_sum = one_keep[0] + one_got[0].astype(WIDE)
    one_send = (one_keep[1] + one_got[1].astype(WIDE)).astype(LOW)
    small = small + hop(small, "ctx", 1)
    for bit in bits_up(parts_f):
        small = small + hop(small, "fsdp", bit)
    low_spread, one_send, pair_have, small = fence(low_spread, one_send, pair_have, small)
    low_have = far_places(jnp.stack(low_spread))
    one_got, small = send_small(one_send, small, 2 * fast)
    pair_packs = both_cores(pair_have)
    in_packs, pair_packs = fence(both_cores(in_have), pair_packs)
    w_gate_grad, w_up_grad, w_query_grad, w_key_grad, w_value_grad, w_out_grad, result = most_finish(
        tick[0], pair_packs, in_packs, resid, out_list, parts_f, width
    )
    w_query_grad, one_got, low_have = fence(w_query_grad, one_got, low_have)
    low_packs = both_cores(low_have)
    small = take_small(one_got, small)[1]
    for bit in bits_down(fast // 2):
        small = small + hop(small, "ctx", 2 * bit)
    x_grad = last(tick[0], gain_one, own_x, grad_resid, one_sum, one_got)
    x_grad, low_packs = fence(x_grad, low_packs)
    w_down_grad = low_finish(tick[0], low_packs, parts_f)

    gain_rows = width // parts_f
    table_rows = bias_table.shape[0] // parts_f
    gain_one_grad = lax.dynamic_slice_in_dim(small[0], f * gain_rows, gain_rows)
    gain_two_grad = lax.dynamic_slice_in_dim(small[1], f * gain_rows, gain_rows)
    table_grad = small[2, : bias_table.size].reshape(bias_table.shape)
    table_grad = lax.dynamic_slice_in_dim(table_grad, f * table_rows, table_rows)

    return (
        result.reshape(micro, 1, block_rows, width),
        x_grad.reshape(micro, 1, block_rows, width),
        gain_one_grad,
        gain_two_grad,
        table_grad,
        w_query_grad,
        w_key_grad,
        w_value_grad,
        w_out_grad,
        w_gate_grad,
        w_up_grad,
        w_down_grad,
    )


def solution(mesh):
    in_specs = (
        P(None, "fsdp", "ctx", None),
        P(None, "fsdp", None),
        P(),
        P(),
        P(),
        P("fsdp", None),
        P("fsdp", None),
        P("fsdp", None),
        P("fsdp", None),
        P("fsdp", None),
        P("fsdp", None),
        P("fsdp", None),
        P(None, "fsdp", "ctx", None),
    )
    out_specs = (
        P(None, "fsdp", "ctx", None),
        P(None, "fsdp", "ctx", None),
        P("fsdp"),
        P("fsdp"),
        P("fsdp", None),
        P("fsdp", None),
        P("fsdp", None),
        P("fsdp", None),
        P("fsdp", None),
        P("fsdp", None),
        P("fsdp", None),
        P("fsdp", None),
    )
    return jax.shard_map(body, mesh=mesh, in_specs=in_specs, out_specs=out_specs, check_vma=False)
```

```python
import functools

import jax
import jax.numpy as jnp
from jax import lax
from jax.experimental import pallas as pl
from jax.experimental.pallas import tpu as pltpu
from jax.sharding import PartitionSpec as P

EPSILON = 1e-06
GROUPS = 4
WIDE = jnp.float32
LOW = jnp.bfloat16
FAR = 91
NEAR_LEAD = 96
VMEM_LIMIT = 60 * 1024 * 1024


def dot(a, b):
    return jnp.dot(a, b, preferred_element_type=WIDE)


def dot_t(a, b):
    return lax.dot_general(a, b, (((1,), (1,)), ((), ())), preferred_element_type=WIDE)


def t_dot(a, b):
    return lax.dot_general(a, b, (((0,), (0,)), ((), ())), preferred_element_type=WIDE)


def bucket_of(relative):
    distance = jnp.abs(relative)
    squared = distance * distance
    counted = jnp.zeros_like(relative)
    for exponent in range(1, 8):
        counted = counted + (squared >= 64 * 2**exponent).astype(jnp.int32)
    within = jnp.where(distance < 8, distance, 8 + counted)
    return jnp.where(relative > 0, 16, 0).astype(jnp.int32) + within


def hop(v, axis, bit):
    size = lax.axis_size(axis)
    return lax.ppermute(v, axis, [(i, i ^ bit) for i in range(size)])


def bits_down(size):
    bit = size // 2
    while bit >= 1:
        yield bit
        bit //= 2


def bits_up(size):
    return reversed(list(bits_down(size)))


def shift(v, steps):
    size = lax.axis_size("ctx")
    stride = size // GROUPS
    return lax.ppermute(v, "ctx", [(i, (i + steps * stride) % size) for i in range(size)])


def slots_out(v, axis, count):
    slots = {0: v}
    for bit in bits_down(count):
        for j in list(slots):
            slots[j ^ bit] = hop(slots[j], axis, bit)
    return [slots[j] for j in range(count)]


def pairs_on(parts, got, count):
    own, evens, _ = parts
    have = {k: evens[k - 1].astype(WIDE) + got[k].astype(WIDE) for k in range(1, count // 2)}
    mine, sent = [(own, False), (got, True)], []
    for bit in bits_up(count // 2):
        for k in sorted(have):
            if k & bit:
                sent.append(have[k].astype(LOW))
                part = hop(sent[-1], "ctx", 2 * bit)
                if k ^ bit:
                    have[k ^ bit] = have[k ^ bit] + part.astype(WIDE)
                else:
                    mine.append((part, False))
                del have[k]
    return mine, sent


def pairs_back(own, evens, odds, count):
    return pairs_on((own, evens, odds), hop(odds, "ctx", 1), count)


def halve(v, axis, unit):
    count = v.shape[0]
    for bit in bits_down(count):
        v = v[:bit] + hop(v[bit:].astype(LOW), axis, bit * unit).astype(WIDE)
    return v[0]


def strip_kernel(blocks, table_ref, strip_ref):
    centre = 64 * (blocks - 1)
    rows = 2 * 64 * blocks
    near = 256
    start = centre - NEAR_LEAD
    chunk = 128
    heads = table_ref.shape[1]

    def relative(first, count):
        u = lax.broadcasted_iota(jnp.int32, (count, 128), 0) + first
        i = lax.broadcasted_iota(jnp.int32, (count, 128), 1)
        return u - centre - jnp.where(i >= 64, i - 64, i)

    for h in range(heads):
        strip_ref[h, : start, :] = jnp.full((start, 128), table_ref[15, h], WIDE)
        strip_ref[h, start + near :, :] = jnp.full((rows - start - near, 128), table_ref[31, h], WIDE)
    for first in range(start, start + near, chunk):
        label = bucket_of(relative(first, chunk))
        for h in range(heads):
            value = jnp.zeros((chunk, 128), WIDE)
            for b in range(32):
                value = jnp.where(label == b, table_ref[b, h], value)
            strip_ref[h, first : first + chunk, :] = value


def make_strip(table_group, blocks):
    heads = table_group.shape[1]
    return pl.pallas_call(
        functools.partial(strip_kernel, blocks),
        out_shape=jax.ShapeDtypeStruct((heads, 2 * 64 * blocks, 128), WIDE),
        in_specs=[pl.BlockSpec(memory_space=pltpu.SMEM)],
        out_specs=pl.BlockSpec(memory_space=pltpu.VMEM),
        compiler_params=pltpu.CompilerParams(vmem_limit_bytes=VMEM_LIMIT),
        name="bias_strip",
    )(table_group)


def split_heads(wide, second_upper):
    lane = lax.broadcasted_iota(jnp.int32, (wide.shape[0], 128), 1)
    low = lane < 64
    zero = jnp.zeros((wide.shape[0], 128), wide.dtype)
    first, second = wide[:, :128], wide[:, 128:]
    third = jnp.where(low, zero, second) if second_upper else jnp.where(low, second, zero)
    return [jnp.where(low, first, zero), jnp.where(low, zero, first), third]


KEY_COLS = (0, 0, 128)
VALUE_COLS = (256, 256, 128)


def sort_blocks(count, m, kplace_ref, kv_refs, sorted_ref):
    for j in range(count):
        for e in range(GROUPS):
            to = pl.multiple_of(kplace_ref[m, j, e] * 64, 64)
            sorted_ref[pl.ds(to, 64), :] = kv_refs[j][e, 0]


def rows_sum(value):
    return jnp.sum(value.reshape(value.shape[0] // 8, 8, value.shape[1]), axis=0)


CHUNK = 128


def chunk_scores(strip_ref, sorted_ref, query, h, start, offs, low):
    scores = dot_t(sorted_ref[start : start + CHUNK, KEY_COLS[h] : KEY_COLS[h] + 128], query)
    parts = []
    for half in range(2):
        a = strip_ref[h, pl.ds(offs[2 * half] + start, CHUNK), :]
        b = strip_ref[h, pl.ds(offs[2 * half + 1] + start, CHUNK), :]
        parts.append(scores[:, half * 128 : half * 128 + 128] + jnp.where(low, a, b))
    return jnp.concatenate(parts, axis=1)


def forward_kernel(count, blocks, qplace_ref, kplace_ref, strip_ref, q_ref, *refs):
    kv_refs = refs[:count]
    o_refs = refs[count : count + GROUPS]
    lse_ref, sorted_ref, score_ref, weight_ref = refs[count + GROUPS :]
    m = pl.program_id(0)
    rows = 64 * blocks
    sort_blocks(count, m, kplace_ref, kv_refs, sorted_ref)
    offs = [pl.multiple_of((blocks - 1 - qplace_ref[m, e]) * 64, 64) for e in range(GROUPS)]
    queries = split_heads(q_ref[:, 0].reshape(GROUPS * 64, 256), False)
    low = lax.broadcasted_iota(jnp.int32, (CHUNK, 128), 1) < 64
    mixed = []
    for h in range(3):
        top = jnp.full((8, GROUPS * 64), -jnp.inf, WIDE)
        for start in range(0, rows, CHUNK):
            s = chunk_scores(strip_ref, sorted_ref, queries[h], h, start, offs, low)
            score_ref[start : start + CHUNK, :] = s
            top = jnp.maximum(top, jnp.max(s.reshape(CHUNK // 8, 8, GROUPS * 64), axis=0))
        top = jnp.max(top, axis=0, keepdims=True)
        total = jnp.zeros((8, GROUPS * 64), WIDE)
        for start in range(0, rows, CHUNK):
            e = jnp.exp(score_ref[start : start + CHUNK, :] - top)
            score_ref[start : start + CHUNK, :] = e
            total = total + rows_sum(e)
        total = jnp.sum(total, axis=0, keepdims=True)
        lse_ref[0, h : h + 1, :] = top + jnp.log(total)
        scale = 1.0 / total
        for start in range(0, rows, CHUNK):
            weight_ref[start : start + CHUNK, :] = (score_ref[start : start + CHUNK, :] * scale).astype(LOW)
        mixed.append(t_dot(sorted_ref[:, VALUE_COLS[h] : VALUE_COLS[h] + 128], weight_ref[...]))
    sub = lax.broadcasted_iota(jnp.int32, (128, GROUPS * 64), 0) < 64
    first = jnp.where(sub, mixed[0], mixed[1]).T
    second = jnp.where(sub, 0.0, mixed[2]).T
    out = jnp.concatenate([first, second], axis=1).astype(LOW)
    for d in range(GROUPS):
        o_refs[d][0] = out[d * 64 : d * 64 + 64]


def attention_forward(places, strip, q, kv_slots, blocks):
    qplace, kplace = places
    count = len(kv_slots)
    micro = q.shape[1]
    rows = 64 * blocks
    kv_cols = kv_slots[0].shape[-1]
    by_micro = lambda width: pl.BlockSpec((GROUPS, 1, 64, width), lambda m, *_: (0, m, 0, 0))
    results = pl.pallas_call(
        functools.partial(forward_kernel, count, blocks),
        out_shape=(jax.ShapeDtypeStruct((micro, 64, 256), LOW),) * GROUPS
        + (jax.ShapeDtypeStruct((micro, 3, GROUPS * 64), WIDE),),
        grid_spec=pltpu.PrefetchScalarGridSpec(
            num_scalar_prefetch=2,
            grid=(micro,),
            in_specs=[pl.BlockSpec(strip.shape, lambda m, *_: (0, 0, 0)), by_micro(256)] + [by_micro(kv_cols)] * count,
            out_specs=(pl.BlockSpec((1, 64, 256), lambda m, *_: (m, 0, 0)),) * GROUPS
            + (pl.BlockSpec((1, 3, GROUPS * 64), lambda m, *_: (m, 0, 0)),),
            scratch_shapes=[
                pltpu.VMEM((rows, kv_cols), LOW),
                pltpu.VMEM((rows, GROUPS * 64), WIDE),
                pltpu.VMEM((rows, GROUPS * 64), LOW),
            ],
        ),
        compiler_params=pltpu.CompilerParams(vmem_limit_bytes=VMEM_LIMIT),
        cost_estimate=pl.CostEstimate(
            flops=micro * 3 * 2 * 2 * rows * GROUPS * 64 * 128 * 2,
            bytes_accessed=micro * rows * kv_cols * 4,
            transcendentals=micro * 3 * rows * GROUPS * 64,
        ),
        name="attention_forward",
    )(qplace, kplace, strip, q, *kv_slots)
    return list(results[:GROUPS]), results[GROUPS]


def backward_kernel(count, blocks, qplace_ref, kplace_ref, place_ref, strip_ref, q_ref, lse_ref, *refs):
    do_refs, refs = refs[:GROUPS], refs[GROUPS:]
    kv_refs = refs[:count]
    dq_ref = refs[count]
    own_ref, even_ref, odd_ref, table_ref = refs[count + 1 : count + 5]
    sorted_ref, grad_ref, p_ref, dp_ref, soft_ref, ds_ref, wide_ref, near_ref, far_ref = refs[count + 5 :]
    m = pl.program_id(0)
    rows = 64 * blocks
    queue = GROUPS * 64
    near = near_ref.shape[1]
    lead = 128

    @pl.when(m == 0)
    def _():
        near_ref[...] = jnp.zeros_like(near_ref)
        far_ref[...] = jnp.zeros_like(far_ref)
        wide_ref[:lead, :] = jnp.zeros((lead, queue), WIDE)
        wide_ref[lead + rows :, :] = jnp.zeros((wide_ref.shape[0] - lead - rows, queue), WIDE)

    sort_blocks(count, m, kplace_ref, kv_refs, sorted_ref)
    offs = [pl.multiple_of((blocks - 1 - qplace_ref[m, e]) * 64, 64) for e in range(GROUPS)]
    queries = split_heads(q_ref[:, 0].reshape(queue, 256), False)
    grads = split_heads(jnp.concatenate([r[0] for r in do_refs], axis=0), True)
    low = lax.broadcasted_iota(jnp.int32, (CHUNK, 128), 1) < 64
    lane_block = lax.broadcasted_iota(jnp.int32, (8, queue), 1) // 64
    own_place = jnp.zeros((8, queue), jnp.int32)
    for e in range(GROUPS):
        own_place = jnp.where(lane_block == e, qplace_ref[m, e], own_place)
    near_low = lax.broadcasted_iota(jnp.int32, (near, 128), 1) < 64
    query_grads = []
    for h in range(3):
        delta = jnp.zeros((8, queue), WIDE)
        lse = lse_ref[0, h : h + 1, :]
        for start in range(0, rows, CHUNK):
            at = slice(start, start + CHUNK)
            p = jnp.exp(chunk_scores(strip_ref, sorted_ref, queries[h], h, start, offs, low) - lse)
            dp = dot_t(sorted_ref[at, VALUE_COLS[h] : VALUE_COLS[h] + 128], grads[h])
            p_ref[at, :] = p
            dp_ref[at, :] = dp
            soft_ref[h, at, :] = p.astype(LOW)
            delta = delta + rows_sum(p * dp)
        delta = jnp.sum(delta, axis=0, keepdims=True)
        before = jnp.zeros((8, queue), WIDE)
        after = jnp.zeros((8, queue), WIDE)
        for start in range(0, rows, CHUNK):
            at = slice(start, start + CHUNK)
            ds = (p_ref[at, :] * (dp_ref[at, :] - delta)).astype(LOW)
            ds_ref[h, at, :] = ds
            wide = ds.astype(WIDE)
            wide_ref[lead + start : lead + start + CHUNK, :] = wide
            for k in range(CHUNK // 64):
                block = start // 64 + k
                part = rows_sum(wide[k * 64 : k * 64 + 64])
                before = before + jnp.where(own_place >= block + 3, part, 0.0)
                after = after + jnp.where(own_place <= block - 3, part, 0.0)
        far_ref[h, 0] += before
        far_ref[h, 1] += after
        for half in range(2):
            cols = slice(half * 128, half * 128 + 128)
            a = wide_ref[pl.ds(pl.multiple_of(qplace_ref[m, 2 * half] * 64, 64), near), cols]
            b = wide_ref[pl.ds(pl.multiple_of(qplace_ref[m, 2 * half + 1] * 64, 64), near), cols]
            near_ref[h] += jnp.where(near_low, a, b)
        query_grads.append(t_dot(sorted_ref[:, KEY_COLS[h] : KEY_COLS[h] + 128], ds_ref[h]))
    sub = lax.broadcasted_iota(jnp.int32, (128, queue), 0) < 64
    first = jnp.where(sub, query_grads[0], query_grads[1]).T
    second = jnp.where(sub, query_grads[2], 0.0).T
    dq_ref[:, 0] = jnp.concatenate([first, second], axis=1).astype(LOW).reshape(GROUPS, 64, 256)
    grad_ref[:, 0:128] = dot(ds_ref[0], queries[0]) + dot(ds_ref[1], queries[1])
    grad_ref[:, 128:256] = dot(ds_ref[2], queries[2]) + dot(soft_ref[2], grads[2])
    grad_ref[:, 256:384] = dot(soft_ref[0], grads[0]) + dot(soft_ref[1], grads[1])
    for j in range(count):
        for e in range(GROUPS):
            at = pl.multiple_of(kplace_ref[m, j, e] * 64, 64)
            value = grad_ref[pl.ds(at, 64), :]
            if j == 0:
                own_ref[e, 0] = value
            elif j % 2:
                odd_ref[j // 2, e, 0] = value.astype(LOW)
            else:
                even_ref[j // 2 - 1, e, 0] = value.astype(LOW)

    @pl.when(m == pl.num_programs(0) - 1)
    def _():
        sums_row = lax.broadcasted_iota(jnp.int32, (32, 128), 0)
        lanes = lax.broadcasted_iota(jnp.int32, (32, 128), 1)
        side = lax.broadcasted_iota(jnp.int32, (near, 128), 1)
        rel = lax.broadcasted_iota(jnp.int32, (near, 128), 0) - lead - jnp.where(side >= 64, side - 64, side)
        label = bucket_of(rel)
        table = jnp.zeros((32, 128), WIDE)
        for h in range(3):
            far = [jnp.sum(far_ref[h, k][:, :128] + far_ref[h, k][:, 128:], axis=0, keepdims=True) for k in range(2)]
            result = jnp.where(sums_row == 15, far[0], jnp.where(sums_row == 31, far[1], 0.0))
            window = near_ref[h]
            for b in range(32):
                part = jnp.sum(jnp.where(label == b, window, 0.0), axis=0, keepdims=True)
                result = result + jnp.where(sums_row == b, part, 0.0)
            total = jnp.sum(result, axis=1, keepdims=True)
            table = jnp.where(lanes == place_ref[0] * 3 + h, total, table)
        table_ref[...] = table


def attention_backward(places, place, strip, q, kv_slots, do_slots, lse, blocks):
    qplace, kplace = places
    count = len(kv_slots)
    micro = q.shape[1]
    rows = 64 * blocks
    kv_cols = kv_slots[0].shape[-1]
    by_micro = lambda width: pl.BlockSpec((GROUPS, 1, 64, width), lambda m, *_: (0, m, 0, 0))
    kv_shape = kv_slots[0].shape
    by_part = lambda n: pl.BlockSpec((n, GROUPS, 1, 64, kv_cols), lambda m, *_: (0, 0, m, 0, 0))
    results = pl.pallas_call(
        functools.partial(backward_kernel, count, blocks),
        out_shape=(jax.ShapeDtypeStruct(q.shape, LOW),)
        + (
            jax.ShapeDtypeStruct(kv_shape, WIDE),
            jax.ShapeDtypeStruct((count // 2 - 1,) + kv_shape, LOW),
            jax.ShapeDtypeStruct((count // 2,) + kv_shape, LOW),
        )
        + (jax.ShapeDtypeStruct((32, 128), WIDE),),
        grid_spec=pltpu.PrefetchScalarGridSpec(
            num_scalar_prefetch=3,
            grid=(micro,),
            in_specs=[
                pl.BlockSpec(strip.shape, lambda m, *_: (0, 0, 0)),
                by_micro(256),
                pl.BlockSpec((1, 3, GROUPS * 64), lambda m, *_: (m, 0, 0)),
            ]
            + [pl.BlockSpec((1, 64, 256), lambda m, *_: (m, 0, 0))] * GROUPS
            + [by_micro(kv_cols)] * count,
            out_specs=(by_micro(256),)
            + (by_micro(kv_cols), by_part(count // 2 - 1), by_part(count // 2))
            + (pl.BlockSpec((32, 128), lambda m, *_: (0, 0)),),
            scratch_shapes=[
                pltpu.VMEM((rows, kv_cols), LOW),
                pltpu.VMEM((rows, kv_cols), WIDE),
                pltpu.VMEM((rows, GROUPS * 64), WIDE),
                pltpu.VMEM((rows, GROUPS * 64), WIDE),
                pltpu.VMEM((3, rows, GROUPS * 64), LOW),
                pltpu.VMEM((3, rows, GROUPS * 64), LOW),
                pltpu.VMEM((rows + 256, GROUPS * 64), WIDE),
                pltpu.VMEM((3, 320, 128), WIDE),
                pltpu.VMEM((3, 2, 8, GROUPS * 64), WIDE),
            ],
        ),
        compiler_params=pltpu.CompilerParams(vmem_limit_bytes=VMEM_LIMIT),
        cost_estimate=pl.CostEstimate(
            flops=micro * 3 * 5 * 2 * rows * GROUPS * 64 * 128 * 2,
            bytes_accessed=micro * rows * kv_cols * 8,
            transcendentals=micro * 3 * rows * GROUPS * 64,
        ),
        name="attention_backward",
    )(qplace, kplace, place, strip, q, lse, *do_slots, *kv_slots)
    return results[0], results[1:4], results[4]


PLACE = pl.BlockSpec(memory_space=pltpu.SMEM)


def whole(count):
    return [pl.BlockSpec(memory_space=pltpu.VMEM)] * count


def first_entry(v):
    return pl.BlockSpec((1,) + v.shape[1:], lambda _: (0,) * v.ndim)


def call(kernel, name, place, operands, out_shape, scratch=(), flops=0):
    operands = [v if isinstance(v, tuple) else (v, False) for v in operands]
    grid = {"grid": (1,)} if any(first for _, first in operands) else {}
    specs = [PLACE] + [first_entry(v) if first else whole(1)[0] for v, first in operands]
    operands = [v for v, _ in operands]
    size = sum(v.size * v.dtype.itemsize for v in operands) + sum(
        v.size * jnp.dtype(v.dtype).itemsize for v in out_shape
    )
    return pl.pallas_call(
        kernel,
        out_shape=tuple(out_shape),
        **grid,
        in_specs=specs,
        out_specs=tuple(whole(len(out_shape))),
        scratch_shapes=list(scratch),
        compiler_params=pltpu.CompilerParams(vmem_limit_bytes=VMEM_LIMIT),
        cost_estimate=pl.CostEstimate(flops=flops, bytes_accessed=size, transcendentals=0),
        name=name,
    )(place, *operands)


def shaped(*shape, dtype=LOW):
    return jax.ShapeDtypeStruct(shape, dtype)


def place_rows(full_ref, slot_refs, index):
    rows = slot_refs[0].shape[0]
    for j, ref in enumerate(slot_refs):
        full_ref[pl.ds(pl.multiple_of((index ^ j) * rows, rows), rows), :] = ref[...]


def rms_scale(values):
    return lax.rsqrt(jnp.mean(values * values, axis=-1, keepdims=True) + EPSILON)


def norm_back(grad_normed, normed, scale):
    return scale * (grad_normed - normed * jnp.mean(grad_normed * normed, axis=-1, keepdims=True))


def project_kernel(parts_f, place_ref, gain_ref, *refs):
    x_refs, w_refs = refs[:GROUPS], refs[GROUPS : GROUPS + parts_f]
    act_ref, q_ref, kv_ref, full_ref = refs[GROUPS + parts_f :]
    place_rows(full_ref, w_refs, place_ref[2])
    micro, rows, width = x_refs[0].shape
    for d in range(GROUPS):
        x = x_refs[d][...].reshape(micro * rows, width).astype(WIDE)
        act_ref[d] = (x * rms_scale(x) * gain_ref[...]).astype(LOW)
    both = dot(act_ref[...].reshape(GROUPS * micro * rows, width), full_ref[...]).astype(LOW)
    q_ref[...] = both[:, :256].reshape(GROUPS, micro, rows, 256)
    kv_ref[...] = both[:, 256:].reshape(GROUPS, micro, rows, 384)


def project(place, gain, x_slots, w_slots):
    micro, rows, width = x_slots[0].shape
    return call(
        functools.partial(project_kernel, len(w_slots)),
        "project",
        place,
        [gain, *x_slots, *w_slots],
        [
            shaped(GROUPS, micro * rows, width),
            shaped(GROUPS, micro, rows, 256),
            shaped(GROUPS, micro, rows, 384),
        ],
        [pltpu.VMEM((width, 640), LOW)],
        flops=2 * GROUPS * micro * rows * width * 640,
    )


def group_rows(place_ref, d):
    return lax.rem(place_ref[0] + d, GROUPS) * 192


def arrange_kernel(parts_f, place_ref, *refs):
    w_refs, (out_ref, full_ref) = refs[:parts_f], refs[parts_f:]
    place_rows(full_ref, w_refs, place_ref[2])
    for d in range(GROUPS):
        at = group_rows(place_ref, d)
        out_ref[d * 256 : d * 256 + 128, :] = full_ref[pl.ds(pl.multiple_of(at, 64), 128), :]
        out_ref[d * 256 + 128 : d * 256 + 256, :] = full_ref[pl.ds(pl.multiple_of(at + 64, 64), 128), :]


def arrange(place, w_slots):
    width = w_slots[0].shape[1]
    return call(
        functools.partial(arrange_kernel, len(w_slots)),
        "arrange",
        place,
        w_slots,
        [shaped(GROUPS * 256, width)],
        [pltpu.VMEM((width, width), LOW)],
    )[0]


def joined_kernel(place_ref, gain_ref, x_ref, w_ref, *refs):
    o_refs, (resid_ref, act_ref) = refs[:GROUPS], refs[GROUPS:]
    micro, rows, width = x_ref.shape
    o = jnp.concatenate([r[...].reshape(micro * rows, 256) for r in o_refs], axis=1)
    total = x_ref[...].reshape(micro * rows, width).astype(WIDE) + dot(o, w_ref[...])
    resid_ref[...] = total
    act_ref[...] = (total * rms_scale(total) * gain_ref[...]).astype(LOW)


def joined(place, gain, x, o_slots, w_rel):
    micro, rows, width = x.shape
    return call(
        joined_kernel,
        "joined",
        place,
        [gain, x, w_rel, *o_slots],
        [shaped(micro * rows, width, dtype=WIDE), shaped(micro * rows, width)],
        flops=2 * micro * rows * width * 1024,
    )


GELU_A = 0.7978845608028654
GELU_B = 0.044715


def put_part(refs, j, value):
    own_ref, even_ref, odd_ref = refs
    if j == 0:
        own_ref[...] = value
    elif j % 2:
        odd_ref[j // 2] = value.astype(odd_ref.dtype)
    else:
        even_ref[j // 2 - 1] = value.astype(even_ref.dtype)


def part_shapes(shape, fast):
    return [
        shaped(*shape, dtype=WIDE),
        shaped(fast // 2 - 1, *shape),
        shaped(fast // 2, *shape),
    ]


def feed_kernel(parts_f, fast, place_ref, *refs):
    act_refs, refs = refs[:fast], refs[fast:]
    g_refs, refs = refs[:fast], refs[fast:]
    pair_refs, refs = refs[:parts_f], refs[parts_f:]
    down_refs, refs = refs[:parts_f], refs[parts_f:]
    two_refs, out_refs, refs = refs[:3], refs[3:6], refs[6:]
    hid_ref, grad_ref, pair_ref, down_ref = refs
    place_rows(pair_ref, pair_refs, place_ref[2])
    place_rows(down_ref, down_refs, place_ref[2])
    cols = hid_ref.shape[-1]
    rows = act_refs[0].shape[0]
    act = jnp.concatenate([r[...] for r in act_refs], axis=0)
    g = jnp.concatenate([r[...] for r in g_refs], axis=0)
    both = dot(act, pair_ref[...])
    dh = dot_t(g, down_ref[...])
    for j in range(fast):
        at = slice(j * rows, j * rows + rows)
        z, up = both[at, :cols], both[at, cols:]
        square = z * z
        t = jnp.tanh(GELU_A * (z + GELU_B * square * z))
        half = 0.5 * (1.0 + t)
        gelu = z * half
        slope = half + (0.5 * z) * (1.0 - t * t) * (GELU_A * (1.0 + 3.0 * GELU_B * square))
        hid_ref[j] = (gelu * up).astype(LOW)
        grad_ref[j, :, :cols] = (dh[at] * up * slope).astype(LOW)
        grad_ref[j, :, cols:] = (dh[at] * gelu).astype(LOW)
    two = dot_t(grad_ref[...].reshape(fast * rows, 2 * cols), pair_ref[...])
    out = dot(hid_ref[...].reshape(fast * rows, cols), down_ref[...])
    for j in range(fast):
        put_part(two_refs, j, two[j * rows : j * rows + rows])
        put_part(out_refs, j, out[j * rows : j * rows + rows])


def feed(place, act_slots, g_slots, pair_slots, down_slots):
    fast, parts_f = len(act_slots), len(pair_slots)
    rows, width = act_slots[0].shape
    cols = down_slots[0].shape[0] * parts_f
    results = call(
        functools.partial(feed_kernel, parts_f, fast),
        "feed",
        place,
        [*act_slots, *g_slots, *pair_slots, *down_slots],
        part_shapes((rows, width), fast) * 2 + [shaped(fast, rows, cols), shaped(fast, rows, 2 * cols)],
        [pltpu.VMEM((width, 2 * cols), LOW), pltpu.VMEM((cols, width), LOW)],
        flops=2 * fast * rows * width * cols * 6,
    )
    return results[:3], results[3:6], results[-2], results[-1]


def packing(piece, rows):
    if rows == 3 * piece:
        return [(0, k * 256, k * piece, 0, piece, 256) for k in range(3)]
    half = piece // 2
    return [
        (0, 0, 0, 0, piece, 512),
        (0, 512, piece, 0, half, 256),
        (half, 512, piece, 256, half, 256),
    ]


def pair_grads_kernel(fast, place_ref, *refs):
    act_refs, grad_ref, refs = refs[:fast], refs[fast], refs[fast + 1 :]
    outs, full_ref = refs[:-1], refs[-1]
    act = jnp.concatenate([r[...] for r in act_refs], axis=0)
    full_ref[...] = t_dot(act, grad_ref[...].reshape(act.shape[0], -1))
    rows = outs[0].shape[0]
    for j, out in enumerate(outs):
        at = pl.multiple_of((place_ref[2] ^ j) * rows, rows)
        out[...] = full_ref[pl.ds(at, rows), :].astype(out.dtype)


def pair_grads(place, act_slots, grads, parts_f):
    fast, rows, double = grads.shape
    width = act_slots[0].shape[1]
    types = [WIDE] + [LOW] * (parts_f - 1)
    return call(
        functools.partial(pair_grads_kernel, fast),
        "pair_grads",
        place,
        [*act_slots, grads],
        [shaped(width // parts_f, double, dtype=t) for t in types],
        [pltpu.VMEM((width, double), WIDE)],
        flops=2 * fast * rows * width * double,
    )


def down_grads_kernel(fast, place_ref, *refs):
    g_refs, hid_ref, refs = refs[:fast], refs[fast], refs[fast + 1 :]
    outs, full_ref = refs[:-1], refs[-1]
    g = jnp.concatenate([r[...] for r in g_refs], axis=0)
    full_ref[...] = t_dot(hid_ref[...].reshape(g.shape[0], -1), g)
    rows = outs[0].shape[0]
    piece = full_ref.shape[0] // len(outs)
    for j, out in enumerate(outs):
        for r, c, to_r, to_c, n, w in packing(piece, rows):
            at = pl.multiple_of((place_ref[2] ^ j) * piece + r, 8)
            out[to_r : to_r + n, to_c : to_c + w] = full_ref[pl.ds(at, n), c : c + w].astype(out.dtype)


def down_grads(place, g_slots, hid, parts_f):
    fast, rows, cols = hid.shape
    width = g_slots[0].shape[1]
    types = [WIDE] + [LOW] * (parts_f - 1)
    return call(
        functools.partial(down_grads_kernel, fast),
        "down_grads",
        place,
        [*g_slots, hid],
        [shaped(width // parts_f, cols, dtype=t) for t in types],
        [pltpu.VMEM((cols, width), WIDE)],
        flops=2 * fast * rows * width * cols,
    )


def group_split_kernel(count, place_ref, *refs):
    own_ref, send_refs = refs[count], refs[count + 1 :]
    rows = own_ref.shape[0]

    def part(d):
        at = pl.ds(pl.multiple_of(lax.rem(place_ref[0] + d, GROUPS) * rows, 8), rows)
        return sum(r[at, :].astype(WIDE) for r in refs[:count])

    own_ref[...] = part(0)
    for d, ref in enumerate(send_refs, 1):
        ref[...] = part(d).astype(ref.dtype)


def group_split(place, parts):
    rows, cols = parts[0].shape
    cut = rows // GROUPS
    results = call(
        functools.partial(group_split_kernel, len(parts)),
        "group_split",
        place,
        parts,
        [shaped(cut, cols, dtype=WIDE)] + [shaped(cut, cols)] * (GROUPS - 1),
    )
    return results[0], list(results[1:])


def group_halves_kernel(count, place_ref, *refs):
    keep_ref, send_ref = refs[count:]
    rows = keep_ref.shape[1]
    for d in range(GROUPS):
        at = pl.ds(pl.multiple_of((place_ref[0] ^ d) * rows, 8), rows)
        total = sum(r[at, :].astype(WIDE) for r in refs[:count])
        if d % 2:
            send_ref[d // 2] = total.astype(send_ref.dtype)
        else:
            keep_ref[d // 2] = total


def group_halves(place, parts):
    rows, cols = parts[0].shape
    cut = (GROUPS // 2, rows // GROUPS, cols)
    return call(
        functools.partial(group_halves_kernel, len(parts)),
        "group_halves",
        place,
        parts,
        [shaped(*cut, dtype=WIDE), shaped(*cut)],
    )


def summed(refs):
    return sum((r[0] if len(r.shape) == 3 else r[...]).astype(WIDE) for r in refs)


def branch_kernel(count, place_ref, gain_ref, resid_ref, g_ref, w_ref, *refs):
    two_refs, refs = refs[:count], refs[count:]
    grad_ref, low_ref, gain_out = refs[:3]
    do_refs = refs[3:]
    micro, rows, _ = do_refs[0].shape
    grad_two = summed(two_refs)
    resid = resid_ref[...]
    scale = rms_scale(resid)
    normed = resid * scale
    gain_out[...] = jnp.sum(grad_two * normed, axis=0, keepdims=True)
    grad = g_ref[...].astype(WIDE) + norm_back(grad_two * gain_ref[...], normed, scale)
    grad_ref[...] = grad
    low = grad.astype(LOW)
    low_ref[...] = low
    both = dot_t(low, w_ref[...]).astype(LOW)
    for d in range(GROUPS):
        do_refs[d][...] = both[:, d * 256 : d * 256 + 256].reshape(micro, rows, 256)


def branch(place, gain, resid, g, two_list, w_rel, micro):
    rows, width = resid.shape
    results = call(
        functools.partial(branch_kernel, len(two_list)),
        "branch",
        place,
        [gain, resid, g, w_rel, *two_list],
        [shaped(rows, width, dtype=WIDE), shaped(rows, width), shaped(1, width, dtype=WIDE)]
        + [shaped(micro, rows // micro, 256)] * GROUPS,
        flops=2 * rows * width * 1024,
    )
    return results[0], results[1], results[2], list(results[3:])


def with_rows(index, rows, count, action):
    if rows % 8 == 0:
        action(pl.ds(pl.multiple_of(index * rows, 8), rows))
        return
    for known in range(count):

        @pl.when(index == known)
        def _():
            action(slice(known * rows, known * rows + rows))


def write_chunks(place_ref, full_ref, keep_ref, send_ref):
    parts_f, halves, rows, _ = keep_ref.shape
    for i in range(parts_f):
        for k in range(halves):
            for odd, ref in ((0, keep_ref), (1, send_ref)):
                index = (place_ref[2] ^ i) * (2 * halves) + (place_ref[1] ^ (2 * k + odd))

                def copy(at):
                    ref[i, k] = full_ref[at, :].astype(ref.dtype)

                with_rows(index, rows, 2 * halves * parts_f, copy)


def out_grads_kernel(place_ref, low_ref, *refs):
    o_refs = refs[:GROUPS]
    keep_ref, send_ref, full_ref = refs[GROUPS:]
    micro, rows, _ = o_refs[0].shape
    low = low_ref[...]
    for d in range(GROUPS):
        both = t_dot(o_refs[d][...].reshape(micro * rows, 256), low)
        at = group_rows(place_ref, d)
        full_ref[pl.ds(pl.multiple_of(at, 64), 128), :] = both[:128]
        full_ref[pl.ds(pl.multiple_of(at + 128, 64), 64), :] = both[192:]
    write_chunks(place_ref, full_ref, keep_ref, send_ref)


def out_grads(place, low, o_slots, parts_f, fast):
    rows, width = low.shape
    chunk = (parts_f, fast // 2, width // (parts_f * fast), width)
    return call(
        out_grads_kernel,
        "out_grads",
        place,
        [low, *o_slots],
        [shaped(*chunk, dtype=WIDE), shaped(*chunk)],
        [pltpu.VMEM((width, width), WIDE)],
        flops=2 * rows * width * 1024,
    )


def input_grads_kernel(parts_f, count, place_ref, act_ref, dq_ref, *refs):
    x_refs, refs = refs[:GROUPS], refs[GROUPS:]
    dkv_refs, refs = refs[:count], refs[count:]
    w_refs, refs = refs[:parts_f], refs[parts_f:]
    one_keep, one_send, gain_out, keep_ref, send_ref, full_ref, sums_ref, both_ref, one_ref = refs
    place_rows(full_ref, w_refs, place_ref[2])
    groups, rows, width = act_ref.shape
    micro = dq_ref.shape[1]
    gain_total = jnp.zeros((1, width), WIDE)
    for d in range(GROUPS):
        dkv = sum((r[0, d] if len(r.shape) == 5 else r[d]).astype(WIDE) for r in dkv_refs)
        dkv = dkv.astype(LOW).reshape(rows, 384)
        both = jnp.concatenate([dq_ref[d].reshape(rows, 256), dkv], axis=1)
        both_ref[d] = both
        one = dot_t(both, full_ref[...])
        x = x_refs[d][...].reshape(rows, width).astype(WIDE)
        gain_total = gain_total + jnp.sum(one * (x * rms_scale(x)), axis=0, keepdims=True)
        one_ref[lax.rem(place_ref[0] + GROUPS - d, GROUPS)] = one
    for d in range(GROUPS):
        value = one_ref[place_ref[0] ^ d]
        if d % 2:
            one_send[d // 2] = value.astype(LOW)
        else:
            one_keep[d // 2] = value
    gain_out[...] = gain_total
    sums_ref[...] = t_dot(act_ref[...].reshape(groups * rows, width), both_ref[...].reshape(groups * rows, 640))
    write_chunks(place_ref, sums_ref, keep_ref, send_ref)


def input_grads(place, act, dq, x_slots, dkv_list, w_slots, fast):
    groups, rows, width = act.shape
    micro = dq.shape[1]
    parts_f = len(w_slots)
    chunk = (parts_f, fast // 2, width // (parts_f * fast), 640)
    return call(
        functools.partial(input_grads_kernel, parts_f, len(dkv_list)),
        "input_grads",
        place,
        [act, dq, *x_slots, *dkv_list, *w_slots],
        [shaped(GROUPS // 2, rows, width, dtype=WIDE), shaped(GROUPS // 2, rows, width)]
        + [shaped(1, width, dtype=WIDE), shaped(*chunk, dtype=WIDE), shaped(*chunk)],
        [
            pltpu.VMEM((width, 640), LOW),
            pltpu.VMEM((width, 640), WIDE),
            pltpu.VMEM((groups, rows, 640), LOW),
            pltpu.VMEM((groups, rows, width), WIDE),
        ],
        flops=4 * groups * rows * width * 640,
    )


def last_kernel(place_ref, gain_ref, x_ref, grad_ref, one_ref, got_ref, x_grad_ref):
    micro, rows, width = x_ref.shape
    grad_one = one_ref[...] + got_ref[: micro * rows, :].astype(WIDE)
    x = x_ref[...].reshape(micro * rows, width).astype(WIDE)
    scale = rms_scale(x)
    x_grad_ref[...] = grad_ref[...] + norm_back(grad_one * gain_ref[...], x * scale, scale)


def last(place, gain, x, grad, one, one_got):
    return call(
        last_kernel, "last", place, [gain, x, grad, one, one_got], [shaped(*grad.shape, dtype=WIDE)]
    )[0]


def pair_finish_kernel(parts_f, fast, place_ref, *refs):
    pair_refs, (gate_ref, up_ref) = refs[:fast], refs[fast:]
    _, rows, double = pair_refs[0].shape
    cols = double // 2
    piece = cols // parts_f
    for j in range(fast):
        other = place_ref[1] ^ j
        for d in range(GROUPS):
            at = pl.ds(pl.multiple_of(lax.rem(place_ref[0] + GROUPS - d, GROUPS) * rows, 8), rows)
            for start, ref in ((0, gate_ref), (cols, up_ref)):
                for k in range(parts_f):
                    value = pair_refs[j][d, :, start + k * piece : start + (k + 1) * piece].astype(WIDE)
                    if piece % 128 == 0:
                        to = pl.multiple_of(k * fast * piece + other * piece, 128)
                        ref[at, pl.ds(to, piece)] = value
                    else:
                        for l in range(fast):

                            @pl.when(other == l)
                            def _():
                                ref[at, (k * fast + l) * piece : (k * fast + l + 1) * piece] = value


def low_finish_kernel(parts_f, fast, place_ref, *refs):
    low_refs, (down_ref, pack_ref) = refs[:fast], refs[fast:]
    _, rows, cols = low_refs[0].shape
    piece = cols // parts_f
    for j in range(fast):
        for d in range(GROUPS):
            at = pl.ds(pl.multiple_of(lax.rem(place_ref[0] + GROUPS - d, GROUPS) * rows, 8), rows)
            pack_ref[at, :] = low_refs[j][d].astype(WIDE)
        for r, c, to_r, to_c, n, w in packing(piece, rows * GROUPS):
            at = pl.ds(pl.multiple_of((place_ref[1] ^ j) * piece + r, 8), n)
            down_ref[at, c : c + w] = pack_ref[to_r : to_r + n, to_c : to_c + w]


def low_finish(place, packs, parts_f):
    fast = len(packs)
    _, rows, cols = packs[0].shape
    return call(
        functools.partial(low_finish_kernel, parts_f, fast),
        "low_finish",
        place,
        packs,
        [shaped(cols // parts_f * fast, rows * GROUPS * parts_f, dtype=WIDE)],
        [pltpu.VMEM((rows * GROUPS, cols), WIDE)],
    )[0]


def input_finish_kernel(fast, place_ref, *refs):
    pack_refs = refs[:fast]
    query_ref, key_ref, value_ref, out_ref = refs[fast:]
    rows = pack_refs[0].shape[0]
    for j in range(fast):
        value = pack_refs[j][:, GROUPS * 640 :].astype(WIDE)

        def place_out(at):
            out_ref[at, :] = value

        with_rows(place_ref[1] ^ j, rows, fast, place_out)
    for h in range(GROUPS):

        @pl.when(place_ref[0] == h)
        def _():
            for j in range(fast):
                starts = [(h - g) % GROUPS * 640 for g in range(GROUPS)]
                part = lambda a, b: pack_refs[j][:, a:b].astype(WIDE)
                query = jnp.concatenate([part(s, s + 192) for s in starts], axis=1)
                key = jnp.concatenate([part(s + 256, s + 448) for s in starts], axis=1)
                value = jnp.concatenate([p for s in starts for p in (part(s + 512, s + 640), part(s + 448, s + 512))], axis=1)

                def place_in(at):
                    query_ref[at, :] = query
                    key_ref[at, :] = key
                    value_ref[at, :] = value

                with_rows(place_ref[1] ^ j, rows, fast, place_in)


def most_finish_kernel(parts_f, fast, place_ref, *refs):
    pair_refs, pack_refs, refs = refs[:fast], refs[fast : 2 * fast], refs[2 * fast :]
    pair_finish_kernel(parts_f, fast, place_ref, *pair_refs, *refs[-7:-5])
    input_finish_kernel(fast, place_ref, *pack_refs, *refs[-5:-1])
    resid_ref, out_refs, out_ref = refs[0], refs[1:-7], refs[-1]
    rows = resid_ref.shape[0]
    parts = [(r[0] if len(r.shape) == 3 else r[r.shape[0] - rows :, :]).astype(WIDE) for r in out_refs]
    out_ref[...] = (resid_ref[...] + sum(parts)).astype(LOW)


def most_finish(place, pair_packs, packs, resid, out_list, parts_f, width):
    fast = len(packs)
    _, rows, double = pair_packs[0].shape
    return call(
        functools.partial(most_finish_kernel, parts_f, fast),
        "most_finish",
        place,
        [*pair_packs, *packs, resid, *out_list],
        [shaped(rows * GROUPS, double // 2 * fast, dtype=WIDE)] * 2
        + [shaped(packs[0].shape[0] * fast, width, dtype=WIDE)] * 4
        + [shaped(*resid.shape)],
    )


def spread_groups(v):
    return [v] + [shift(v, d) for d in range(1, GROUPS)]


def gather_pack(pack, fast):
    slots = {0: pack}
    for bit in bits_down(fast):
        for j in list(slots):
            slots[j ^ bit] = hop(slots[j], "ctx", bit)
    return [slots[j] for j in range(fast)]


def after(value, *others):
    return lax.optimization_barrier((value, *others))[0]


def body(
    tokens,
    offsets,
    norm1_gain,
    norm2_gain,
    bias_table,
    w_query,
    w_key,
    w_value,
    w_out,
    w_gate,
    w_up,
    w_down,
    cotangent,
):
    micro, _, block_rows, width = tokens.shape
    blocks = lax.axis_size("ctx")
    parts_f = lax.axis_size("fsdp")
    fast = blocks // GROUPS
    ctx = lax.axis_index("ctx")
    f = lax.axis_index("fsdp")
    hi, lo = ctx // fast, ctx % fast
    group_cols = w_query.shape[1] // GROUPS
    own_rows = micro * block_rows
    hidden = w_gate.shape[1]
    piece = hidden // (parts_f * fast)
    part_rows = w_query.shape[0]
    gain_one = norm1_gain.reshape(1, width)
    gain_two = norm2_gain.reshape(1, width)
    place = jnp.stack([hi, lo, f]).astype(jnp.int32)

    own_x = tokens[:, 0]
    g_low = cotangent[:, 0].reshape(own_rows, width)
    x_slots = spread_groups(own_x)

    def group_of(matrix):
        return lax.dynamic_slice_in_dim(matrix, hi * group_cols, group_cols, axis=1)

    q_part, k_part, v_part = group_of(w_query), group_of(w_key), group_of(w_value)
    gap = jnp.zeros((part_rows, 64), LOW)
    qkv_part = jnp.concatenate([q_part, gap, k_part, v_part[:, 128:], v_part[:, :128]], axis=1)
    qkv_slots = slots_out(qkv_part, "fsdp", parts_f)

    def pieces(matrix):
        return [
            lax.dynamic_slice_in_dim(matrix, (k * fast + lo) * piece, piece, axis=1) for k in range(parts_f)
        ]

    pair_part = jnp.concatenate(pieces(w_gate) + pieces(w_up), axis=1)
    down_part = lax.dynamic_slice_in_dim(w_down, lo * piece, piece, axis=0)

    starts = offsets[:, 0]
    group_ids = (hi + GROUPS - jnp.arange(GROUPS, dtype=jnp.int32)) % GROUPS
    slot_ids = lo ^ jnp.arange(fast, dtype=jnp.int32)
    kplace = jnp.take(starts, group_ids[None, :] * fast + slot_ids[:, None], axis=1)
    table_group = lax.dynamic_slice_in_dim(bias_table, hi * 3, 3, axis=1)
    strip = make_strip(table_group, blocks)

    tick = [place]

    def fence(*values):
        tick[0], *values = lax.optimization_barrier((tick[0], *values))
        return values[0] if len(values) == 1 else values

    def shifted(parts, sign):
        return [shift(v, sign * d) for d, v in enumerate(parts, 1)]

    def to_f(parts):
        return [hop(v, "fsdp", j) for j, v in enumerate(parts, 1)]

    def groups_sum(own, parts):
        return (own + sum(v.astype(WIDE) for v in parts)).astype(LOW)

    def far_places(v):
        have = {0: v}
        for bit in bits_down(fast // 2):
            for j in list(have):
                have[j ^ (2 * bit)] = hop(have[j], "ctx", 2 * bit)
        return have

    def both_cores(have):
        return [v for j in range(0, fast, 2) for v in (have[j], hop(have[j], "ctx", 1))]

    strip, kplace = fence(strip, kplace)
    places = (kplace[:, 0], kplace)
    g_have = far_places(g_low)
    out_w, pair_w, x_slots, qkv_slots, g_have = fence(w_out, pair_part, x_slots, qkv_slots, g_have)
    act_one, q, kv = project(tick[0], gain_one, x_slots, qkv_slots)
    kv_slots = slots_out(kv, "ctx", fast)
    out_w_slots = slots_out(out_w, "fsdp", parts_f)
    g_slots = both_cores(g_have)
    g_low, kv_slots, out_w_slots, g_slots, pair_w = fence(g_low, kv_slots, out_w_slots, g_slots, pair_w)
    pair_slots = slots_out(pair_w, "fsdp", parts_f)
    o_group, lse = attention_forward(places, strip, q, kv_slots, blocks)
    o_group, down_w = fence(o_group, down_part)
    o_slots = [o_group[0]] + shifted(o_group[1:], -1)
    down_slots = slots_out(down_w, "fsdp", parts_f)
    w_rel = arrange(tick[0], out_w_slots)
    o_slots, w_rel = fence(o_slots, w_rel)
    resid, act_two = joined(tick[0], gain_two, own_x, o_slots, w_rel)
    act_two = fence(act_two)
    act_slots = slots_out(act_two, "ctx", fast)
    two_parts, out_parts, hid, grads = feed(tick[0], act_slots, g_slots, pair_slots, down_slots)
    two_parts, out_parts = fence(two_parts, out_parts)

    two_odd = two_parts[2]
    two_got = hop(two_odd, "ctx", 1)
    pair_keep, *pair_sends = pair_grads(tick[0], act_slots, grads, parts_f)
    out_got_one = hop(out_parts[2], "ctx", 1)
    two_got, pair_keep, pair_sends, out_got_one = fence(two_got, pair_keep, pair_sends, out_got_one)
    pair_got = to_f(pair_sends)
    two_list, sent = pairs_on(two_parts, two_got, fast)
    low_keep, *low_sends = down_grads(fence(tick[0], sent)[0], g_slots, hid, parts_f)
    got, low_keep, low_sends = fence([v for v, _ in two_list], low_keep, low_sends)
    two_list = [(v, first) for v, (_, first) in zip(got, two_list)]
    grad_resid, grad_low, gain_two_part, do_own = branch(
        tick[0], gain_two, resid, g_low, two_list, w_rel, micro
    )
    do_own = fence(*do_own)
    do_slots = [do_own[0]] + shifted(do_own[1:], 1)
    out_list, _ = pairs_on(out_parts, out_got_one, fast)
    out_keep, out_send = out_grads(tick[0], grad_low, o_slots, parts_f, fast)
    out_keep, out_send, do_slots, pair_got, got = fence(
        out_keep, out_send, do_slots, pair_got, [v for v, _ in out_list]
    )
    out_list = [(v, first) for v, (_, first) in zip(got, out_list)]
    out_got = hop(out_send, "ctx", 1)
    pair_own, pair_sends = group_split(tick[0], [pair_keep, *pair_got])
    pair_own, pair_sends, low_sends, out_total = fence(
        pair_own, pair_sends, low_sends, out_keep + out_got.astype(WIDE)
    )

    pair_parts = shifted(pair_sends, 1)
    low_got = to_f(low_sends)
    out_total = halve(out_total, "fsdp", 1)
    dq, dkv_parts, table_part = attention_backward(
        places, tick[0], strip, q, kv_slots, do_slots, lse, blocks
    )
    dq, dkv_parts, pair_parts, low_got, out_total = fence(dq, dkv_parts, pair_parts, low_got, out_total)
    dkv_list, sent = pairs_on(dkv_parts, hop(dkv_parts[2], "ctx", 1), fast)
    low_keep, low_send = group_halves(tick[0], [low_keep, *low_got])
    pair_chunk, low_send, out_total, _ = fence(groups_sum(pair_own, pair_parts), low_send, out_total, sent)
    pair_spread = spread_groups(pair_chunk)
    out_low = halve(out_total, "ctx", 2).astype(LOW)
    got = fence([v for v, _ in dkv_list])
    dkv_list = [(v, first) for v, (_, first) in zip(got, dkv_list)]
    one_keep, one_send, gain_one_part, in_keep, in_send = input_grads(
        tick[0], act_one, dq, x_slots, dkv_list, qkv_slots, fast
    )
    one_keep, one_send, in_keep, in_send, low_send, pair_spread, out_low = fence(
        one_keep, one_send, in_keep, in_send, low_send, pair_spread, out_low
    )
    def send_small(v, small, bit):
        high = small.astype(LOW)
        rest = (small - high.astype(WIDE)).astype(LOW)
        return hop(jnp.concatenate([v, high, rest]), "ctx", bit), high.astype(WIDE) + rest.astype(WIDE)

    def take_small(got, own):
        lines = own.shape[0]
        count = got.shape[0] - 2 * lines
        return got[:count], own + got[count : count + lines].astype(WIDE) + got[count + lines :].astype(WIDE)

    def two_hops(a, b, bit):
        if a.shape[:-1] != b.shape[:-1]:
            return hop(a, "ctx", bit), hop(b, "ctx", bit)
        got = hop(jnp.concatenate([a, b], axis=-1), "ctx", bit)
        return got[..., : a.shape[-1]], got[..., a.shape[-1] :]

    head_count = bias_table.shape[1]
    table_row = table_part[:, :head_count].reshape(1, -1)
    table_row = jnp.pad(table_row, ((0, 5), (0, width - table_row.shape[1])))
    small = jnp.concatenate([gain_one_part, gain_two_part, table_row])
    in_got = hop(in_send, "ctx", 1)
    out_two = jnp.stack([out_low[:, : width // 2], out_low[:, width // 2 :]])
    low_got, out_got = two_hops(low_send, out_two, fast)
    pair_have = far_places(jnp.stack(pair_spread))
    one_got, small = send_small(one_send.reshape(-1, width), small, fast)
    in_total = fence(in_keep + in_got.astype(WIDE))
    in_total, low_got, out_got = fence(halve(in_total, "fsdp", 1), low_got, out_got)
    low_sum = low_keep + low_got.astype(WIDE)
    out_two = (out_two.astype(WIDE) + out_got.astype(WIDE)).astype(LOW)
    out_low = jnp.concatenate([out_two[0], out_two[1]], axis=1)
    low_got, out_got = two_hops(low_sum[1].astype(LOW), out_low, 2 * fast)
    in_chunk, pair_have = fence(halve(in_total, "ctx", 2).astype(LOW), pair_have)
    in_spread = spread_groups(in_chunk)
    in_spread, low_got, out_got, one_got = fence(in_spread, low_got, out_got, one_got)
    low_spread = spread_groups((low_sum[0] + low_got.astype(WIDE)).astype(LOW))
    out_low = (out_low.astype(WIDE) + out_got.astype(WIDE)).astype(LOW)
    in_have = far_places(jnp.concatenate([*in_spread, out_low], axis=1))
    one_got, small = take_small(one_got, small)
    one_got = one_got.reshape(one_keep.shape)
    one_sum = one_keep[0] + one_got[0].astype(WIDE)
    one_send = (one_keep[1] + one_got[1].astype(WIDE)).astype(LOW)
    small = small + hop(small, "ctx", 1)
    for bit in bits_up(parts_f):
        small = small + hop(small, "fsdp", bit)
    low_spread, one_send, pair_have, small = fence(low_spread, one_send, pair_have, small)
    low_have = far_places(jnp.stack(low_spread))
    one_got, small = send_small(one_send, small, 2 * fast)
    pair_packs = both_cores(pair_have)
    in_packs, pair_packs = fence(both_cores(in_have), pair_packs)
    w_gate_grad, w_up_grad, w_query_grad, w_key_grad, w_value_grad, w_out_grad, result = most_finish(
        tick[0], pair_packs, in_packs, resid, out_list, parts_f, width
    )
    w_query_grad, one_got, low_have = fence(w_query_grad, one_got, low_have)
    low_packs = both_cores(low_have)
    small = take_small(one_got, small)[1]
    for bit in bits_down(fast // 2):
        small = small + hop(small, "ctx", 2 * bit)
    x_grad = last(tick[0], gain_one, own_x, grad_resid, one_sum, one_got)
    x_grad, low_packs = fence(x_grad, low_packs)
    w_down_grad = low_finish(tick[0], low_packs, parts_f)

    gain_rows = width // parts_f
    table_rows = bias_table.shape[0] // parts_f
    gain_one_grad = lax.dynamic_slice_in_dim(small[0], f * gain_rows, gain_rows)
    gain_two_grad = lax.dynamic_slice_in_dim(small[1], f * gain_rows, gain_rows)
    table_grad = small[2, : bias_table.size].reshape(bias_table.shape)
    table_grad = lax.dynamic_slice_in_dim(table_grad, f * table_rows, table_rows)

    return (
        result.reshape(micro, 1, block_rows, width),
        x_grad.reshape(micro, 1, block_rows, width),
        gain_one_grad,
        gain_two_grad,
        table_grad,
        w_query_grad,
        w_key_grad,
        w_value_grad,
        w_out_grad,
        w_gate_grad,
        w_up_grad,
        w_down_grad,
    )


def solution(mesh):
    in_specs = (
        P(None, "fsdp", "ctx", None),
        P(None, "fsdp", None),
        P(),
        P(),
        P(),
        P("fsdp", None),
        P("fsdp", None),
        P("fsdp", None),
        P("fsdp", None),
        P("fsdp", None),
        P("fsdp", None),
        P("fsdp", None),
        P(None, "fsdp", "ctx", None),
    )
    out_specs = (
        P(None, "fsdp", "ctx", None),
        P(None, "fsdp", "ctx", None),
        P("fsdp"),
        P("fsdp"),
        P("fsdp", None),
        P("fsdp", None),
        P("fsdp", None),
        P("fsdp", None),
        P("fsdp", None),
        P("fsdp", None),
        P("fsdp", None),
        P("fsdp", None),
    )
    return jax.shard_map(body, mesh=mesh, in_specs=in_specs, out_specs=out_specs, check_vma=False)
```
